32 devices in a mesh: pb: 2 (over y), blk: 16 (over z, x, core).
Axes of the slice: x: 2, y: 2, z: 4, core: 2. Of those that a mesh axis runs over, the one named last changes fastest.
Arguments:
- decoder_in: float32 [16, 20, 768], P('pb'), may hold values from -6 to 6
- encoded: bfloat16 [16, 16384, 768], P('pb', 'blk'), may hold values from -6 to 6
- key_ids: int32 [16, 16384], P('pb', 'blk'), may hold values 0 or 1
- buckets: int32 [20, 20], replicated, may hold values from 0 to 31
- gain_self: float32 [768], replicated, may hold values from 0.25 to 1.75
- gain_cross: float32 [768], replicated, may hold values from 0.25 to 1.75
- gain_ffn: float32 [768], replicated, may hold values from 0.25 to 1.75
- rel_bias: float32 [32, 12], replicated, may hold values from -4 to 4
- self_q: bfloat16 [768, 768], replicated, may hold values from -0.109375 to 0.109375
- self_k: bfloat16 [768, 768], replicated, may hold values from -0.109375 to 0.109375
- self_v: bfloat16 [768, 768], replicated, may hold values from -0.21875 to 0.21875
- self_o: bfloat16 [768, 768], replicated, may hold values from -0.4375 to 0.4375
- cross_q: bfloat16 [768, 768], replicated, may hold values from -0.109375 to 0.109375
- cross_k: bfloat16 [768, 768], replicated, may hold values from -0.109375 to 0.109375
- cross_v: bfloat16 [768, 768], replicated, may hold values from -0.21875 to 0.21875
- cross_o: bfloat16 [768, 768], replicated, may hold values from -1.75 to 1.75
- ffn_in: bfloat16 [768, 3072], replicated, may hold values from -0.21875 to 0.21875
- ffn_out: bfloat16 [3072, 768], replicated, may hold values from -0.15625 to 0.15625
- cotangent: float32 [16, 20, 768], P('pb'), may hold values from -6 to 6
Outputs:
- output: float32 [16, 20, 768], P('pb')
- grad_in: float32 [16, 20, 768], P('pb')
- grad_encoded: bfloat16 [16, 16384, 768], P('pb', 'blk')
- grad_gain_self: float32 [768], replicated
- grad_gain_cross: float32 [768], replicated
- grad_gain_ffn: float32 [768], replicated
- grad_rel_bias: float32 [32, 12], replicated
- grad_self_q: float32 [768, 768], P('blk')
- grad_self_k: float32 [768, 768], P('blk')
- grad_self_v: float32 [768, 768], P('blk')
- grad_self_o: float32 [768, 768], P('blk')
- grad_cross_q: float32 [768, 768], P('blk')
- grad_cross_k: float32 [768, 768], P('blk')
- grad_cross_v: float32 [768, 768], P('blk')
- grad_cross_o: float32 [768, 768], P('blk')
- grad_ffn_in: float32 [768, 3072], P('blk')
- grad_ffn_out: float32 [3072, 768], P('blk')
The draws below stay inside these ranges and needn't reach their ends.
Inputs may be any that keep to these rules, and one draw needn't show every extreme that they name: `key_ids`: 1 marks a real encoder token, 0 a padding one.
All inputs are finite; a program needn't handle non-finite values. No bound on the sum of `key_ids` on one device may be relied on, other than what follows from the above.
Results may differ from the reference program's by a relative error of at most 0.023.
The reference program's roundings to bfloat16 on the way count: a program that leaves them out, or rounds other values in their place, can miss the bound.
Values sent between devices are 32-bit elements; how exact they have to be, the bound alone decides.
No kernel may reach another device: no remote copies, remote signals or barrier semaphores. Data moves between devices by JAX's collectives and lax.ppermute only.
A program may use at most 192 MiB of HBM per device.

```python
import jax
import jax.numpy as jnp
from jax import lax

D = 768
HEADS = 12
FF = 3072
BUCKETS = 32
ANS = 20
QUESTIONS = 16
ENCODED = 16384


def touch_ends(entries, own_key, smallest, high):
    dims = entries.shape
    spot = [jax.random.randint(jax.random.fold_in(own_key, axis), (), 0, dims[axis]) for axis in range(len(dims))]
    entries = entries.at[tuple(spot)].set(smallest)
    longest = dims.index(max(dims))
    spot[longest] = (spot[longest] + 1) % dims[longest]
    return entries.at[tuple(spot)].set(high)


def block_levels(key, extent, pieces, least, largest):
    factor_of, own = 1.0, jax.random.fold_in(key, 6)
    for dim, parts in pieces:
        heights = jnp.exp(jax.random.uniform(jax.random.fold_in(own, dim), (parts,), jnp.float32, least / len(pieces), largest / len(pieces)))
        factor_of = factor_of * jnp.repeat(heights, extent[dim] // parts).reshape([-1 if axis == dim else 1 for axis in range(len(extent))])
    return factor_of


def centred(own_key, shape, spread, limit, pieces=(), held_as=jnp.bfloat16):
    result = spread * jax.random.normal(own_key, shape, jnp.float32)
    if pieces:
        result = result * block_levels(own_key, shape, pieces, -0.22, 0.18)
    return jnp.clip(result, -limit, limit).astype(held_as)


def setup_inputs(seed: int = 0) -> dict:
    key_of = jax.random.split(jax.random.key(seed), 20)
    return {
        "decoder_in": centred(key_of[0], (QUESTIONS, ANS, D), 1.0, 6.0, ((0, 2),), jnp.float32),
        "encoded": centred(key_of[1], (QUESTIONS, ENCODED, D), 1.0, 6.0, ((0, 2), (1, 16))),
        "key_ids": touch_ends((jax.random.randint(key_of[2], (QUESTIONS, ENCODED), 0, 4) < 3).astype(jnp.int32), jax.random.fold_in(key_of[2], 1), 0, 1),
        "buckets": touch_ends(jax.random.randint(key_of[3], (ANS, ANS), 0, BUCKETS), jax.random.fold_in(key_of[3], 1), 0, BUCKETS - 1).astype(jnp.int32),
        "gain_self": jnp.clip(1.0 + 0.15 * jax.random.normal(key_of[4], (D,), jnp.float32), 0.25, 1.75),
        "gain_cross": jnp.clip(1.0 + 0.15 * jax.random.normal(key_of[5], (D,), jnp.float32), 0.25, 1.75),
        "gain_ffn": jnp.clip(1.0 + 0.15 * jax.random.normal(key_of[6], (D,), jnp.float32), 0.25, 1.75),
        "rel_bias": centred(key_of[7], (BUCKETS, HEADS), 1.0, 4.0, (), jnp.float32),
        "self_q": centred(key_of[8], (D, D), (4 * D) ** -0.5, 0.109375),
        "self_k": centred(key_of[9], (D, D), (4 * D) ** -0.5, 0.109375),
        "self_v": centred(key_of[10], (D, D), D ** -0.5, 0.21875),
        "self_o": centred(key_of[11], (D, D), (D // 4) ** -0.5, 0.4375),
        "cross_q": centred(key_of[12], (D, D), (4 * D) ** -0.5, 0.109375),
        "cross_k": centred(key_of[13], (D, D), (4 * D) ** -0.5, 0.109375),
        "cross_v": centred(key_of[14], (D, D), D ** -0.5, 0.21875),
        "cross_o": centred(key_of[15], (D, D), (D // 64) ** -0.5, 1.75),
        "ffn_in": centred(key_of[16], (D, FF), D ** -0.5, 0.21875),
        "ffn_out": centred(key_of[17], (FF, D), (FF // 2) ** -0.5, 0.15625),
        "cotangent": centred(key_of[18], (QUESTIONS, ANS, D), 1.0, 6.0, ((0, 2),), jnp.float32),
    }


EPSILON = 1e-06
MASKED = -1000000000.0
HIGHEST = lax.Precision.HIGHEST

@jax.custom_vjp
def low(v):
    return lax.optimization_barrier(v.astype(jnp.bfloat16)).astype(jnp.float32)

@jax.custom_vjp
def low_back(v):
    return v

def low_keep(v):
    return (low(v), None)

def low_pass(kept, grad):
    return (grad,)

def back_keep(v):
    return (v, None)

def back_low(kept, grad):
    return (low(grad),)
low.defvjp(low_keep, low_pass)
low_back.defvjp(back_keep, back_low)

def both_round(values):
    return low(low_back(values))

def rms_norm(values, gain_vec):
    inv_scale = lax.rsqrt(lax.optimization_barrier(jnp.mean(values * values, axis=-1, keepdims=True)) + EPSILON)
    return values * inv_scale * gain_vec

def project(left_side, right_side):
    return jnp.einsum('qnd,de->qne', left_side, right_side, precision=HIGHEST)

def to_heads(values, head_count):
    return values.reshape(values.shape[0], values.shape[1], head_count, values.shape[2] // head_count)

def forward(decoder_in, encoded, gain_self, gain_cross, gain_ffn, rel_bias, self_q, self_k, self_v, self_o, cross_q, cross_k, cross_v, cross_o, ffn_in, ffn_out, key_ids, buckets):
    questions, answer_len, features = decoder_in.shape
    head_count = rel_bias.shape[1]
    normed_one = low(rms_norm(decoder_in, gain_self))
    query_self = to_heads(both_round(project(normed_one, self_q)), head_count)
    key_self = to_heads(both_round(project(normed_one, self_k)), head_count)
    value_self = to_heads(both_round(project(normed_one, self_v)), head_count)
    raw_self = low_back(jnp.einsum('qihd,qjhd->qhij', query_self, key_self, precision=HIGHEST))
    position_bias = jnp.transpose(rel_bias[buckets], (2, 0, 1))
    positions = jnp.arange(answer_len)
    causal = jnp.where(positions[None, :] <= positions[:, None], 0.0, MASKED)
    probs_self = jax.nn.softmax(raw_self + position_bias + causal, axis=-1)
    context_self = jnp.einsum('qhij,qjhd->qihd', low(probs_self), value_self, precision=HIGHEST)
    context_self = both_round(context_self.reshape(questions, answer_len, features))
    after_self = decoder_in + low_back(project(context_self, self_o))
    normed_two = low(rms_norm(after_self, gain_cross))
    query_cross = to_heads(low(project(normed_two, cross_q)), head_count)
    key_cross = to_heads(both_round(project(encoded, cross_k)), head_count)
    value_cross = to_heads(both_round(project(encoded, cross_v)), head_count)
    key_mask = jnp.where(key_ids != 0, 0.0, MASKED)[:, None, None, :]
    raw_cross = low_back(jnp.einsum('qihd,qjhd->qhij', query_cross, key_cross, precision=HIGHEST))
    probs_cross = jax.nn.softmax(raw_cross + key_mask, axis=-1)
    context_cross = jnp.einsum('qhij,qjhd->qihd', low(probs_cross), value_cross, precision=HIGHEST)
    context_cross = low_back(context_cross.reshape(questions, answer_len, features))
    after_cross = after_self + low_back(project(context_cross, cross_o))
    normed_three = low(rms_norm(after_cross, gain_ffn))
    ffn_inner = low_back(project(normed_three, ffn_in))
    active = both_round(jax.nn.gelu(ffn_inner))
    return after_cross + low_back(project(active, ffn_out))

def reference(decoder_in, encoded, key_ids, buckets, gain_self, gain_cross, gain_ffn, rel_bias, self_q, self_k, self_v, self_o, cross_q, cross_k, cross_v, cross_o, ffn_in, ffn_out, cotangent):
    floats = (decoder_in, encoded.astype(jnp.float32), gain_self, gain_cross, gain_ffn, rel_bias, self_q.astype(jnp.float32), self_k.astype(jnp.float32), self_v.astype(jnp.float32), self_o.astype(jnp.float32), cross_q.astype(jnp.float32), cross_k.astype(jnp.float32), cross_v.astype(jnp.float32), cross_o.astype(jnp.float32), ffn_in.astype(jnp.float32), ffn_out.astype(jnp.float32))

    def wrapped(*values):
        return forward(*values, key_ids, buckets)
    output, pullback = jax.vjp(wrapped, *floats)
    gradients = pullback(cotangent)
    return (output, gradients[0], gradients[1].astype(jnp.bfloat16), gradients[2], gradients[3], gradients[4], gradients[5], gradients[6], gradients[7], gradients[8], gradients[9], gradients[10], gradients[11], gradients[12], gradients[13], gradients[14], gradients[15])
```

```python
import functools

import jax
import jax.numpy as jnp
from jax import lax
from jax.experimental import pallas as pl
from jax.experimental.pallas import tpu as pltpu
from jax.sharding import PartitionSpec as P

EPSILON = 1e-06
MASKED = -1000000000.0
HIGHEST = lax.Precision.HIGHEST

HEAD = 64
GROUP = 4
WIDE = GROUP * HEAD
LANES = 128


def nt(a, b):
    return lax.dot_general(a, b, (((1,), (1,)), ((), ())), preferred_element_type=jnp.float32)


def nn(a, b):
    return jnp.dot(a, b, preferred_element_type=jnp.float32)


def tn(a, b):
    return lax.dot_general(a, b, (((0,), (0,)), ((), ())), preferred_element_type=jnp.float32)


def row_head(ans, width):
    row = lax.broadcasted_iota(jnp.int32, (GROUP * ans, width), 0)
    head = jnp.zeros_like(row)
    for k in range(1, GROUP):
        head = head + (row >= k * ans).astype(jnp.int32)
    return head


def own_columns(ans):
    col = lax.broadcasted_iota(jnp.int32, (GROUP * ans, WIDE), 1)
    return (col // HEAD) == row_head(ans, WIDE)


def own_lane(ans, group, first=0):
    col = lax.broadcasted_iota(jnp.int32, (GROUP * ans, LANES), 1)
    return col == row_head(ans, LANES) + (group * GROUP + first)


def fold(block, ans):
    half = block[: 2 * ans] + block[2 * ans :]
    return half[:ans] + half[ans:]


def spread(rows):
    twice = jnp.concatenate([rows, rows], axis=0)
    return jnp.concatenate([twice, twice], axis=0)


def block_diagonal(values_ref, dest_ref, questions, ans, groups):
    own = own_columns(ans)
    per = GROUP * ans
    for q in range(questions):
        rows = spread(values_ref[q * ans : (q + 1) * ans, :])
        for g in range(groups):
            part = jnp.where(own, rows[:, g * WIDE : (g + 1) * WIDE], 0.0)
            dest_ref[g, q * per : (q + 1) * per, :] = part.astype(jnp.bfloat16)


def absorb(bd_ref, weight_ref, dest_ref, questions, ans, groups):
    per = GROUP * ans
    for g in range(groups):
        got = nt(bd_ref[g], weight_ref[:, g * WIDE : (g + 1) * WIDE]).astype(jnp.bfloat16)
        for q in range(questions):
            dest_ref[q, g * per : (g + 1) * per, :] = got[q * per : (q + 1) * per]


def project_heads(wide_ref, weight_ref, dest_ref, questions, ans, groups):
    own = own_columns(ans)
    per = GROUP * ans
    for g in range(groups):
        got = nn(wide_ref[g], weight_ref[:, g * WIDE : (g + 1) * WIDE])
        for q in range(questions):
            part = jnp.where(own, got[q * per : (q + 1) * per], 0.0)
            dest_ref[q * ans : (q + 1) * ans, g * WIDE : (g + 1) * WIDE] = fold(part, ans)


def forward_kernel(questions, ans, groups, q_ref, enc_ref, ids_ref, wk_ref, wv_ref,
                   ctx_ref, p_ref, c_ref, a_ref, bd_ref, stat_ref, m_scr, l_scr):
    step = pl.program_id(0)
    per = GROUP * ans

    @pl.when(step == 0)
    def _():
        block_diagonal(q_ref, bd_ref, questions, ans, groups)
        absorb(bd_ref, wk_ref, a_ref, questions, ans, groups)

    scores = nt(a_ref[step], enc_ref[0])
    scores = scores + jnp.where(ids_ref[0] != 0, 0.0, MASKED)
    top = jnp.max(scores, axis=1, keepdims=True)
    probs = jnp.exp(scores - top)
    total = jnp.sum(probs, axis=1, keepdims=True)
    low = probs.astype(jnp.bfloat16)
    p_ref[0] = low
    wide = nn(low, enc_ref[0]).astype(jnp.bfloat16)
    for g in range(groups):
        c_ref[g, pl.ds(pl.multiple_of(step * per, per), per), :] = wide[g * per : (g + 1) * per]
    m_scr[step] = jnp.broadcast_to(top, m_scr.shape[1:])
    l_scr[step] = jnp.broadcast_to(total, l_scr.shape[1:])

    @pl.when(step == questions - 1)
    def _():
        project_heads(c_ref, wv_ref, ctx_ref, questions, ans, groups)
        for q in range(questions):
            stats = jnp.zeros((ans, LANES), jnp.float32)
            for src, first in ((m_scr, 0), (l_scr, HEAD)):
                for g in range(groups):
                    part = jnp.where(own_lane(ans, g, first), src[q, g * per : (g + 1) * per, :], 0.0)
                    stats = stats + fold(part, ans)
            stat_ref[q * ans : (q + 1) * ans, :] = stats


def whole(shape):
    return pl.BlockSpec(shape, lambda q: (0,) * len(shape))


def per_question(shape):
    return pl.BlockSpec((1,) + shape, lambda q: (q,) + (0,) * len(shape))


def cross_forward(query, encoded, ids, wk, wv, ans):
    questions, tokens, features = encoded.shape
    groups = features // WIDE
    per = GROUP * ans
    rows = groups * per
    f32, bf16 = jnp.float32, jnp.bfloat16
    outs = [
        ((questions * ans, features), f32),
        ((questions, rows, tokens), bf16),
        ((groups, questions * per, features), bf16),
        ((questions, rows, features), bf16),
        ((groups, questions * per, WIDE), bf16),
        ((questions * ans, LANES), f32),
    ]
    specs = [whole(s) for s, _ in outs]
    specs[1] = per_question((rows, tokens))
    return pl.pallas_call(
        functools.partial(forward_kernel, questions, ans, groups),
        grid=(questions,),
        in_specs=[whole(query.shape), per_question((tokens, features)), per_question((1, tokens)),
                  whole(wk.shape), whole(wv.shape)],
        out_specs=specs,
        out_shape=[jax.ShapeDtypeStruct(s, t) for s, t in outs],
        scratch_shapes=[pltpu.VMEM((questions, rows, LANES), f32)] * 2,
        compiler_params=pltpu.CompilerParams(vmem_limit_bytes=48 * 2**20),
        name="cross_forward",
    )(query, encoded, ids.reshape(questions, 1, tokens), wk, wv)


def backward_kernel(questions, ans, groups, g_ref, w_ref, d_ref, p_ref, enc_ref, wk_ref, wv_ref,
                    s_ref, wide_ref, b_ref, bd_ref, gq_ref, raw_scr, w_scr, d_scr):
    step = pl.program_id(0)
    per = GROUP * ans

    @pl.when(step == 0)
    def _():
        block_diagonal(g_ref, bd_ref, questions, ans, groups)
        for q in range(questions):
            for src, dst in ((w_ref, w_scr), (d_ref, d_scr)):
                rows = spread(src[q * ans : (q + 1) * ans, :])
                for g in range(groups):
                    part = jnp.sum(jnp.where(own_lane(ans, g), rows, 0.0), axis=1, keepdims=True)
                    dst[q, g * per : (g + 1) * per, :] = jnp.broadcast_to(part, (per, LANES))
        for g in range(groups):
            got = nt(bd_ref[g], wv_ref[:, g * WIDE : (g + 1) * WIDE])
            for q in range(questions):
                part = got[q * per : (q + 1) * per]
                raw_scr[q, g * per : (g + 1) * per, :] = part.astype(jnp.bfloat16)
                scale = w_scr[q, g * per : (g + 1) * per, :1]
                b_ref[q, g * per : (g + 1) * per, :] = (part * scale).astype(jnp.bfloat16)
        for g in range(groups):
            for q in range(questions):
                scale = w_scr[q, g * per : (g + 1) * per, :1]
                part = bd_ref[g, q * per : (q + 1) * per, :].astype(jnp.float32) * scale
                bd_ref[g, q * per : (q + 1) * per, :] = part.astype(jnp.bfloat16)

    grad_probs = nt(raw_scr[step], enc_ref[0])
    probs = p_ref[0].astype(jnp.float32) * w_scr[step][:, :1]
    grad_scores = (probs * (grad_probs - d_scr[step][:, :1])).astype(jnp.bfloat16)
    s_ref[0] = grad_scores
    wide = nn(grad_scores, enc_ref[0]).astype(jnp.bfloat16)
    for g in range(groups):
        wide_ref[g, pl.ds(pl.multiple_of(step * per, per), per), :] = wide[g * per : (g + 1) * per]

    @pl.when(step == questions - 1)
    def _():
        project_heads(wide_ref, wk_ref, gq_ref, questions, ans, groups)


def cross_backward(grad_context, weight, delta, probs, encoded, wk, wv, ans):
    questions, tokens, features = encoded.shape
    groups = features // WIDE
    per = GROUP * ans
    rows = groups * per
    f32, bf16 = jnp.float32, jnp.bfloat16
    outs = [
        ((questions, rows, tokens), bf16),
        ((groups, questions * per, features), bf16),
        ((questions, rows, features), bf16),
        ((groups, questions * per, WIDE), bf16),
        ((questions * ans, features), f32),
    ]
    specs = [per_question((rows, tokens))] + [whole(s) for s, _ in outs[1:]]
    return pl.pallas_call(
        functools.partial(backward_kernel, questions, ans, groups),
        grid=(questions,),
        in_specs=[whole(grad_context.shape), whole(weight.shape), whole(delta.shape),
                  per_question((rows, tokens)), per_question((tokens, features)),
                  whole(wk.shape), whole(wv.shape)],
        out_specs=specs,
        out_shape=[jax.ShapeDtypeStruct(s, t) for s, t in outs],
        scratch_shapes=[pltpu.VMEM((questions, rows, features), bf16),
                        pltpu.VMEM((questions, rows, LANES), f32),
                        pltpu.VMEM((questions, rows, LANES), f32)],
        compiler_params=pltpu.CompilerParams(vmem_limit_bytes=48 * 2**20),
        name="cross_backward",
    )(grad_context, weight, delta, probs, encoded, wk, wv)


def encoded_kernel(s_ref, p_ref, a_ref, b_ref, out_ref):
    left = jnp.concatenate([s_ref[0], p_ref[0]], axis=0)
    right = jnp.concatenate([a_ref[0], b_ref[0]], axis=0)
    out_ref[0] = tn(left, right).astype(jnp.bfloat16)


def encoded_gradient(grad_scores, probs, a, b):
    questions, rows, tokens = probs.shape
    features = a.shape[2]
    return pl.pallas_call(
        encoded_kernel,
        grid=(questions,),
        in_specs=[per_question((rows, tokens))] * 2 + [per_question((rows, features))] * 2,
        out_specs=per_question((tokens, features)),
        out_shape=jax.ShapeDtypeStruct((questions, tokens, features), jnp.bfloat16),
        compiler_params=pltpu.CompilerParams(vmem_limit_bytes=48 * 2**20),
        name="encoded_gradient",
    )(grad_scores, probs, a, b)


def rms_norm(values, gain_vec):
    inv_scale = lax.rsqrt(jnp.mean(values * values, axis=-1, keepdims=True) + EPSILON)
    return values * inv_scale * gain_vec


def matmul(left_side, right_side):
    return jnp.dot(left_side, right_side, preferred_element_type=jnp.float32)


def matmul_nt(left_side, right_side):
    return lax.dot_general(
        left_side, right_side, (((1,), (1,)), ((), ())), preferred_element_type=jnp.float32
    )


def matmul_tn(left_side, right_side):
    return lax.dot_general(
        left_side, right_side, (((0,), (0,)), ((), ())), preferred_element_type=jnp.float32
    )


def exact_mm(left_side, right_side):
    return jnp.dot(left_side, right_side.astype(jnp.float32), precision=HIGHEST)


def exact_nt(left_side, right_side):
    return lax.dot_general(
        left_side, right_side.astype(jnp.float32), (((1,), (1,)), ((), ())), precision=HIGHEST
    )


def exact_tn(left_side, right_side):
    return lax.dot_general(
        left_side.astype(jnp.float32),
        right_side.astype(jnp.float32),
        (((0,), (0,)), ((), ())),
        precision=HIGHEST,
    )


def columns(values, blk_index, share):
    return lax.dynamic_slice_in_dim(values, blk_index * share, share, 1)


def partner(value, axis, bit):
    count = lax.axis_size(axis)
    return lax.ppermute(value, axis, [(k, k ^ bit) for k in range(count)])


def axis_bits(axis):
    bits, bit = [], 1
    while bit < lax.axis_size(axis):
        bits.append(bit)
        bit *= 2
    return bits


def halves(value, axis, bit):
    rows = value.shape[0] // 2
    mine = (lax.axis_index(axis) // bit) % 2
    keep = lax.dynamic_slice_in_dim(value, mine * rows, rows, 0)
    give = lax.dynamic_slice_in_dim(value, (1 - mine) * rows, rows, 0)
    return keep, give


def joined(value, axis, bit):
    other = partner(value, axis, bit)
    mine = (lax.axis_index(axis) // bit) % 2
    first = jnp.where(mine == 0, value, other)
    second = jnp.where(mine == 0, other, value)
    return jnp.concatenate([first, second], axis=0)


def sum_all(value, axis):
    bits = axis_bits(axis)
    keep, give = halves(value, axis, bits[0])
    keep = keep + partner(give, axis, bits[0])
    for bit in bits[1:]:
        keep = keep + partner(keep, axis, bit)
    return joined(keep, axis, bits[0])


def sum_pair(value, axis):
    for bit in axis_bits(axis):
        value = value + partner(value, axis, bit)
    return value


def scatter_rows(value, axis):
    bits = axis_bits(axis)
    count = lax.axis_size(axis)
    index = lax.axis_index(axis)
    rows, width = value.shape
    value = value.reshape(count, rows // count, width)
    for bit in bits:
        mine = (index // bit) % 2
        left = value.shape[0] // 2
        pairs = value.reshape(left, 2, rows // count, width)
        keep = lax.dynamic_index_in_dim(pairs, mine, 1, keepdims=False)
        give = lax.dynamic_index_in_dim(pairs, 1 - mine, 1, keepdims=False)
        value = keep + partner(give, axis, bit)
    return value.reshape(rows // count, width)


def merge_kernel(heads, mine_ref, other_ref, out_ref):
    features = heads * HEAD
    mine = mine_ref[:, features:]
    other = other_ref[:, features:]
    lane = lax.broadcasted_iota(jnp.int32, mine.shape, 1)
    top_lane = lane < HEAD
    top_mine = jnp.where(top_lane, mine, pltpu.roll(mine, HEAD, 1))
    top_other = jnp.where(top_lane, other, pltpu.roll(other, HEAD, 1))
    top = jnp.maximum(top_mine, top_other)
    scale_mine = jnp.exp(top_mine - top)
    scale_other = jnp.exp(top_other - top)
    out_ref[:, features:] = jnp.where(top_lane, top, mine * scale_mine + other * scale_other)
    for pair in range(heads // 2):
        at = slice(pair * LANES, (pair + 1) * LANES)
        a = jnp.where(top_lane, scale_mine[:, 2 * pair : 2 * pair + 1], scale_mine[:, 2 * pair + 1 : 2 * pair + 2])
        b = jnp.where(top_lane, scale_other[:, 2 * pair : 2 * pair + 1], scale_other[:, 2 * pair + 1 : 2 * pair + 2])
        out_ref[:, at] = mine_ref[:, at] * a + other_ref[:, at] * b


def merge(mine, other, heads):
    return pl.pallas_call(
        functools.partial(merge_kernel, heads),
        out_shape=jax.ShapeDtypeStruct(mine.shape, mine.dtype),
        name="merge_partials",
    )(mine, other)


def merge_all(value, axis, heads):
    bits = axis_bits(axis)
    keep, give = halves(value, axis, bits[0])
    keep = merge(keep, partner(give, axis, bits[0]), heads)
    for bit in bits[1:]:
        keep = merge(keep, partner(keep, axis, bit), heads)
    return joined(keep, axis, bits[0])


def body(
    decoder_in,
    encoded,
    key_ids,
    buckets,
    gain_self,
    gain_cross,
    gain_ffn,
    rel_bias,
    self_q,
    self_k,
    self_v,
    self_o,
    cross_q,
    cross_k,
    cross_v,
    cross_o,
    ffn_in,
    ffn_out,
    cotangent,
):
    low_type = jnp.bfloat16
    questions, answer_len, features = decoder_in.shape
    head_count = rel_bias.shape[1]
    head_size = features // head_count
    hidden_units = ffn_in.shape[1]
    blk_count = lax.axis_size("blk")
    blk_index = lax.axis_index("blk")
    row_count = questions * answer_len
    feature_share = features // blk_count
    hidden_share = hidden_units // blk_count
    flat_in = decoder_in.reshape(row_count, features)
    norm_one, norm_one_back = jax.vjp(rms_norm, flat_in, gain_self)
    normed_one = norm_one.astype(low_type)
    self_weights = jnp.concatenate([self_q, self_k, self_v], axis=1)
    projected = matmul(normed_one, self_weights).astype(low_type)
    projected = projected.reshape(questions, answer_len, 3, head_count, head_size)
    query_self = projected[:, :, 0]
    key_self = projected[:, :, 1]
    value_self = projected[:, :, 2]
    bucket_hot = (buckets[:, :, None] == jnp.arange(rel_bias.shape[0], dtype=jnp.int32)).astype(
        jnp.float32
    )
    position_bias = jnp.einsum("ijb,bh->hij", bucket_hot, rel_bias, precision=HIGHEST)
    positions = jnp.arange(answer_len)
    causal = jnp.where(positions[None, :] <= positions[:, None], 0.0, MASKED)
    raw_self = jnp.einsum(
        "qihd,qjhd->qhij", query_self, key_self, preferred_element_type=jnp.float32
    )
    probs_self = jax.nn.softmax(raw_self + position_bias + causal, axis=-1)
    probs_self_low = probs_self.astype(low_type)
    context_self = jnp.einsum(
        "qhij,qjhd->qihd", probs_self_low, value_self, preferred_element_type=jnp.float32
    )
    context_self = context_self.reshape(row_count, features).astype(low_type)
    after_self = flat_in + matmul(context_self, self_o)
    norm_two, norm_two_back = jax.vjp(rms_norm, after_self, gain_cross)
    normed_two = norm_two.astype(low_type)
    query_cross = (
        matmul(normed_two, cross_q)
        .astype(low_type)
    )
    ctx_part, probs_low, ctx_wide, q_wide, q_blocks, stat_part = cross_forward(
        query_cross.astype(jnp.float32), encoded, key_ids, cross_k, cross_v, answer_len
    )
    merged_all = merge_all(jnp.concatenate([ctx_part, stat_part], axis=1), "blk", head_count)
    lane = jnp.arange(LANES)
    spread_heads = (jnp.arange(features)[None, :] // HEAD == lane[:, None]).astype(jnp.float32)
    top_all = merged_all[:, features : features + HEAD]
    total_all = merged_all[:, features + HEAD :]
    per_head = jnp.where(jnp.arange(HEAD) < head_count, 1.0 / total_all, 0.0)
    weight = jnp.exp(stat_part[:, :HEAD] - top_all) * per_head
    weight = jnp.concatenate([weight, jnp.zeros_like(weight)], axis=1)
    context_cross = merged_all[:, :features] * jnp.dot(per_head, spread_heads[:HEAD], precision=HIGHEST)
    after_cross = after_self + exact_mm(context_cross, cross_o)
    norm_three, norm_three_back = jax.vjp(rms_norm, after_cross, gain_ffn)
    normed_three = norm_three.astype(low_type)
    ffn_inner = matmul(normed_three, ffn_in)
    active, active_back = jax.vjp(jax.nn.gelu, ffn_inner)
    active_low = active.astype(low_type)
    output = after_cross + matmul(active_low, ffn_out)
    grad_out = cotangent.reshape(row_count, features)
    grad_out_low = grad_out.astype(low_type)
    grad_active = matmul_nt(grad_out_low, ffn_out).astype(low_type)
    grad_inner = active_back(grad_active.astype(jnp.float32))[0].astype(low_type)
    back_three, grad_gain_ffn = norm_three_back(matmul_nt(grad_inner, ffn_in))
    grad_after_cross = grad_out + back_three
    grad_ffn_out = matmul_tn(columns(active_low, blk_index, hidden_share), grad_out_low)
    grad_ffn_in = matmul_tn(columns(normed_three, blk_index, feature_share), grad_inner)
    grad_branch_cross = grad_after_cross.astype(low_type)
    grad_cross_o = exact_tn(columns(context_cross, blk_index, feature_share), grad_branch_cross)
    grad_context_cross = matmul_nt(grad_branch_cross, cross_o).astype(low_type)
    grad_context_cross = grad_context_cross.astype(jnp.float32)
    delta = lax.dot_general(
        grad_context_cross * context_cross, spread_heads, (((1,), (1,)), ((), ())), precision=HIGHEST
    )
    grad_scores_cross, query_wide, g_wide, g_blocks, partial_query = cross_backward(
        grad_context_cross, weight, delta, probs_low, encoded, cross_k, cross_v, answer_len
    )
    grad_query_cross = sum_all(partial_query, "blk")
    grad_encoded = encoded_gradient(grad_scores_cross, probs_low, q_wide, g_wide)
    wide_pairs = jnp.concatenate([query_wide, ctx_wide], axis=0)
    blocks = jnp.concatenate([q_blocks, g_blocks], axis=0)
    kv_part = jnp.einsum("grm,grd->mgd", wide_pairs, blocks, preferred_element_type=jnp.float32)
    kv_grad_share = scatter_rows(kv_part.reshape(features, 2 * features), "blk")
    grad_cross_q = exact_tn(columns(normed_two, blk_index, feature_share), grad_query_cross)
    back_two, grad_gain_cross = norm_two_back(exact_nt(grad_query_cross, cross_q))
    grad_after_self = grad_after_cross + back_two
    grad_branch_self = grad_after_self.astype(low_type)
    grad_self_o = matmul_tn(columns(context_self, blk_index, feature_share), grad_branch_self)
    grad_context_self = matmul_nt(grad_branch_self, self_o).astype(low_type)
    grad_context_self = grad_context_self.reshape(questions, answer_len, head_count, head_size)
    grad_probs_self = jnp.einsum(
        "qihd,qjhd->qhij", grad_context_self, value_self, preferred_element_type=jnp.float32
    )
    grad_scores_self = probs_self * (
        grad_probs_self - jnp.sum(probs_self * grad_probs_self, axis=-1, keepdims=True)
    )
    grad_bias = jnp.einsum("qhij,ijb->bh", grad_scores_self, bucket_hot, precision=HIGHEST)
    grad_scores_low = grad_scores_self.astype(low_type)
    grad_query_self = jnp.einsum(
        "qhij,qjhd->qihd", grad_scores_low, key_self, preferred_element_type=jnp.float32
    )
    grad_key_self = jnp.einsum(
        "qhij,qihd->qjhd", grad_scores_low, query_self, preferred_element_type=jnp.float32
    )
    grad_value_self = jnp.einsum(
        "qhij,qihd->qjhd", probs_self_low, grad_context_self, preferred_element_type=jnp.float32
    )
    grad_qkv = jnp.stack([grad_query_self, grad_key_self, grad_value_self], axis=2).astype(low_type)
    grad_qkv = grad_qkv.reshape(row_count, 3 * features)
    back_one, grad_gain_self = norm_one_back(matmul_nt(grad_qkv, self_weights))
    grad_in = grad_after_self + back_one
    grad_self_qkv = matmul_tn(columns(normed_one, blk_index, feature_share), grad_qkv)
    summed = jax.tree.map(
        lambda part: sum_pair(part, "pb"),
        (
            grad_self_qkv,
            grad_self_o,
            grad_cross_q,
            kv_grad_share,
            grad_cross_o,
            grad_ffn_in,
            grad_ffn_out,
            grad_gain_self,
            grad_gain_cross,
            grad_gain_ffn,
            grad_bias,
        ),
    )
    self_qkv_sum = summed[0]
    kv_sum = summed[3]
    return (
        output.reshape(questions, answer_len, features),
        grad_in.reshape(questions, answer_len, features),
        grad_encoded,
        summed[7],
        summed[8],
        summed[9],
        summed[10],
        self_qkv_sum[:, :features],
        self_qkv_sum[:, features : 2 * features],
        self_qkv_sum[:, 2 * features :],
        summed[1],
        summed[2],
        kv_sum[:, :features],
        kv_sum[:, features:],
        summed[4],
        summed[5],
        summed[6],
    )


def solution(mesh):
    placed = (
        P("pb", None, None),
        P("pb", "blk", None),
        P("pb", "blk"),
        P(),
        P(),
        P(),
        P(),
        P(),
        P(),
        P(),
        P(),
        P(),
        P(),
        P(),
        P(),
        P(),
        P(),
        P(),
        P("pb", None, None),
    )
    return jax.shard_map(
        body,
        mesh=mesh,
        in_specs=placed,
        out_specs=(
            P("pb", None, None),
            P("pb", None, None),
            P("pb", "blk", None),
            P(),
            P(),
            P(),
            P(),
            P("blk", None),
            P("blk", None),
            P("blk", None),
            P("blk", None),
            P("blk", None),
            P("blk", None),
            P("blk", None),
            P("blk", None),
            P("blk", None),
            P("blk", None),
        ),
        check_vma=False,
    )
```

```python
import functools

import jax
import jax.numpy as jnp
from jax import lax
from jax.experimental import pallas as pl
from jax.experimental.pallas import tpu as pltpu
from jax.sharding import PartitionSpec as P

EPSILON = 1e-06
MASKED = -1000000000.0
HIGHEST = lax.Precision.HIGHEST
HEAD = 64
GROUP = 4
WIDE = GROUP * HEAD
LANES = 128
LOW = jnp.bfloat16
F32 = jnp.float32
GELU_A = 0.7978845608028654
GELU_B = 0.044715
FORWARD_DEPTH = 8
BACKWARD_DEPTH = 16
FORWARD_BATCH = 4
BACKWARD_BATCH = 8


def nn(a, b):
    return jnp.dot(a, b, preferred_element_type=F32)


def nt(a, b):
    return lax.dot_general(a, b, (((1,), (1,)), ((), ())), preferred_element_type=F32)


def tn(a, b):
    return lax.dot_general(a, b, (((0,), (0,)), ((), ())), preferred_element_type=F32)


def split(values):
    high = values.astype(LOW)
    return high, (values - high.astype(F32)).astype(LOW)


def call(kernel, outs, name, args, scratch=(), smem=(), hbm=(), hbm_out=(), limit=24, aliases=None):
    spaces = [pltpu.SMEM if k in smem else pltpu.HBM if k in hbm else pltpu.VMEM for k in range(len(args))]
    out_spaces = [pltpu.HBM if k in hbm_out else pltpu.VMEM for k in range(len(outs))]
    args = [
        each if space == pltpu.SMEM else pltpu.with_memory_space_constraint(each, space)
        for each, space in zip(args, spaces)
    ]
    return pl.pallas_call(
        kernel,
        in_specs=[pl.BlockSpec(memory_space=space) for space in spaces],
        out_specs=[pl.BlockSpec(memory_space=space) for space in out_spaces],
        out_shape=[space(shape, dtype) for space, (shape, dtype) in zip(out_spaces, outs)],
        scratch_shapes=list(scratch),
        input_output_aliases=aliases or {},
        compiler_params=pltpu.CompilerParams(vmem_limit_bytes=int(limit * 2**20)),
        name=name,
    )(*args)


def copies(pairs, sems, first=0):
    started = planned(pairs, sems, first)
    for each in started:
        each.start()
    return started


def planned(pairs, sems, first=0):
    return [pltpu.make_async_copy(src, dst, sems.at[first + k]) for k, (src, dst) in enumerate(pairs)]


class Stream:
    def __init__(self, pairs, sems, depth, first=0):
        self.copies = planned(pairs, sems, first)
        self.depth, self.done = depth, 0
        for each in self.copies[:depth]:
            each.start()

    def take(self, count=1):
        for _ in range(count):
            self.copies[self.done].wait()
            if self.done + self.depth < len(self.copies):
                self.copies[self.done + self.depth].start()
            self.done += 1


def flat(ref3):
    return jnp.concatenate([ref3[:, q, :] for q in range(ref3.shape[1])], axis=0)


def unflat(dest_ref, values):
    ans, questions, _ = dest_ref.shape
    for q in range(questions):
        dest_ref[:, q, :] = values[q * ans : (q + 1) * ans]


def row_head(ans, width):
    row = lax.broadcasted_iota(jnp.int32, (GROUP * ans, width), 0)
    head = jnp.zeros_like(row)
    for k in range(1, GROUP):
        head = head + (row >= k * ans).astype(jnp.int32)
    return head


def own_columns(ans):
    col = lax.broadcasted_iota(jnp.int32, (GROUP * ans, WIDE), 1)
    return (col // HEAD) == row_head(ans, WIDE)


def own_lane(ans, group, first=0):
    col = lax.broadcasted_iota(jnp.int32, (GROUP * ans, LANES), 1)
    return col == row_head(ans, LANES) + (group * GROUP + first)


def fold(block, ans):
    half = block[: 2 * ans] + block[2 * ans :]
    return half[:ans] + half[ans:]


def spread(rows):
    twice = jnp.concatenate([rows, rows], axis=0)
    return jnp.concatenate([twice, twice], axis=0)


def block_diagonal(values_ref, dest_ref, questions, ans, groups):
    own = own_columns(ans)
    per = GROUP * ans
    for q in range(questions):
        rows = spread(values_ref[q * ans : (q + 1) * ans, :])
        for g in range(groups):
            part = jnp.where(own, rows[:, g * WIDE : (g + 1) * WIDE], 0.0)
            dest_ref[g, q * per : (q + 1) * per, :] = part.astype(LOW)


def group_rows(wide_ref, group, per):
    return jnp.concatenate([wide_ref[q, group * per : (group + 1) * per, :] for q in range(wide_ref.shape[0])], axis=0)


def project_heads(wide_ref, weight_ref, dest_ref, questions, ans, groups):
    own = own_columns(ans)
    per = GROUP * ans
    for g in range(groups):
        got = nn(group_rows(wide_ref, g, per), weight_ref[:, g * WIDE : (g + 1) * WIDE])
        for q in range(questions):
            part = jnp.where(own, got[q * per : (q + 1) * per], 0.0)
            dest_ref[q * ans : (q + 1) * ans, g * WIDE : (g + 1) * WIDE] = fold(part, ans)


def head_lanes(values, pair, rows):
    lane = lax.broadcasted_iota(jnp.int32, (rows, LANES), 1)
    return jnp.where(lane < HEAD, values[:, 2 * pair : 2 * pair + 1], values[:, 2 * pair + 1 : 2 * pair + 2])


def norm_of(values, gain):
    inv = lax.rsqrt(jnp.mean(values * values, axis=1, keepdims=True) + EPSILON)
    return inv, values * inv * gain


def norm_back(values, gain, upstream):
    inv = lax.rsqrt(jnp.mean(values * values, axis=1, keepdims=True) + EPSILON)
    unit = values * inv
    scaled = upstream * gain
    grad = inv * (scaled - unit * jnp.mean(scaled * unit, axis=1, keepdims=True))
    return grad, jnp.sum(upstream * unit, axis=0, keepdims=True)


def decoder_forward_kernel(
    ans, heads, core_ref, rel_hbm, x_hbm, bucket_hbm, gain_self_hbm, gain_cross_hbm, wq_hbm, wk_hbm, wv_hbm, wo_hbm,
    cq_hbm, ck_hbm, cv_hbm, ids_hbm, enc_hbm,
    keep_ref, give_ref, stat_ref,
    query_hbm, after_hbm, norm_one_hbm, norm_two_hbm, ctx_hbm, q_hbm, k_hbm, v_hbm, probs_hbm, a_hbm, c_hbm, p_hbm,
    rel_ref, x_ref, bucket_ref, gain_self_ref, gain_cross_ref, wq_ref, wk_ref, wv_ref, wo_ref, cq_ref, ck_ref, cv_ref,
    ids_ref, enc_ref,
    query_ref, after_ref, norm_one_ref, norm_two_ref, ctx_ref, q_ref, k_ref, v_ref, probs_ref, a_ref, c_ref, p_ref,
    bd_ref, full_scr, m_scr, l_scr, load_sems, store_sems,
):
    questions, _, features = enc_ref.shape
    rows = questions * ans
    groups = features // WIDE
    per = GROUP * ans
    first_loads = [
        (x_hbm, x_ref), (gain_self_hbm, gain_self_ref), (wq_hbm, wq_ref), (wk_hbm, wk_ref), (wv_hbm, wv_ref),
        (rel_hbm, rel_ref), (bucket_hbm, bucket_ref), (wo_hbm, wo_ref), (gain_cross_hbm, gain_cross_ref),
        (cq_hbm, cq_ref), (ck_hbm, ck_ref), (ids_hbm, ids_ref),
    ]
    enc_loads = [(enc_hbm.at[q], enc_ref.at[q]) for q in range(questions)]
    loads = Stream(first_loads + enc_loads + [(cv_hbm, cv_ref)], load_sems, FORWARD_DEPTH)
    stores = []

    def store(*pairs):
        stores.extend(copies(pairs, store_sems, len(stores)))

    loads.take(2)
    x = flat(x_ref)
    normed = norm_of(x, gain_self_ref[...])[1].astype(LOW)
    row = lax.broadcasted_iota(jnp.int32, (rows, rows), 0)
    col = lax.broadcasted_iota(jnp.int32, (rows, rows), 1)
    mask = jnp.where((col <= row) & (col >= (row // ans) * ans), 0.0, MASKED)
    first = lax.broadcasted_iota(jnp.int32, (rows, LANES), 1) < HEAD
    for weight, dest in zip((wq_ref, wk_ref, wv_ref), (q_ref, k_ref, v_ref)):
        loads.take()
        dest[...] = nn(normed, weight[...]).astype(LOW)
    store((q_ref, q_hbm), (k_ref, k_hbm), (v_ref, v_hbm))
    norm_one_ref[...] = normed
    store((norm_one_ref, norm_one_hbm))
    loads.take(2)
    bucket = jnp.concatenate([bucket_ref[...]] * questions, axis=1)
    for pair in range(heads // 2):
        at = slice(pair * LANES, (pair + 1) * LANES)
        query, key, value = q_ref[:, at], k_ref[:, at], v_ref[:, at]
        parts = []
        for half in range(2):
            head = 2 * pair + half
            bias = jnp.zeros(bucket.shape, F32)
            for b in range(rel_ref.shape[1]):
                bias = jnp.where(bucket == b, rel_ref[head, b], bias)
            twice = jnp.concatenate([bias, bias], axis=0)
            bias = jnp.concatenate([twice] * (questions // 2), axis=0)
            own = jnp.where(first if half == 0 else ~first, query.astype(F32), 0.0).astype(LOW)
            scores = nt(own, key) + bias + mask
            top = jnp.max(scores, axis=1, keepdims=True)
            probs = jnp.exp(scores - top)
            probs = probs / jnp.sum(probs, axis=1, keepdims=True)
            probs_ref[head] = probs
            parts.append(nn(probs.astype(LOW), value))
        ctx_ref[:, at] = jnp.where(first, parts[0], parts[1]).astype(LOW)
    store((probs_ref, probs_hbm))
    loads.take()
    after = x + nn(ctx_ref[...], wo_ref[...])
    after_ref[...] = after
    store((ctx_ref, ctx_hbm), (after_ref, after_hbm))
    loads.take()
    normed = norm_of(after, gain_cross_ref[...])[1].astype(LOW)
    loads.take()
    query_ref[...] = nn(normed, cq_ref[...]).astype(LOW).astype(F32)
    norm_two_ref[...] = normed
    store((norm_two_ref, norm_two_hbm), (query_ref, query_hbm))

    block_diagonal(query_ref, bd_ref, questions, ans, groups)
    loads.take()
    for g in range(groups):
        got = nt(bd_ref[g], ck_ref[:, g * WIDE : (g + 1) * WIDE]).astype(LOW)
        for q in range(questions):
            a_ref[q, g * per : (g + 1) * per, :] = got[q * per : (q + 1) * per]
    store((a_ref, a_hbm))
    loads.take()
    for q in range(questions):
        if q % FORWARD_BATCH == 0:
            loads.take(FORWARD_BATCH)
        tokens = enc_ref[q]
        scores = nt(a_ref[q], tokens) + jnp.where(ids_ref[q : q + 1, :] != 0, 0.0, MASKED)
        top = jnp.max(scores, axis=1, keepdims=True)
        probs = jnp.exp(scores - top)
        total = jnp.sum(probs, axis=1, keepdims=True)
        low = probs.astype(LOW)
        p_ref[q] = low
        c_ref[q] = nn(low, tokens).astype(LOW)
        if q % FORWARD_BATCH == FORWARD_BATCH - 1:
            span = pl.ds(q + 1 - FORWARD_BATCH, FORWARD_BATCH)
            store((p_ref.at[span], p_hbm.at[span]), (c_ref.at[span], c_hbm.at[span]))
        m_scr[q] = jnp.broadcast_to(top, m_scr.shape[1:])
        l_scr[q] = jnp.broadcast_to(total, l_scr.shape[1:])
    loads.take()
    project_heads(c_ref, cv_ref, full_scr, questions, ans, groups)
    for q in range(questions):
        stats = jnp.zeros((ans, LANES), F32)
        for src, lane in ((m_scr, 0), (l_scr, HEAD)):
            for g in range(groups):
                part = jnp.where(own_lane(ans, g, lane), src[q, g * per : (g + 1) * per, :], 0.0)
                stats = stats + fold(part, ans)
        stat_ref[q * ans : (q + 1) * ans, :] = stats
    full_scr[:, features:] = stat_ref[...]
    by_side(full_scr, (keep_ref, give_ref), core_ref)
    for each in stores:
        each.wait()


def decoder_forward(core, x, encoded, ids, buckets, rel_turned, gain_self, gain_cross, wq, wk, wv, wo, cq, ck, cv):
    ans, questions, features = x.shape
    tokens = encoded.shape[1]
    heads = rel_turned.shape[0]
    groups = features // WIDE
    rows, per = questions * ans, GROUP * ans
    low, full = ((rows, features), LOW), ((rows, features), F32)
    by_token = ((questions, groups * per, tokens), LOW)
    by_feature = ((questions, groups * per, features), LOW)
    hbm_outs = [full, full, low, low, low, low, low, low, ((heads, rows, rows), F32), by_feature, by_feature, by_token]
    packed = ((rows // 2, features + LANES), F32)
    outs = [packed, packed, ((rows, LANES), F32)]
    weights = [wq, wk, wv, wo, cq, ck, cv]
    inputs = [rel_turned, x, buckets, gain_self, gain_cross] + weights + [ids, encoded]
    return call(
        functools.partial(decoder_forward_kernel, ans, heads),
        outs + hbm_outs,
        "decoder_forward",
        [core] + inputs,
        scratch=[pltpu.SMEM(rel_turned.shape, F32)]
        + [pltpu.VMEM(each.shape, each.dtype) for each in inputs[1:]]
        + [pltpu.VMEM(shape, dtype) for shape, dtype in hbm_outs]
        + [
            pltpu.VMEM((groups, questions * per, WIDE), LOW),
            pltpu.VMEM((rows, features + LANES), F32),
            pltpu.VMEM((questions, groups * per, LANES), F32),
            pltpu.VMEM((questions, groups * per, LANES), F32),
            pltpu.SemaphoreType.DMA((13 + questions,)),
            pltpu.SemaphoreType.DMA((10 + 2 * questions,)),
        ],
        smem=(0,),
        hbm=tuple(range(1, 1 + len(inputs))),
        hbm_out=tuple(range(len(outs), len(outs) + len(hbm_outs))),
        limit=44,
    )


def by_side(dest, outs, side_ref):
    rows = outs[0].shape[0]
    side = side_ref[0]
    outs[0][...] = dest[pl.ds(pl.multiple_of(side * rows, rows), rows), :]
    outs[1][...] = dest[pl.ds(pl.multiple_of((1 - side) * rows, rows), rows), :]


def merge_kernel(heads, side_ref, mine_ref, other_ref, *refs):
    outs, out_ref = refs[:-1], refs[-1]
    rows = mine_ref.shape[0]
    features = heads * HEAD
    mine, other = mine_ref[:, features:], other_ref[:, features:]
    stat = lax.broadcasted_iota(jnp.int32, mine.shape, 1) < HEAD
    top_mine = jnp.where(stat, mine, pltpu.roll(mine, HEAD, 1))
    top_other = jnp.where(stat, other, pltpu.roll(other, HEAD, 1))
    top = jnp.maximum(top_mine, top_other)
    by_mine, by_other = jnp.exp(top_mine - top), jnp.exp(top_other - top)
    out_ref[:, features:] = jnp.where(stat, top, mine * by_mine + other * by_other)
    for pair in range(heads // 2):
        at = slice(pair * LANES, (pair + 1) * LANES)
        out_ref[:, at] = mine_ref[:, at] * head_lanes(by_mine, pair, rows) + other_ref[:, at] * head_lanes(
            by_other, pair, rows
        )
    if outs:
        by_side(out_ref, outs, side_ref)


def merge(side, mine, other, heads, halved=False):
    rows, width = mine.shape
    return call(
        functools.partial(merge_kernel, heads),
        [((rows // 2, width), F32)] * 2 if halved else [(mine.shape, F32)],
        "merge_partials",
        (side, mine, other),
        scratch=[pltpu.VMEM(mine.shape, F32)] if halved else [],
        smem=(0,),
        limit=4,
    )


def join_kernel(side_ref, mine_ref, other_ref, out_ref):
    rows = mine_ref.shape[0]
    side = side_ref[0]
    out_ref[pl.ds(pl.multiple_of(side * rows, rows), rows), :] = mine_ref[...]
    out_ref[pl.ds(pl.multiple_of((1 - side) * rows, rows), rows), :] = other_ref[...]


def join(side, mine, other):
    rows, width = mine.shape
    return call(join_kernel, [((2 * rows, width), F32)], "join_halves", (side, mine, other), smem=(0,), limit=4)[0]


def decoder_backward_kernel(
    ans, heads, blocks, core_ref, own_ref, other_ref, stat_ref, after_hbm, cot_hbm, gain_hbm, co_hbm,
    fin_hbm, fout_hbm, cv_hbm, ck_hbm, enc_hbm, p_hbm,
    keep_ref, give_ref, gctx_ref, w_ref, wide_ref,
    out_hbm, gain_grad_hbm, gac_hbm, ctx_hbm, norm_hbm, active_hbm, inner_hbm, gcross_hbm, gout_hbm, s_hbm, b_hbm,
    after_ref, cot_ref, gain_ref, co_ref, fin_ref, fout_ref, cv_ref, ck_ref, enc_ref, p_ref,
    out_ref, gain_grad_ref, gac_ref, ctx_ref, norm_ref, active_ref, inner_ref, gcross_ref, gout_ref, s_ref, b_ref,
    full_scr, delta_ref, bd_ref, back_scr, raw_scr, w_scr, d_scr, load_sems, store_sems,
):
    questions, _, features = enc_ref.shape
    rows, per = questions * ans, GROUP * ans
    groups = features // WIDE
    hidden = fin_ref.shape[1]
    width = hidden // blocks
    spans = [slice(c * width, (c + 1) * width) for c in range(blocks)]
    pairs = [(co_hbm, co_ref), (after_hbm, after_ref), (gain_hbm, gain_ref), (cot_hbm, cot_ref)]
    for at in spans:
        pairs += [(fin_hbm.at[:, at], fin_ref.at[:, at]), (fout_hbm.at[at, :], fout_ref.at[at, :])]
    pairs += [(cv_hbm, cv_ref)]
    for q in range(questions):
        pairs += [(enc_hbm.at[q], enc_ref.at[q]), (p_hbm.at[q], p_ref.at[q])]
    loads = Stream(pairs + [(ck_hbm, ck_ref)], load_sems, BACKWARD_DEPTH)
    stores = []

    def store(*pairs):
        stores.extend(copies(pairs, store_sems, len(stores)))

    core = core_ref[0]
    half = own_ref.shape[0]
    full_scr[pl.ds(pl.multiple_of(core * half, half), half), :] = own_ref[...]
    full_scr[pl.ds(pl.multiple_of((1 - core) * half, half), half), :] = other_ref[...]
    stats = full_scr[:, features:]
    lane = lax.broadcasted_iota(jnp.int32, stats.shape, 1)
    used = lane < heads
    inverse = jnp.where(used, 1.0 / jnp.where(used, pltpu.roll(stats, HEAD, 1), 1.0), 0.0)
    w_ref[...] = jnp.where(used, jnp.exp(jnp.where(used, stat_ref[...] - stats, 0.0)) * inverse, 0.0)
    for pair in range(heads // 2):
        at = slice(pair * LANES, (pair + 1) * LANES)
        ctx_ref[:, at] = full_scr[:, at] * head_lanes(inverse, pair, rows)
    store((ctx_ref, ctx_hbm))
    high, low = split(ctx_ref[...])
    loads.take(2)
    after = after_ref[...] + (nn(high, co_ref[...]) + nn(low, co_ref[...]))
    loads.take(2)
    gain = gain_ref[...]
    normed = norm_of(after, gain)[1].astype(LOW)
    norm_ref[...] = normed
    cot = flat(cot_ref)
    gout = cot.astype(LOW)
    gout_ref[...] = gout
    store((norm_ref, norm_hbm), (gout_ref, gout_hbm))
    total = jnp.zeros((rows, features), F32)
    back = jnp.zeros((rows, features), F32)
    for at in spans:
        loads.take()
        inner = nn(normed, fin_ref[:, at])
        square = inner * inner
        wave = jnp.tanh(GELU_A * inner * (1.0 + GELU_B * square))
        active = (0.5 * inner * (1.0 + wave)).astype(LOW)
        slope = 0.5 * (1.0 + wave) + 0.5 * inner * (1.0 - wave * wave) * (GELU_A * (1.0 + 3.0 * GELU_B * square))
        active_ref[:, at] = active
        loads.take()
        total = total + nn(active, fout_ref[at, :])
        grad_active = nt(gout, fout_ref[at, :]).astype(LOW).astype(F32)
        grad_inner = (grad_active * slope).astype(LOW)
        inner_ref[:, at] = grad_inner
        back = back + nt(grad_inner, fin_ref[:, at])
    unflat(out_ref, after + total)
    store((active_ref, active_hbm), (inner_ref, inner_hbm), (out_ref, out_hbm))
    grad, gain_grad = norm_back(after, gain, back)
    gain_grad_ref[...] = gain_grad
    gac = cot + grad
    gac_ref[...] = gac
    gcross = gac.astype(LOW)
    gcross_ref[...] = gcross
    gctx = nt(gcross, co_ref[...]).astype(LOW).astype(F32)
    gctx_ref[...] = gctx
    store((gac_ref, gac_hbm), (gcross_ref, gcross_hbm), (gain_grad_ref, gain_grad_hbm))
    select_row = lax.broadcasted_iota(jnp.int32, (features, LANES), 0) // HEAD
    select = jnp.where(select_row == lax.broadcasted_iota(jnp.int32, (features, LANES), 1), 1.0, 0.0).astype(LOW)
    high, low = split(gctx * ctx_ref[...])
    delta_ref[...] = nn(high, select) + nn(low, select)

    block_diagonal(gctx_ref, bd_ref, questions, ans, groups)
    for q in range(questions):
        for src, dst in ((w_ref, w_scr), (delta_ref, d_scr)):
            wide_rows = spread(src[q * ans : (q + 1) * ans, :])
            for g in range(groups):
                part = jnp.sum(jnp.where(own_lane(ans, g), wide_rows, 0.0), axis=1, keepdims=True)
                dst[q, g * per : (g + 1) * per, :] = jnp.broadcast_to(part, (per, LANES))
    loads.take()
    for g in range(groups):
        got = nt(bd_ref[g], cv_ref[:, g * WIDE : (g + 1) * WIDE])
        for q in range(questions):
            part = got[q * per : (q + 1) * per]
            raw_scr[q, g * per : (g + 1) * per, :] = part.astype(LOW)
            b_ref[q, g * per : (g + 1) * per, :] = (part * w_scr[q, g * per : (g + 1) * per, :1]).astype(LOW)
    store((b_ref, b_hbm))
    for q in range(questions):
        if q % BACKWARD_BATCH == 0:
            loads.take(2 * BACKWARD_BATCH)
        tokens = enc_ref[q]
        grad_probs = nt(raw_scr[q], tokens)
        probs = p_ref[q].astype(F32) * w_scr[q][:, :1]
        grad_scores = (probs * (grad_probs - d_scr[q][:, :1])).astype(LOW)
        s_ref[q] = grad_scores
        wide_ref[q] = nn(grad_scores, tokens).astype(LOW)
        if q % BACKWARD_BATCH == BACKWARD_BATCH - 1:
            span = pl.ds(q + 1 - BACKWARD_BATCH, BACKWARD_BATCH)
            store((s_ref.at[span], s_hbm.at[span]))
    loads.take()
    project_heads(wide_ref, ck_ref, back_scr, questions, ans, groups)
    by_side(back_scr, (keep_ref, give_ref), core_ref)
    for each in stores:
        each.wait()


def decoder_backward(core, own, other, stat, after, cot, gain, co, fin, fout, cv, ck, encoded, probs, heads):
    rows, features = after.shape
    ans, questions, _ = cot.shape
    tokens = encoded.shape[1]
    groups, per = features // WIDE, GROUP * ans
    hidden = fin.shape[1]
    blocks = 6
    low, full = ((rows, features), LOW), ((rows, features), F32)
    thin = ((rows, LANES), F32)
    wide = ((rows, hidden), LOW)
    half = ((rows // 2, features), F32)
    by_token = ((questions, groups * per, tokens), LOW)
    by_feature = ((questions, groups * per, features), LOW)
    outs = [half, half, full, thin, by_feature]
    hbm_outs = [(cot.shape, F32), ((1, features), F32), full, full, low, wide, wide, low, low, by_token, by_feature]
    inputs = [after, cot, gain, co, fin, fout, cv, ck, encoded, probs]
    return call(
        functools.partial(decoder_backward_kernel, ans, heads, blocks),
        outs + hbm_outs,
        "decoder_backward",
        [core, own, other, stat] + inputs,
        scratch=[pltpu.VMEM(each.shape, each.dtype) for each in inputs]
        + [pltpu.VMEM(shape, dtype) for shape, dtype in hbm_outs]
        + [
            pltpu.VMEM((rows, features + LANES), F32),
            pltpu.VMEM((rows, LANES), F32),
            pltpu.VMEM((groups, questions * per, WIDE), LOW),
            pltpu.VMEM((rows, features), F32),
            pltpu.VMEM(by_feature[0], LOW),
            pltpu.VMEM((questions, groups * per, LANES), F32),
            pltpu.VMEM((questions, groups * per, LANES), F32),
            pltpu.SemaphoreType.DMA((6 + 2 * blocks + 2 * questions,)),
            pltpu.SemaphoreType.DMA((10 + questions,)),
        ],
        smem=(0,),
        hbm=tuple(range(4, 4 + len(inputs))),
        hbm_out=tuple(range(len(outs), len(outs) + len(hbm_outs))),
        limit=54,
    )


def window(ref, index, share):
    start = index * share
    base = jnp.minimum((start // LANES) * LANES, ref.shape[1] - 2 * LANES)
    block = ref[:, pl.ds(pl.multiple_of(base, LANES), 2 * LANES)].astype(F32)
    return pltpu.roll(block, lax.rem(2 * LANES - (start - base), 2 * LANES), 1)[:, :share]


def weight_kernel(
    share, hidden_share, index_ref, active_hbm, inner_hbm, norm_hbm, gout_hbm, gcross_hbm, ctx_hbm, out_ref,
    active_ref, inner_ref, norm_ref, gout_ref, gcross_ref, ctx_ref, sems,
):
    loads = Stream(
        [(norm_hbm, norm_ref), (inner_hbm, inner_ref), (active_hbm, active_ref), (gout_hbm, gout_ref),
         (ctx_hbm, ctx_ref), (gcross_hbm, gcross_ref)],
        sems,
        3,
    )
    index = index_ref[0]
    features = gout_ref.shape[1]
    loads.take(2)
    normed = window(norm_ref, index, share).astype(LOW)
    at = 0
    for c in range(inner_ref.shape[1] // features):
        out_ref[at : at + share, :] = tn(normed, inner_ref[:, c * features : (c + 1) * features])
        at += share
    loads.take(2)
    out_ref[at : at + hidden_share, :] = tn(window(active_ref, index, hidden_share).astype(LOW), gout_ref[...])
    at += hidden_share
    loads.take(2)
    high, low = split(window(ctx_ref, index, share))
    out_ref[at : at + share, :] = tn(high, gcross_ref[...]) + tn(low, gcross_ref[...])


def weight_gradients(index, active, inner, norm, gout, gcross, ctx, share, hidden_share):
    features, hidden = gout.shape[1], inner.shape[1]
    inputs = [active, inner, norm, gout, gcross, ctx]
    rows = share * (hidden // features) + hidden_share + share
    return call(
        functools.partial(weight_kernel, share, hidden_share),
        [((rows, features), F32)],
        "weight_gradients",
        [index] + inputs,
        scratch=[pltpu.VMEM(each.shape, each.dtype) for each in inputs] + [pltpu.SemaphoreType.DMA((6,))],
        smem=(0,),
        hbm=tuple(range(1, 7)),
        limit=16,
    )[0]


def weight_sum_kernel(
    share, hidden_share, mine_hbm, other_hbm, fin_hbm, fout_hbm, co_hbm,
    mine_ref, other_ref, fin_ref, fout_ref, co_ref, sems,
):
    for load in copies([(mine_hbm, mine_ref), (other_hbm, other_ref)], sems):
        load.wait()
    features = mine_ref.shape[1]
    at = 0
    for c in range(fin_ref.shape[1] // features):
        fin_ref[:, c * features : (c + 1) * features] = mine_ref[at : at + share, :] + other_ref[at : at + share, :]
        at += share
    fout_ref[...] = mine_ref[at : at + hidden_share, :] + other_ref[at : at + hidden_share, :]
    at += hidden_share
    co_ref[...] = mine_ref[at : at + share, :] + other_ref[at : at + share, :]
    for each in copies([(fin_ref, fin_hbm), (fout_ref, fout_hbm), (co_ref, co_hbm)], sems, 2):
        each.wait()


def weight_sum(mine, other, share, hidden_share, hidden):
    features = mine.shape[1]
    outs = [((share, hidden), F32), ((hidden_share, features), F32), ((share, features), F32)]
    return call(
        functools.partial(weight_sum_kernel, share, hidden_share),
        outs,
        "weight_sum",
        (mine, other),
        scratch=[pltpu.VMEM(mine.shape, F32)] * 2
        + [pltpu.VMEM(shape, dtype) for shape, dtype in outs]
        + [pltpu.SemaphoreType.DMA((5,))],
        hbm=(0, 1),
        hbm_out=(0, 1, 2),
        limit=8,
    )


def last_sum_kernel(stacks, side_ref, *refs):
    count = 2 * (stacks + 2)
    inputs, refs = refs[:count], refs[count:]
    sems = refs[-1]
    places = refs[len(refs) - 1 - count : -1]
    outs = refs[: (len(refs) - 1 - count) // 2]
    held = refs[len(outs) : 2 * len(outs)]
    for load in copies(list(zip(inputs, places)), sems):
        load.wait()
    at = 0
    for k in range(stacks):
        mine, other = places[2 * k], places[2 * k + 1]
        for row in range(mine.shape[0]):
            held[at][...] = mine[row] + other[row]
            at += 1
    side = side_ref[0]
    width = places[2 * stacks].shape[2]
    for part, place in zip(places[2 * stacks : 2 * stacks + 2], (side, 1 - side)):
        held[at][:, pl.ds(pl.multiple_of(place * width, width), width)] = part[0]
    at += 1
    total = places[-2][...] + places[-1][...]
    for k in range(3):
        held[at + k][...] = total[k]
    heads, buckets = held[at + 3].shape
    held[at + 3][...] = total[8 : 8 + heads, :buckets]
    for each in copies(list(zip(held, outs)), sems, count):
        each.wait()


def last_sum(side, pairs, halves, small, bias_shape):
    inputs = [each for pair in pairs + [halves, small] for each in pair]
    row = ((small[0].shape[1],), F32)
    outs = [(mine.shape[1:], F32) for mine, _ in pairs for _ in range(mine.shape[0])]
    outs += [outs[-1], row, row, row, (bias_shape, F32)]
    return call(
        functools.partial(last_sum_kernel, len(pairs)),
        outs,
        "last_sum",
        [side] + inputs,
        scratch=[pltpu.VMEM(shape, dtype) for shape, dtype in outs]
        + [pltpu.VMEM(each.shape, each.dtype) for each in inputs]
        + [pltpu.SemaphoreType.DMA((len(outs) + len(inputs),))],
        smem=(0,),
        hbm=tuple(range(1, 1 + len(inputs))),
        hbm_out=tuple(range(len(outs))),
        limit=16,
    )


def encoded_kernel(start, stop, has_base, s_hbm, p_hbm, a_hbm, b_hbm, *refs):
    out_ref, s_ref, p_ref, a_ref, b_ref, slots, in_sems, sems = refs[1:] if has_base else refs
    count = stop - start
    pairs = ((p_hbm, p_ref), (b_hbm, b_ref), (s_hbm, s_ref), (a_hbm, a_ref))
    loads = Stream([(src.at[start + k], dst.at[k]) for k in range(count) for src, dst in pairs], in_sems, 8)

    def copy(k, slot):
        return pltpu.make_async_copy(slots.at[slot], out_ref.at[start + k], sems.at[slot])

    for k in range(count):
        if k % 2 == 0:
            loads.take(8)
            if k >= 4:
                copy(k - 4, k % 4).wait()
                copy(k - 3, (k + 1) % 4).wait()
        slots[k % 4] = (tn(p_ref[k], b_ref[k]) + tn(s_ref[k], a_ref[k])).astype(LOW)
        if k % 2 == 1:
            copy(k - 1, (k - 1) % 4).start()
            copy(k, k % 4).start()
    for k in range(max(count - 4, 0), count):
        copy(k, k % 4).wait()


def encoded_gradient(grad_scores, probs, a, b, start, stop, base=None):
    questions, _, tokens = probs.shape
    features = a.shape[2]
    args = [grad_scores, probs, a, b] + ([] if base is None else [base])
    return call(
        functools.partial(encoded_kernel, start, stop, base is not None),
        [((questions, tokens, features), LOW)],
        "encoded_gradient",
        args,
        scratch=[pltpu.VMEM((stop - start,) + x.shape[1:], LOW) for x in (grad_scores, probs, a, b)]
        + [
            pltpu.VMEM((4, tokens, features), LOW),
            pltpu.SemaphoreType.DMA((4 * (stop - start),)),
            pltpu.SemaphoreType.DMA((4,)),
        ],
        hbm=tuple(range(len(args))),
        hbm_out=(0,),
        limit=26,
        aliases={} if base is None else {4: 0},
    )[0]


def split_owner(full_ref, outs, core_ref):
    count, share, _ = outs[0].shape
    core = core_ref[0]
    for k in range(count):
        for out, side in zip(outs, (core, 1 - core)):
            out[k] = full_ref[pl.ds(pl.multiple_of((2 * k + side) * share, share), share), :]


def key_value_kernel(ans, core_ref, wide_ref, gctx_ref, w_ref, c_hbm, query_hbm, *refs):
    outs, (c_ref, query_ref, blocks_ref, scaled_ref, full_ref, sems) = refs[:-6], refs[-6:]
    questions, per = wide_ref.shape[0], GROUP * ans
    groups = wide_ref.shape[2] // WIDE
    loads = Stream([(query_hbm, query_ref), (c_hbm, c_ref)], sems, 2)
    for pair in range(groups * GROUP // 2):
        at = slice(pair * LANES, (pair + 1) * LANES)
        scaled_ref[:, at] = gctx_ref[:, at] * head_lanes(w_ref[...], pair, gctx_ref.shape[0])
    loads.take()
    count = len(outs) // 2
    for left, values, dests in ((wide_ref, query_ref, outs[:count]), (c_ref, scaled_ref, outs[count:])):
        block_diagonal(values, blocks_ref, questions, ans, groups)
        if left is c_ref:
            loads.take()
        dest = full_ref if count == 2 else dests[0]
        for g in range(groups):
            dest[:, g * WIDE : (g + 1) * WIDE] = tn(group_rows(left, g, per), blocks_ref[g])
        if count == 2:
            split_owner(full_ref, dests, core_ref)


def key_value_gradients(core, wide, gctx, weight, ctx_wide, query, count, ans):
    questions, _, features = wide.shape
    groups, per = features // WIDE, GROUP * ans
    share = features // count
    split_rows = share % 8 == 0
    half = ((count // 2, share, features), F32)
    outs = call(
        functools.partial(key_value_kernel, ans),
        [half] * 4 if split_rows else [((features, features), F32)] * 2,
        "key_value_gradients",
        (core, wide, gctx, weight, ctx_wide, query),
        scratch=[
            pltpu.VMEM(ctx_wide.shape, LOW),
            pltpu.VMEM(query.shape, F32),
            pltpu.VMEM((groups, questions * per, WIDE), LOW),
            pltpu.VMEM(gctx.shape, F32),
            pltpu.VMEM((features, features), F32),
            pltpu.SemaphoreType.DMA((2,)),
        ],
        smem=(0,),
        hbm=(4, 5),
        limit=16,
    )
    if split_rows:
        return outs
    pairs = [each.reshape(count // 2, 2, share, features) for each in outs]
    return [
        lax.dynamic_index_in_dim(each, side, 1, keepdims=False) for each in pairs for side in (core[0], 1 - core[0])
    ]


def halve_kernel(place, side_ref, keep_ref, got_ref, *outs):
    count = keep_ref.shape[0]
    if count == 1:
        outs[0][...] = keep_ref[...] + got_ref[...]
        return
    side = side_ref[0]
    low = 1 << place
    for k in range(count // 2):
        base = (k // low) * 2 * low + k % low
        for out, bit in zip(outs, (side, 1 - side)):
            at = base + bit * low
            out[k] = keep_ref[at] + got_ref[at]


def halve_columns_kernel(side_ref, keep_ref, got_ref, *outs):
    width = outs[0].shape[2]
    side = side_ref[0]
    for out, at in zip(outs, (side, 1 - side)):
        span = pl.ds(pl.multiple_of(at * width, width), width)
        out[...] = keep_ref[:, :, span] + got_ref[:, :, span]


def halve_columns(side, keep, got):
    count, share, width = keep.shape
    half = ((count, share, width // 2), F32)
    return call(halve_columns_kernel, [half, half], "halve_columns", (side, keep, got), smem=(0,), limit=8)


def halve(side, keep, got, place):
    count = keep.shape[0]
    half = ((max(count // 2, 1),) + keep.shape[1:], F32)
    return call(
        functools.partial(halve_kernel, place),
        [half] if count == 1 else [half, half],
        "halve_blocks",
        (side, keep, got),
        smem=(0,),
        limit=8,
    )


def self_backward_kernel(
    ans, share, core_ref, index_ref, own_ref, other_ref, *refs,
):
    inputs = refs[:19]
    packed_hbm, small_hbm, grad_in_hbm = refs[19:22]
    (
        cq_ref, after_ref, gain_cross_ref, gac_ref, wo_ref, norm_two_ref, ctx_ref, v_ref, k_ref, q_ref, probs_ref,
        norm_one_ref, bucket_ref, gain_ffn_grad_ref, wq_ref, wk_ref, wv_ref, x_ref, gain_self_ref,
    ) = places = refs[22:41]
    packed_ref, small_ref, grad_in_ref, gq_ref, gctx_ref, gqkv_ref, table_ref, sems, store_sems = refs[41:]
    rows, features = gac_ref.shape
    heads = probs_ref.shape[0]
    loads = Stream(list(zip(inputs, places)), sems, 8)
    half = own_ref.shape[0]
    core, index = core_ref[0], index_ref[0]
    gq_ref[pl.ds(pl.multiple_of(core * half, half), half), :] = own_ref[...]
    gq_ref[pl.ds(pl.multiple_of((1 - core) * half, half), half), :] = other_ref[...]
    high, low = split(gq_ref[...])
    loads.take()
    upstream = nt(high, cq_ref[...]) + nt(low, cq_ref[...])
    loads.take(6)
    grad, gain_cross_grad = norm_back(after_ref[...], gain_cross_ref[...], upstream)
    gas = gac_ref[...] + grad
    gself = gas.astype(LOW)
    gctx_ref[...] = nt(gself, wo_ref[...]).astype(LOW)
    normed = window(norm_two_ref, index, share).astype(LOW)
    packed_ref[0] = tn(normed, high) + tn(normed, low)
    packed_ref[1] = tn(window(ctx_ref, index, share).astype(LOW), gself)
    loads.take(6)
    first = lax.broadcasted_iota(jnp.int32, (rows, LANES), 1) < HEAD
    for pair in range(heads // 2):
        at = slice(pair * LANES, (pair + 1) * LANES)
        query, key, value, grad_ctx = q_ref[:, at], k_ref[:, at], v_ref[:, at], gctx_ref[:, at]
        gqs, gks, gvs = [], [], []
        for part in range(2):
            head = 2 * pair + part
            own = jnp.where(first if part == 0 else ~first, grad_ctx.astype(F32), 0.0).astype(LOW)
            grad_probs = nt(own, value)
            probs = probs_ref[head]
            grad_scores = probs * (grad_probs - jnp.sum(probs * grad_probs, axis=1, keepdims=True))
            blocks = [grad_scores[k * 2 * ans : (k + 1) * 2 * ans] for k in range(rows // (2 * ans))]
            both = functools.reduce(lambda a, b: a + b, blocks)
            table_ref[head] = both[:ans] + both[ans:]
            low_scores = grad_scores.astype(LOW)
            gqs.append(nn(low_scores, key))
            gks.append(tn(low_scores, query))
            gvs.append(tn(probs.astype(LOW), grad_ctx))
        for k, parts in enumerate((gqs, gks, gvs)):
            place = slice(k * features + pair * LANES, k * features + (pair + 1) * LANES)
            gqkv_ref[:, place] = jnp.where(first, parts[0], parts[1]).astype(LOW)
    normed = window(norm_one_ref, index, share).astype(LOW)
    for k in range(3):
        packed_ref[2 + k] = tn(normed, gqkv_ref[:, k * features : (k + 1) * features])
    stores = copies([(packed_ref, packed_hbm)], store_sems)
    total = jnp.zeros((heads, LANES), F32)
    which = lax.broadcasted_iota(jnp.int32, (LANES, rows), 0)
    wide_bucket = jnp.concatenate([bucket_ref[...]] * (rows // ans), axis=1)
    for i in range(ans):
        hot = jnp.where(which == wide_bucket[i : i + 1, :], 1.0, 0.0).astype(LOW)
        table_high, table_low = split(table_ref[:, i, :])
        total = total + (nt(table_high, hot) + nt(table_low, hot))
    loads.take(6)
    upstream = jnp.zeros((rows, features), F32)
    for k, weight in enumerate((wq_ref, wk_ref, wv_ref)):
        upstream = upstream + nt(gqkv_ref[:, k * features : (k + 1) * features], weight[...])
    grad, gain_self_grad = norm_back(flat(x_ref), gain_self_ref[...], upstream)
    small_ref[...] = jnp.zeros(small_ref.shape, F32)
    for k, row in enumerate((gain_self_grad, gain_cross_grad, gain_ffn_grad_ref[...])):
        small_ref[k : k + 1, :] = row
    small_ref[8 : 8 + heads, :LANES] = total
    unflat(grad_in_ref, gas + grad)
    for each in stores + copies([(small_ref, small_hbm), (grad_in_ref, grad_in_hbm)], store_sems, 1):
        each.wait()


def self_backward(core, index, own, other, inputs, ans, share):
    gac, probs, x = inputs[3], inputs[10], inputs[17]
    rows, features = gac.shape
    heads = probs.shape[0]
    outs = [((5, share, features), F32), ((8 + heads, features), F32), (x.shape, F32)]
    return call(
        functools.partial(self_backward_kernel, ans, share),
        outs,
        "self_backward",
        [core, index, own, other] + inputs,
        scratch=[pltpu.VMEM(each.shape, each.dtype) for each in inputs]
        + [pltpu.VMEM(shape, dtype) for shape, dtype in outs]
        + [
            pltpu.VMEM((rows, features), F32),
            pltpu.VMEM((rows, features), LOW),
            pltpu.VMEM((rows, 3 * features), LOW),
            pltpu.VMEM((heads, ans, rows), F32),
            pltpu.SemaphoreType.DMA((len(inputs),)),
            pltpu.SemaphoreType.DMA((3,)),
        ],
        smem=(0, 1),
        hbm=tuple(range(4, 4 + len(inputs))),
        hbm_out=(0, 1, 2),
        limit=24,
    )


def partner(value, axis, bit):
    count = lax.axis_size(axis)
    return lax.ppermute(value, axis, [(k, k ^ bit) for k in range(count)])


def axis_bits(axis):
    bits, bit = [], 1
    while bit < lax.axis_size(axis):
        bits.append(bit)
        bit *= 2
    return bits


def add_kernel(side_ref, a_ref, b_ref, *refs):
    outs, out_ref = refs[:-1], refs[-1]
    out_ref[...] = a_ref[...] + b_ref[...]
    if outs:
        by_side(out_ref, outs, side_ref)


def add(side, a, b, halved=False):
    rows, width = a.shape
    return call(
        add_kernel,
        [((rows // 2, width), F32)] * 2 if halved else [(a.shape, F32)],
        "add_partials",
        (side, a, b),
        scratch=[pltpu.VMEM(a.shape, F32)] if halved else [],
        smem=(0,),
        limit=4,
    )


def exchange(keep, give, combine, sides):
    bits = axis_bits("blk")
    keep, give = combine(sides[1], keep, partner(give, "blk", bits[0]), True)
    (keep,) = combine(sides[1], keep, partner(give, "blk", bits[1]), False)
    for bit in bits[2:]:
        (keep,) = combine(sides[1], keep, partner(keep, "blk", bit), False)
    keep = join(sides[1], keep, partner(keep, "blk", bits[1]))
    return keep, partner(keep, "blk", bits[0])


def after(value, *others):
    return lax.optimization_barrier((value,) + others)[0]


def body(
    decoder_in, encoded, key_ids, buckets, gain_self, gain_cross, gain_ffn, rel_bias, self_q, self_k, self_v, self_o,
    cross_q, cross_k, cross_v, cross_o, ffn_in, ffn_out, cotangent,
):
    questions, ans, features = decoder_in.shape
    heads = rel_bias.shape[1]
    hidden = ffn_in.shape[1]
    blk_count = lax.axis_size("blk")
    blk_index = lax.axis_index("blk")
    index, core = blk_index.reshape(1), (blk_index % 2).reshape(1)
    share, hidden_share = features // blk_count, hidden // blk_count
    bits = axis_bits("blk")
    sides = [((blk_index // bit) % 2).reshape(1) for bit in bits[:2]]
    turned_in, turned_cot = jnp.transpose(decoder_in, (1, 0, 2)), jnp.transpose(cotangent, (1, 0, 2))
    (
        keep, give, stat, query, after_self, norm_one, norm_two, ctx_self, qs, ks, vs, probs_self, q_wide, ctx_wide,
        probs,
    ) = decoder_forward(
        core, turned_in, encoded, key_ids, buckets, rel_bias.T, gain_self, gain_cross, self_q, self_k, self_v, self_o,
        cross_q, cross_k, cross_v,
    )
    keep, other = exchange(keep, give, lambda s, a, b, halved: merge(s, a, b, heads, halved), sides)
    (
        keep, give, gctx, weight, query_wide, output, grad_gain_ffn, gac, context, norm_three, active, grad_inner,
        gcross, gout, grad_scores, g_wide,
    ) = decoder_backward(
        core, keep, other, stat, after_self, turned_cot, gain_ffn, cross_o, ffn_in, ffn_out, cross_v, cross_k, encoded,
        probs, heads,
    )

    def scatter_step(state, bit, *others):
        held, got, left = state
        place = sum(1 for b in left if b < bit)
        side = ((blk_index // bit) % 2).reshape(1)
        held, give = halve(side, held, after(got, *others), place)
        return held, partner(give, "blk", bit), [b for b in left if b != bit]

    pb_side = lax.axis_index("pb").reshape(1)
    got = partner(give, "blk", bits[0])
    key_keep, key_give, value_keep, value_give = key_value_gradients(
        core, query_wide, gctx, weight, ctx_wide, query, blk_count, ans
    )
    key_state = (key_keep, partner(key_give, "blk", bits[0]), list(bits[1:]))
    value_got = partner(value_give, "blk", bits[0])
    keep, give = add(sides[1], keep, after(got, value_keep), True)
    got = partner(give, "blk", bits[1])
    value_keep, value_give = halve_columns(pb_side, value_keep, after(value_got, keep))
    value_state = (value_keep, partner(value_give, "pb", 1), list(bits[1:]))
    (keep,) = add(sides[1], keep, after(got, value_keep))
    got = partner(keep, "blk", bits[2])
    key_state = scatter_step(key_state, bits[1], keep)
    for bit in bits[3:]:
        (keep,) = add(sides[1], keep, after(got, key_state[0]))
        got = partner(keep, "blk", bit)
    packed = weight_gradients(
        index, after(active, keep), grad_inner, norm_three, gout, gcross, context, share, hidden_share
    )
    packed_got = partner(packed, "pb", 1)
    value_state = scatter_step(value_state, bits[1], packed)
    (keep,) = add(sides[1], keep, after(got, value_state[0]))
    got = partner(keep, "blk", bits[1])
    key_state = scatter_step(key_state, bits[2], keep)
    keep = join(sides[1], keep, after(got, key_state[0]))
    other = partner(keep, "blk", bits[0])
    value_state = scatter_step(value_state, bits[2], keep)
    stack, small, grad_in = self_backward(
        core, index, keep, after(other, value_state[0]),
        [
            cross_q, after_self, gain_cross, gac, self_o, norm_two, ctx_self, vs, ks, qs, probs_self, norm_one, buckets,
            grad_gain_ffn, self_q, self_k, self_v, turned_in, gain_self,
        ],
        ans, share,
    )
    stack_got, small_got = partner(stack, "pb", 1), partner(small, "pb", 1)
    last = stack
    for bit in bits[3:]:
        key_state = scatter_step(key_state, bit, last)
        value_state = scatter_step(value_state, bit, key_state[0])
        last = value_state[0]
    middle = questions // 2
    grad_encoded = encoded_gradient(after(grad_scores, last), probs, q_wide, g_wide, 0, middle)
    zero = jnp.zeros((1,), jnp.int32)
    grad_cross_k = halve(zero, key_state[0], after(key_state[1], grad_encoded), 0)[0]
    key_got = partner(grad_cross_k, "pb", 1)
    grad_cross_v = halve(zero, value_state[0], after(value_state[1], grad_cross_k), 0)[0]
    value_got = partner(grad_cross_v, "pb", 1)
    grad_encoded = encoded_gradient(
        after(grad_scores, grad_cross_v), probs, q_wide, g_wide, middle, questions, grad_encoded
    )
    grad_ffn_in, grad_ffn_out, grad_cross_o = weight_sum(
        after(packed, grad_encoded), packed_got, share, hidden_share, hidden
    )
    (
        grad_cross_q, grad_self_o, grad_self_q, grad_self_k, grad_self_v, grad_cross_k, grad_cross_v, gain_self_sum,
        gain_cross_sum, gain_ffn_sum, bias_sum,
    ) = last_sum(
        pb_side, [(after(stack, grad_cross_o), stack_got), (grad_cross_k, key_got)], (grad_cross_v, value_got),
        (small, small_got), rel_bias.shape[::-1],
    )
    return (
        jnp.transpose(output, (1, 0, 2)),
        jnp.transpose(grad_in, (1, 0, 2)),
        grad_encoded,
        gain_self_sum,
        gain_cross_sum,
        gain_ffn_sum,
        bias_sum.T,
        grad_self_q,
        grad_self_k,
        grad_self_v,
        grad_self_o,
        grad_cross_q,
        grad_cross_k,
        grad_cross_v,
        grad_cross_o,
        grad_ffn_in,
        grad_ffn_out,
    )


def solution(mesh):
    rows, tokens, share = P("pb", None, None), P("pb", "blk", None), P("blk", None)
    return jax.shard_map(
        body,
        mesh=mesh,
        in_specs=(rows, tokens, P("pb", "blk")) + (P(),) * 15 + (rows,),
        out_specs=(rows, rows, tokens) + (P(),) * 4 + (share,) * 10,
        check_vma=False,
    )
```

```python
import functools

import jax
import jax.numpy as jnp
from jax import lax
from jax.experimental import pallas as pl
from jax.experimental.pallas import tpu as pltpu
from jax.sharding import PartitionSpec as P

EPSILON = 1e-06
MASKED = -1000000000.0
HIGHEST = lax.Precision.HIGHEST
HEAD = 64
GROUP = 4
WIDE = GROUP * HEAD
LANES = 128
LOW = jnp.bfloat16
F32 = jnp.float32
GELU_A = 0.7978845608028654
GELU_B = 0.044715
FORWARD_DEPTH = 8
BACKWARD_DEPTH = 16
FORWARD_BATCH = 4
BACKWARD_BATCH = 8
SELF_US = 0.1
LAST_US = 0.1


def nn(a, b):
    return jnp.dot(a, b, preferred_element_type=F32)


def nt(a, b):
    return lax.dot_general(a, b, (((1,), (1,)), ((), ())), preferred_element_type=F32)


def tn(a, b):
    return lax.dot_general(a, b, (((0,), (0,)), ((), ())), preferred_element_type=F32)


def split(values):
    high = values.astype(LOW)
    return high, (values - high.astype(F32)).astype(LOW)


def call(kernel, outs, name, args, scratch=(), smem=(), hbm=(), hbm_out=(), limit=24, aliases=None, us=1.0):
    spaces = [pltpu.SMEM if k in smem else pltpu.HBM if k in hbm else pltpu.VMEM for k in range(len(args))]
    out_spaces = [pltpu.HBM if k in hbm_out else pltpu.VMEM for k in range(len(outs))]
    args = [
        each if space == pltpu.SMEM else pltpu.with_memory_space_constraint(each, space)
        for each, space in zip(args, spaces)
    ]
    return pl.pallas_call(
        kernel,
        in_specs=[pl.BlockSpec(memory_space=space) for space in spaces],
        out_specs=[pl.BlockSpec(memory_space=space) for space in out_spaces],
        out_shape=[space(shape, dtype) for space, (shape, dtype) in zip(out_spaces, outs)],
        scratch_shapes=list(scratch),
        input_output_aliases=aliases or {},
        compiler_params=pltpu.CompilerParams(vmem_limit_bytes=int(limit * 2**20)),
        cost_estimate=pl.CostEstimate(flops=int(us * 1.15e9), bytes_accessed=int(us * 3.6e6), transcendentals=0),
        name=name,
    )(*args)


def copies(pairs, sems, first=0):
    started = planned(pairs, sems, first)
    for each in started:
        each.start()
    return started


def planned(pairs, sems, first=0):
    return [pltpu.make_async_copy(src, dst, sems.at[first + k]) for k, (src, dst) in enumerate(pairs)]


class Stream:
    def __init__(self, pairs, sems, depth, first=0):
        self.copies = planned(pairs, sems, first)
        self.depth, self.done = depth, 0
        for each in self.copies[:depth]:
            each.start()

    def take(self, count=1):
        for _ in range(count):
            self.copies[self.done].wait()
            if self.done + self.depth < len(self.copies):
                self.copies[self.done + self.depth].start()
            self.done += 1


def flat(ref3):
    return jnp.concatenate([ref3[:, q, :] for q in range(ref3.shape[1])], axis=0)


def unflat(dest_ref, values):
    ans, questions, _ = dest_ref.shape
    for q in range(questions):
        dest_ref[:, q, :] = values[q * ans : (q + 1) * ans]


def row_head(ans, width):
    row = lax.broadcasted_iota(jnp.int32, (GROUP * ans, width), 0)
    head = jnp.zeros_like(row)
    for k in range(1, GROUP):
        head = head + (row >= k * ans).astype(jnp.int32)
    return head


def own_columns(ans):
    col = lax.broadcasted_iota(jnp.int32, (GROUP * ans, WIDE), 1)
    return (col // HEAD) == row_head(ans, WIDE)


def own_lane(ans, group, first=0):
    col = lax.broadcasted_iota(jnp.int32, (GROUP * ans, LANES), 1)
    return col == row_head(ans, LANES) + (group * GROUP + first)


def fold(block, ans):
    half = block[: 2 * ans] + block[2 * ans :]
    return half[:ans] + half[ans:]


def spread(rows):
    twice = jnp.concatenate([rows, rows], axis=0)
    return jnp.concatenate([twice, twice], axis=0)


def block_diagonal(values_ref, dest_ref, questions, ans, groups):
    own = own_columns(ans)
    per = GROUP * ans
    for q in range(questions):
        rows = spread(values_ref[q * ans : (q + 1) * ans, :])
        for g in range(groups):
            part = jnp.where(own, rows[:, g * WIDE : (g + 1) * WIDE], 0.0)
            dest_ref[g, q * per : (q + 1) * per, :] = part.astype(LOW)


def group_rows(wide_ref, group, per):
    return jnp.concatenate([wide_ref[q, group * per : (group + 1) * per, :] for q in range(wide_ref.shape[0])], axis=0)


def project_heads(wide_ref, weight_ref, dest_ref, questions, ans, groups):
    own = own_columns(ans)
    per = GROUP * ans
    for g in range(groups):
        got = nn(group_rows(wide_ref, g, per), weight_ref[:, g * WIDE : (g + 1) * WIDE])
        for q in range(questions):
            part = jnp.where(own, got[q * per : (q + 1) * per], 0.0)
            dest_ref[q * ans : (q + 1) * ans, g * WIDE : (g + 1) * WIDE] = fold(part, ans)


def head_lanes(values, pair, rows):
    lane = lax.broadcasted_iota(jnp.int32, (rows, LANES), 1)
    return jnp.where(lane < HEAD, values[:, 2 * pair : 2 * pair + 1], values[:, 2 * pair + 1 : 2 * pair + 2])


def norm_of(values, gain):
    inv = lax.rsqrt(jnp.mean(values * values, axis=1, keepdims=True) + EPSILON)
    return inv, values * inv * gain


def norm_back(values, gain, upstream):
    inv = lax.rsqrt(jnp.mean(values * values, axis=1, keepdims=True) + EPSILON)
    unit = values * inv
    scaled = upstream * gain
    grad = inv * (scaled - unit * jnp.mean(scaled * unit, axis=1, keepdims=True))
    return grad, jnp.sum(upstream * unit, axis=0, keepdims=True)


def decoder_forward_kernel(
    ans, heads, core_ref, rel_hbm, x_hbm, bucket_hbm, gain_self_hbm, gain_cross_hbm, wq_hbm, wk_hbm, wv_hbm, wo_hbm,
    cq_hbm, ck_hbm, cv_hbm, ids_hbm, enc_hbm,
    keep_ref, give_ref, stat_ref,
    query_hbm, after_hbm, norm_one_hbm, norm_two_hbm, ctx_hbm, q_hbm, k_hbm, v_hbm, probs_hbm, a_hbm, c_hbm, p_hbm,
    rel_ref, x_ref, bucket_ref, gain_self_ref, gain_cross_ref, wq_ref, wk_ref, wv_ref, wo_ref, cq_ref, ck_ref, cv_ref,
    ids_ref, enc_ref,
    query_ref, after_ref, norm_one_ref, norm_two_ref, ctx_ref, q_ref, k_ref, v_ref, probs_ref, a_ref, c_ref, p_ref,
    bd_ref, full_scr, m_scr, l_scr, load_sems, store_sems,
):
    questions, _, features = enc_ref.shape
    rows = questions * ans
    groups = features // WIDE
    per = GROUP * ans
    first_loads = [
        (x_hbm, x_ref), (gain_self_hbm, gain_self_ref), (wq_hbm, wq_ref), (wk_hbm, wk_ref), (wv_hbm, wv_ref),
        (rel_hbm, rel_ref), (bucket_hbm, bucket_ref), (wo_hbm, wo_ref), (gain_cross_hbm, gain_cross_ref),
        (cq_hbm, cq_ref), (ck_hbm, ck_ref), (ids_hbm, ids_ref),
    ]
    enc_loads = [(enc_hbm.at[q], enc_ref.at[q]) for q in range(questions)]
    loads = Stream(first_loads + enc_loads + [(cv_hbm, cv_ref)], load_sems, FORWARD_DEPTH)
    stores = []

    def store(*pairs):
        stores.extend(copies(pairs, store_sems, len(stores)))

    loads.take(2)
    x = flat(x_ref)
    normed = norm_of(x, gain_self_ref[...])[1].astype(LOW)
    row = lax.broadcasted_iota(jnp.int32, (rows, rows), 0)
    col = lax.broadcasted_iota(jnp.int32, (rows, rows), 1)
    mask = jnp.where((col <= row) & (col >= (row // ans) * ans), 0.0, MASKED)
    first = lax.broadcasted_iota(jnp.int32, (rows, LANES), 1) < HEAD
    for weight, dest in zip((wq_ref, wk_ref, wv_ref), (q_ref, k_ref, v_ref)):
        loads.take()
        dest[...] = nn(normed, weight[...]).astype(LOW)
    store((q_ref, q_hbm), (k_ref, k_hbm), (v_ref, v_hbm))
    norm_one_ref[...] = normed
    store((norm_one_ref, norm_one_hbm))
    loads.take(2)
    bucket = jnp.concatenate([bucket_ref[...]] * questions, axis=1)
    for pair in range(heads // 2):
        at = slice(pair * LANES, (pair + 1) * LANES)
        query, key, value = q_ref[:, at], k_ref[:, at], v_ref[:, at]
        parts = []
        for half in range(2):
            head = 2 * pair + half
            bias = jnp.zeros(bucket.shape, F32)
            for b in range(rel_ref.shape[1]):
                bias = jnp.where(bucket == b, rel_ref[head, b], bias)
            twice = jnp.concatenate([bias, bias], axis=0)
            bias = jnp.concatenate([twice] * (questions // 2), axis=0)
            own = jnp.where(first if half == 0 else ~first, query.astype(F32), 0.0).astype(LOW)
            scores = nt(own, key) + bias + mask
            top = jnp.max(scores, axis=1, keepdims=True)
            probs = jnp.exp(scores - top)
            probs = probs / jnp.sum(probs, axis=1, keepdims=True)
            probs_ref[head] = probs
            parts.append(nn(probs.astype(LOW), value))
        ctx_ref[:, at] = jnp.where(first, parts[0], parts[1]).astype(LOW)
    store((probs_ref, probs_hbm))
    loads.take()
    after = x + nn(ctx_ref[...], wo_ref[...])
    after_ref[...] = after
    store((ctx_ref, ctx_hbm), (after_ref, after_hbm))
    loads.take()
    normed = norm_of(after, gain_cross_ref[...])[1].astype(LOW)
    loads.take()
    query_ref[...] = nn(normed, cq_ref[...]).astype(LOW).astype(F32)
    norm_two_ref[...] = normed
    store((norm_two_ref, norm_two_hbm), (query_ref, query_hbm))

    block_diagonal(query_ref, bd_ref, questions, ans, groups)
    loads.take()
    for g in range(groups):
        got = nt(bd_ref[g], ck_ref[:, g * WIDE : (g + 1) * WIDE]).astype(LOW)
        for q in range(questions):
            a_ref[q, g * per : (g + 1) * per, :] = got[q * per : (q + 1) * per]
    store((a_ref, a_hbm))
    loads.take()
    for q in range(questions):
        if q % FORWARD_BATCH == 0:
            loads.take(FORWARD_BATCH)
        tokens = enc_ref[q]
        scores = nt(a_ref[q], tokens) + jnp.where(ids_ref[q : q + 1, :] != 0, 0.0, MASKED)
        top = jnp.max(scores, axis=1, keepdims=True)
        probs = jnp.exp(scores - top)
        total = jnp.sum(probs, axis=1, keepdims=True)
        low = probs.astype(LOW)
        p_ref[q] = low
        c_ref[q] = nn(low, tokens).astype(LOW)
        if q % FORWARD_BATCH == FORWARD_BATCH - 1:
            span = pl.ds(q + 1 - FORWARD_BATCH, FORWARD_BATCH)
            store((p_ref.at[span], p_hbm.at[span]), (c_ref.at[span], c_hbm.at[span]))
        m_scr[q] = jnp.broadcast_to(top, m_scr.shape[1:])
        l_scr[q] = jnp.broadcast_to(total, l_scr.shape[1:])
    loads.take()
    project_heads(c_ref, cv_ref, full_scr, questions, ans, groups)
    for q in range(questions):
        stats = jnp.zeros((ans, LANES), F32)
        for src, lane in ((m_scr, 0), (l_scr, HEAD)):
            for g in range(groups):
                part = jnp.where(own_lane(ans, g, lane), src[q, g * per : (g + 1) * per, :], 0.0)
                stats = stats + fold(part, ans)
        stat_ref[q * ans : (q + 1) * ans, :] = stats
    full_scr[:, features:] = stat_ref[...]
    by_side(full_scr, (keep_ref, give_ref), core_ref)
    for each in stores:
        each.wait()


def decoder_forward(core, x, encoded, ids, buckets, rel_turned, gain_self, gain_cross, wq, wk, wv, wo, cq, ck, cv):
    ans, questions, features = x.shape
    tokens = encoded.shape[1]
    heads = rel_turned.shape[0]
    groups = features // WIDE
    rows, per = questions * ans, GROUP * ans
    low, full = ((rows, features), LOW), ((rows, features), F32)
    by_token = ((questions, groups * per, tokens), LOW)
    by_feature = ((questions, groups * per, features), LOW)
    hbm_outs = [full, full, low, low, low, low, low, low, ((heads, rows, rows), F32), by_feature, by_feature, by_token]
    packed = ((rows // 2, features + LANES), F32)
    outs = [packed, packed, ((rows, LANES), F32)]
    weights = [wq, wk, wv, wo, cq, ck, cv]
    inputs = [rel_turned, x, buckets, gain_self, gain_cross] + weights + [ids, encoded]
    return call(
        functools.partial(decoder_forward_kernel, ans, heads),
        outs + hbm_outs,
        "decoder_forward",
        [core] + inputs,
        scratch=[pltpu.SMEM(rel_turned.shape, F32)]
        + [pltpu.VMEM(each.shape, each.dtype) for each in inputs[1:]]
        + [pltpu.VMEM(shape, dtype) for shape, dtype in hbm_outs]
        + [
            pltpu.VMEM((groups, questions * per, WIDE), LOW),
            pltpu.VMEM((rows, features + LANES), F32),
            pltpu.VMEM((questions, groups * per, LANES), F32),
            pltpu.VMEM((questions, groups * per, LANES), F32),
            pltpu.SemaphoreType.DMA((13 + questions,)),
            pltpu.SemaphoreType.DMA((10 + 2 * questions,)),
        ],
        smem=(0,),
        hbm=tuple(range(1, 1 + len(inputs))),
        hbm_out=tuple(range(len(outs), len(outs) + len(hbm_outs))),
        us=19, limit=44,
    )


def by_side(dest, outs, side_ref):
    rows = outs[0].shape[0]
    side = side_ref[0]
    outs[0][...] = dest[pl.ds(pl.multiple_of(side * rows, rows), rows), :]
    outs[1][...] = dest[pl.ds(pl.multiple_of((1 - side) * rows, rows), rows), :]


def merge_kernel(heads, side_ref, mine_ref, other_ref, *refs):
    outs, out_ref = refs[:-1], refs[-1]
    rows = mine_ref.shape[0]
    features = heads * HEAD
    mine, other = mine_ref[:, features:], other_ref[:, features:]
    stat = lax.broadcasted_iota(jnp.int32, mine.shape, 1) < HEAD
    top_mine = jnp.where(stat, mine, pltpu.roll(mine, HEAD, 1))
    top_other = jnp.where(stat, other, pltpu.roll(other, HEAD, 1))
    top = jnp.maximum(top_mine, top_other)
    by_mine, by_other = jnp.exp(top_mine - top), jnp.exp(top_other - top)
    out_ref[:, features:] = jnp.where(stat, top, mine * by_mine + other * by_other)
    for pair in range(heads // 2):
        at = slice(pair * LANES, (pair + 1) * LANES)
        out_ref[:, at] = mine_ref[:, at] * head_lanes(by_mine, pair, rows) + other_ref[:, at] * head_lanes(
            by_other, pair, rows
        )
    if outs:
        by_side(out_ref, outs, side_ref)


def merge(side, mine, other, heads, halved=False):
    rows, width = mine.shape
    return call(
        functools.partial(merge_kernel, heads),
        [((rows // 2, width), F32)] * 2 if halved else [(mine.shape, F32)],
        "merge_partials",
        (side, mine, other),
        scratch=[pltpu.VMEM(mine.shape, F32)] if halved else [],
        smem=(0,),
        us=0.5, limit=4,
    )


def join_kernel(side_ref, mine_ref, other_ref, out_ref):
    rows = mine_ref.shape[0]
    side = side_ref[0]
    out_ref[pl.ds(pl.multiple_of(side * rows, rows), rows), :] = mine_ref[...]
    out_ref[pl.ds(pl.multiple_of((1 - side) * rows, rows), rows), :] = other_ref[...]


def join(side, mine, other):
    rows, width = mine.shape
    return call(join_kernel, [((2 * rows, width), F32)], "join_halves", (side, mine, other), smem=(0,), us=0.05, limit=4)[0]


def decoder_backward_kernel(
    ans, heads, blocks, core_ref, own_ref, other_ref, stat_ref, after_hbm, cot_hbm, gain_hbm, co_hbm,
    fin_hbm, fout_hbm, cv_hbm, ck_hbm, enc_hbm, p_hbm,
    keep_ref, give_ref, gctx_ref, w_ref, wide_ref,
    out_hbm, gain_grad_hbm, gac_hbm, ctx_hbm, norm_hbm, active_hbm, inner_hbm, gcross_hbm, gout_hbm, s_hbm, b_hbm,
    after_ref, cot_ref, gain_ref, co_ref, fin_ref, fout_ref, cv_ref, ck_ref, enc_ref, p_ref,
    out_ref, gain_grad_ref, gac_ref, ctx_ref, norm_ref, active_ref, inner_ref, gcross_ref, gout_ref, s_ref, b_ref,
    full_scr, delta_ref, bd_ref, back_scr, raw_scr, w_scr, d_scr, load_sems, store_sems,
):
    questions, _, features = enc_ref.shape
    rows, per = questions * ans, GROUP * ans
    groups = features // WIDE
    hidden = fin_ref.shape[1]
    width = hidden // blocks
    spans = [slice(c * width, (c + 1) * width) for c in range(blocks)]
    pairs = [(co_hbm, co_ref), (after_hbm, after_ref), (gain_hbm, gain_ref), (cot_hbm, cot_ref)]
    for at in spans:
        pairs += [(fin_hbm.at[:, at], fin_ref.at[:, at]), (fout_hbm.at[at, :], fout_ref.at[at, :])]
    pairs += [(cv_hbm, cv_ref)]
    for q in range(questions):
        pairs += [(enc_hbm.at[q], enc_ref.at[q]), (p_hbm.at[q], p_ref.at[q])]
    loads = Stream(pairs + [(ck_hbm, ck_ref)], load_sems, BACKWARD_DEPTH)
    stores = []

    def store(*pairs):
        stores.extend(copies(pairs, store_sems, len(stores)))

    core = core_ref[0]
    half = own_ref.shape[0]
    full_scr[pl.ds(pl.multiple_of(core * half, half), half), :] = own_ref[...]
    full_scr[pl.ds(pl.multiple_of((1 - core) * half, half), half), :] = other_ref[...]
    stats = full_scr[:, features:]
    lane = lax.broadcasted_iota(jnp.int32, stats.shape, 1)
    used = lane < heads
    inverse = jnp.where(used, 1.0 / jnp.where(used, pltpu.roll(stats, HEAD, 1), 1.0), 0.0)
    w_ref[...] = jnp.where(used, jnp.exp(jnp.where(used, stat_ref[...] - stats, 0.0)) * inverse, 0.0)
    for pair in range(heads // 2):
        at = slice(pair * LANES, (pair + 1) * LANES)
        ctx_ref[:, at] = full_scr[:, at] * head_lanes(inverse, pair, rows)
    store((ctx_ref, ctx_hbm))
    high, low = split(ctx_ref[...])
    loads.take(2)
    after = after_ref[...] + (nn(high, co_ref[...]) + nn(low, co_ref[...]))
    loads.take(2)
    gain = gain_ref[...]
    normed = norm_of(after, gain)[1].astype(LOW)
    norm_ref[...] = normed
    cot = flat(cot_ref)
    gout = cot.astype(LOW)
    gout_ref[...] = gout
    store((norm_ref, norm_hbm), (gout_ref, gout_hbm))
    total = jnp.zeros((rows, features), F32)
    back = jnp.zeros((rows, features), F32)
    for at in spans:
        loads.take()
        inner = nn(normed, fin_ref[:, at])
        square = inner * inner
        wave = jnp.tanh(GELU_A * inner * (1.0 + GELU_B * square))
        active = (0.5 * inner * (1.0 + wave)).astype(LOW)
        slope = 0.5 * (1.0 + wave) + 0.5 * inner * (1.0 - wave * wave) * (GELU_A * (1.0 + 3.0 * GELU_B * square))
        active_ref[:, at] = active
        loads.take()
        total = total + nn(active, fout_ref[at, :])
        grad_active = nt(gout, fout_ref[at, :]).astype(LOW).astype(F32)
        grad_inner = (grad_active * slope).astype(LOW)
        inner_ref[:, at] = grad_inner
        back = back + nt(grad_inner, fin_ref[:, at])
    unflat(out_ref, after + total)
    store((active_ref, active_hbm), (inner_ref, inner_hbm), (out_ref, out_hbm))
    grad, gain_grad = norm_back(after, gain, back)
    gain_grad_ref[...] = gain_grad
    gac = cot + grad
    gac_ref[...] = gac
    gcross = gac.astype(LOW)
    gcross_ref[...] = gcross
    gctx = nt(gcross, co_ref[...]).astype(LOW).astype(F32)
    gctx_ref[...] = gctx
    store((gac_ref, gac_hbm), (gcross_ref, gcross_hbm), (gain_grad_ref, gain_grad_hbm))
    select_row = lax.broadcasted_iota(jnp.int32, (features, LANES), 0) // HEAD
    select = jnp.where(select_row == lax.broadcasted_iota(jnp.int32, (features, LANES), 1), 1.0, 0.0).astype(LOW)
    high, low = split(gctx * ctx_ref[...])
    delta_ref[...] = nn(high, select) + nn(low, select)

    block_diagonal(gctx_ref, bd_ref, questions, ans, groups)
    for q in range(questions):
        for src, dst in ((w_ref, w_scr), (delta_ref, d_scr)):
            wide_rows = spread(src[q * ans : (q + 1) * ans, :])
            for g in range(groups):
                part = jnp.sum(jnp.where(own_lane(ans, g), wide_rows, 0.0), axis=1, keepdims=True)
                dst[q, g * per : (g + 1) * per, :] = jnp.broadcast_to(part, (per, LANES))
    loads.take()
    for g in range(groups):
        got = nt(bd_ref[g], cv_ref[:, g * WIDE : (g + 1) * WIDE])
        for q in range(questions):
            part = got[q * per : (q + 1) * per]
            raw_scr[q, g * per : (g + 1) * per, :] = part.astype(LOW)
            b_ref[q, g * per : (g + 1) * per, :] = (part * w_scr[q, g * per : (g + 1) * per, :1]).astype(LOW)
    store((b_ref, b_hbm))
    for q in range(questions):
        if q % BACKWARD_BATCH == 0:
            loads.take(2 * BACKWARD_BATCH)
        tokens = enc_ref[q]
        grad_probs = nt(raw_scr[q], tokens)
        probs = p_ref[q].astype(F32) * w_scr[q][:, :1]
        grad_scores = (probs * (grad_probs - d_scr[q][:, :1])).astype(LOW)
        s_ref[q] = grad_scores
        wide_ref[q] = nn(grad_scores, tokens).astype(LOW)
        if q % BACKWARD_BATCH == BACKWARD_BATCH - 1:
            span = pl.ds(q + 1 - BACKWARD_BATCH, BACKWARD_BATCH)
            store((s_ref.at[span], s_hbm.at[span]))
    loads.take()
    project_heads(wide_ref, ck_ref, back_scr, questions, ans, groups)
    by_side(back_scr, (keep_ref, give_ref), core_ref)
    for each in stores:
        each.wait()


def decoder_backward(core, own, other, stat, after, cot, gain, co, fin, fout, cv, ck, encoded, probs, heads):
    rows, features = after.shape
    ans, questions, _ = cot.shape
    tokens = encoded.shape[1]
    groups, per = features // WIDE, GROUP * ans
    hidden = fin.shape[1]
    blocks = 6
    low, full = ((rows, features), LOW), ((rows, features), F32)
    thin = ((rows, LANES), F32)
    wide = ((rows, hidden), LOW)
    half = ((rows // 2, features), F32)
    by_token = ((questions, groups * per, tokens), LOW)
    by_feature = ((questions, groups * per, features), LOW)
    outs = [half, half, full, thin, by_feature]
    hbm_outs = [(cot.shape, F32), ((1, features), F32), full, full, low, wide, wide, low, low, by_token, by_feature]
    inputs = [after, cot, gain, co, fin, fout, cv, ck, encoded, probs]
    return call(
        functools.partial(decoder_backward_kernel, ans, heads, blocks),
        outs + hbm_outs,
        "decoder_backward",
        [core, own, other, stat] + inputs,
        scratch=[pltpu.VMEM(each.shape, each.dtype) for each in inputs]
        + [pltpu.VMEM(shape, dtype) for shape, dtype in hbm_outs]
        + [
            pltpu.VMEM((rows, features + LANES), F32),
            pltpu.VMEM((rows, LANES), F32),
            pltpu.VMEM((groups, questions * per, WIDE), LOW),
            pltpu.VMEM((rows, features), F32),
            pltpu.VMEM(by_feature[0], LOW),
            pltpu.VMEM((questions, groups * per, LANES), F32),
            pltpu.VMEM((questions, groups * per, LANES), F32),
            pltpu.SemaphoreType.DMA((6 + 2 * blocks + 2 * questions,)),
            pltpu.SemaphoreType.DMA((10 + questions,)),
        ],
        smem=(0,),
        hbm=tuple(range(4, 4 + len(inputs))),
        hbm_out=tuple(range(len(outs), len(outs) + len(hbm_outs))),
        us=22.5, limit=54,
    )


def window(ref, index, share):
    start = index * share
    base = jnp.minimum((start // LANES) * LANES, ref.shape[1] - 2 * LANES)
    block = ref[:, pl.ds(pl.multiple_of(base, LANES), 2 * LANES)].astype(F32)
    return pltpu.roll(block, lax.rem(2 * LANES - (start - base), 2 * LANES), 1)[:, :share]


def weight_kernel(
    share, hidden_share, index_ref, active_hbm, inner_hbm, norm_hbm, gout_hbm, gcross_hbm, ctx_hbm, out_ref,
    active_ref, inner_ref, norm_ref, gout_ref, gcross_ref, ctx_ref, sems,
):
    loads = Stream(
        [(norm_hbm, norm_ref), (inner_hbm, inner_ref), (active_hbm, active_ref), (gout_hbm, gout_ref),
         (ctx_hbm, ctx_ref), (gcross_hbm, gcross_ref)],
        sems,
        3,
    )
    index = index_ref[0]
    features = gout_ref.shape[1]
    loads.take(2)
    normed = window(norm_ref, index, share).astype(LOW)
    at = 0
    for c in range(inner_ref.shape[1] // features):
        out_ref[at : at + share, :] = tn(normed, inner_ref[:, c * features : (c + 1) * features])
        at += share
    loads.take(2)
    out_ref[at : at + hidden_share, :] = tn(window(active_ref, index, hidden_share).astype(LOW), gout_ref[...])
    at += hidden_share
    loads.take(2)
    high, low = split(window(ctx_ref, index, share))
    out_ref[at : at + share, :] = tn(high, gcross_ref[...]) + tn(low, gcross_ref[...])


def weight_gradients(index, active, inner, norm, gout, gcross, ctx, share, hidden_share):
    features, hidden = gout.shape[1], inner.shape[1]
    inputs = [active, inner, norm, gout, gcross, ctx]
    rows = share * (hidden // features) + hidden_share + share
    return call(
        functools.partial(weight_kernel, share, hidden_share),
        [((rows, features), F32)],
        "weight_gradients",
        [index] + inputs,
        scratch=[pltpu.VMEM(each.shape, each.dtype) for each in inputs] + [pltpu.SemaphoreType.DMA((6,))],
        smem=(0,),
        hbm=tuple(range(1, 7)),
        us=3.3, limit=16,
    )[0]


def weight_sum_kernel(
    share, hidden_share, table_hbm, bucket_hbm, gains_hbm, ffn_hbm, mine_hbm, other_hbm,
    small_hbm, fin_hbm, fout_hbm, co_hbm,
    table_ref, bucket_ref, gains_ref, ffn_ref, mine_ref, other_ref, small_ref, fin_ref, fout_ref, co_ref, sems,
):
    loads = copies(
        [(table_hbm, table_ref), (bucket_hbm, bucket_ref), (gains_hbm, gains_ref), (ffn_hbm, ffn_ref),
         (mine_hbm, mine_ref), (other_hbm, other_ref)],
        sems,
    )
    for load in loads[:4]:
        load.wait()
    heads, ans, rows = table_ref.shape
    total = jnp.zeros((heads, LANES), F32)
    which = lax.broadcasted_iota(jnp.int32, (LANES, rows), 0)
    wide_bucket = jnp.concatenate([bucket_ref[...]] * (rows // ans), axis=1)
    for i in range(ans):
        hot = jnp.where(which == wide_bucket[i : i + 1, :], 1.0, 0.0).astype(LOW)
        high, low = split(table_ref[:, i, :])
        total = total + (nt(high, hot) + nt(low, hot))
    small_ref[...] = jnp.zeros(small_ref.shape, F32)
    small_ref[:8, :] = gains_ref[...]
    small_ref[2:3, :] = ffn_ref[...]
    small_ref[8 : 8 + heads, :LANES] = total
    for load in loads[4:]:
        load.wait()
    features = mine_ref.shape[1]
    at = 0
    for c in range(fin_ref.shape[1] // features):
        fin_ref[:, c * features : (c + 1) * features] = mine_ref[at : at + share, :] + other_ref[at : at + share, :]
        at += share
    fout_ref[...] = mine_ref[at : at + hidden_share, :] + other_ref[at : at + hidden_share, :]
    at += hidden_share
    co_ref[...] = mine_ref[at : at + share, :] + other_ref[at : at + share, :]
    pairs = [(small_ref, small_hbm), (fin_ref, fin_hbm), (fout_ref, fout_hbm), (co_ref, co_hbm)]
    for each in copies(pairs, sems, 6):
        each.wait()


def weight_sum(table, buckets, gains, gain_ffn_grad, mine, other, share, hidden_share, hidden):
    features = mine.shape[1]
    inputs = [table, buckets, gains, gain_ffn_grad, mine, other]
    outs = [
        ((8 + table.shape[0], features), F32), ((share, hidden), F32), ((hidden_share, features), F32),
        ((share, features), F32),
    ]
    return call(
        functools.partial(weight_sum_kernel, share, hidden_share),
        outs,
        "weight_sum",
        inputs,
        scratch=[pltpu.VMEM(each.shape, each.dtype) for each in inputs]
        + [pltpu.VMEM(shape, dtype) for shape, dtype in outs]
        + [pltpu.SemaphoreType.DMA((10,))],
        hbm=tuple(range(6)),
        hbm_out=(0, 1, 2, 3),
        us=0.1, limit=10,
    )


def last_sum_kernel(stacks, *refs):
    count = 2 * (stacks + 1)
    inputs, refs = refs[:count], refs[count:]
    sems = refs[-1]
    places = refs[len(refs) - 1 - count : -1]
    outs = refs[: (len(refs) - 1 - count) // 2]
    held = refs[len(outs) : 2 * len(outs)]
    for load in copies(list(zip(inputs, places)), sems):
        load.wait()
    at = 0
    for k in range(stacks):
        mine, other = places[2 * k], places[2 * k + 1]
        for row in range(mine.shape[0]):
            held[at][...] = mine[row] + other[row]
            at += 1
    total = places[-2][...] + places[-1][...]
    for k in range(3):
        held[at + k][...] = total[k]
    heads, buckets = held[at + 3].shape
    held[at + 3][...] = total[8 : 8 + heads, :buckets]
    for each in copies(list(zip(held, outs)), sems, count):
        each.wait()


def last_sum(pairs, bias_shape):
    inputs = [each for pair in pairs for each in pair]
    row = ((inputs[-1].shape[1],), F32)
    outs = [(mine.shape[1:], F32) for mine, _ in pairs[:-1] for _ in range(mine.shape[0])]
    outs += [row, row, row, (bias_shape, F32)]
    return call(
        functools.partial(last_sum_kernel, len(pairs) - 1),
        outs,
        "last_sum",
        inputs,
        scratch=[pltpu.VMEM(shape, dtype) for shape, dtype in outs]
        + [pltpu.VMEM(each.shape, each.dtype) for each in inputs]
        + [pltpu.SemaphoreType.DMA((len(outs) + len(inputs),))],
        hbm=tuple(range(len(inputs))),
        hbm_out=tuple(range(len(outs))),
        us=0.1, limit=16,
    )


def encoded_kernel(start, stop, has_base, s_hbm, p_hbm, a_hbm, b_hbm, *refs):
    out_ref, s_ref, p_ref, a_ref, b_ref, slots, in_sems, sems = refs[1:] if has_base else refs
    count = stop - start
    pairs = ((p_hbm, p_ref), (b_hbm, b_ref), (s_hbm, s_ref), (a_hbm, a_ref))
    loads = Stream([(src.at[start + k], dst.at[k]) for k in range(count) for src, dst in pairs], in_sems, 8)

    def copy(k, slot):
        return pltpu.make_async_copy(slots.at[slot], out_ref.at[start + k], sems.at[slot])

    for k in range(count):
        if k % 2 == 0:
            loads.take(8)
            if k >= 4:
                copy(k - 4, k % 4).wait()
                copy(k - 3, (k + 1) % 4).wait()
        slots[k % 4] = (tn(p_ref[k], b_ref[k]) + tn(s_ref[k], a_ref[k])).astype(LOW)
        if k % 2 == 1:
            copy(k - 1, (k - 1) % 4).start()
            copy(k, k % 4).start()
    for k in range(max(count - 4, 0), count):
        copy(k, k % 4).wait()


def encoded_gradient(grad_scores, probs, a, b, start, stop, base=None, us=5):
    questions, _, tokens = probs.shape
    features = a.shape[2]
    args = [grad_scores, probs, a, b] + ([] if base is None else [base])
    return call(
        functools.partial(encoded_kernel, start, stop, base is not None),
        [((questions, tokens, features), LOW)],
        "encoded_gradient",
        args,
        scratch=[pltpu.VMEM((stop - start,) + x.shape[1:], LOW) for x in (grad_scores, probs, a, b)]
        + [
            pltpu.VMEM((4, tokens, features), LOW),
            pltpu.SemaphoreType.DMA((4 * (stop - start),)),
            pltpu.SemaphoreType.DMA((4,)),
        ],
        hbm=tuple(range(len(args))),
        hbm_out=(0,),
        us=us, limit=26,
        aliases={} if base is None else {4: 0},
    )[0]


def split_owner(full_ref, outs, core_ref):
    count, share, _ = outs[0].shape
    core = core_ref[0]
    for k in range(count):
        for out, side in zip(outs, (core, 1 - core)):
            out[k] = full_ref[pl.ds(pl.multiple_of((2 * k + side) * share, share), share), :]


def key_value_kernel(ans, core_ref, wide_ref, gctx_ref, w_ref, c_hbm, query_hbm, *refs):
    outs, (c_ref, query_ref, blocks_ref, scaled_ref, full_ref, sems) = refs[:-8], refs[-8:-2]
    held, store_sems = refs[-2:]
    stores = []
    questions, per = wide_ref.shape[0], GROUP * ans
    groups = wide_ref.shape[2] // WIDE
    loads = Stream([(query_hbm, query_ref), (c_hbm, c_ref)], sems, 2)
    for pair in range(groups * GROUP // 2):
        at = slice(pair * LANES, (pair + 1) * LANES)
        scaled_ref[:, at] = gctx_ref[:, at] * head_lanes(w_ref[...], pair, gctx_ref.shape[0])
    loads.take()
    count = len(outs) // 2
    for turn, (left, values, dests) in enumerate(
        ((wide_ref, query_ref, outs[:count]), (c_ref, scaled_ref, outs[count:]))
    ):
        block_diagonal(values, blocks_ref, questions, ans, groups)
        if left is c_ref:
            loads.take()
        dest = full_ref if count == 2 else dests[0]
        for g in range(groups):
            dest[:, g * WIDE : (g + 1) * WIDE] = tn(group_rows(left, g, per), blocks_ref[g])
        if count == 2:
            split_owner(full_ref, (held.at[turn], dests[1]), core_ref)
            stores += copies([(held.at[turn], dests[0])], store_sems, turn)
    for each in stores:
        each.wait()


def key_value_gradients(core, wide, gctx, weight, ctx_wide, query, count, ans):
    questions, _, features = wide.shape
    groups, per = features // WIDE, GROUP * ans
    share = features // count
    split_rows = share % 8 == 0
    half = ((count // 2, share, features), F32)
    outs = call(
        functools.partial(key_value_kernel, ans),
        [half] * 4 if split_rows else [((features, features), F32)] * 2,
        "key_value_gradients",
        (core, wide, gctx, weight, ctx_wide, query),
        scratch=[
            pltpu.VMEM(ctx_wide.shape, LOW),
            pltpu.VMEM(query.shape, F32),
            pltpu.VMEM((groups, questions * per, WIDE), LOW),
            pltpu.VMEM(gctx.shape, F32),
            pltpu.VMEM((features, features), F32),
            pltpu.SemaphoreType.DMA((2,)),
            pltpu.VMEM((2,) + half[0], F32),
            pltpu.SemaphoreType.DMA((2,)),
        ],
        smem=(0,),
        hbm=(4, 5),
        hbm_out=(0, 2) if split_rows else (),
        us=4.3, limit=20,
    )
    if split_rows:
        return outs
    pairs = [each.reshape(count // 2, 2, share, features) for each in outs]
    return [
        lax.dynamic_index_in_dim(each, side, 1, keepdims=False) for each in pairs for side in (core[0], 1 - core[0])
    ]


def halve_kernel(place, side_ref, keep_ref, got_ref, *outs):
    count = keep_ref.shape[0]
    if count == 1:
        outs[0][...] = keep_ref[...] + got_ref[...]
        return
    side = side_ref[0]
    low = 1 << place
    for k in range(count // 2):
        base = (k // low) * 2 * low + k % low
        for out, bit in zip(outs, (side, 1 - side)):
            at = base + bit * low
            out[k] = keep_ref[at] + got_ref[at]


def halve(side, keep, got, place):
    count = keep.shape[0]
    half = ((max(count // 2, 1),) + keep.shape[1:], F32)
    return call(
        functools.partial(halve_kernel, place),
        [half] if count == 1 else [half, half],
        "halve_blocks",
        (side, keep, got),
        smem=(0,),
        us=0.05, limit=8,
    )


def final_kernel(key_keep_ref, key_got_ref, value_keep_ref, value_got_ref, out_ref):
    out_ref[0] = key_keep_ref[0] + key_got_ref[0]
    out_ref[1] = value_keep_ref[0] + value_got_ref[0]


def final_blocks(key_keep, key_got, value_keep, value_got):
    shape = ((2,) + key_keep.shape[1:], F32)
    return call(final_kernel, [shape], "final_blocks", (key_keep, key_got, value_keep, value_got), us=0.3, limit=4)[0]


def self_backward_kernel(
    ans, share, core_ref, index_ref, own_ref, other_ref, *refs,
):
    inputs = refs[:17]
    packed_hbm, table_hbm, gains_hbm, grad_in_hbm = refs[17:21]
    (
        cq_ref, after_ref, gain_cross_ref, gac_ref, wo_ref, norm_two_ref, ctx_ref, v_ref, k_ref, q_ref, probs_ref,
        norm_one_ref, wq_ref, wk_ref, wv_ref, x_ref, gain_self_ref,
    ) = places = refs[21:38]
    packed_ref, table_ref, gains_ref, grad_in_ref, gq_ref, gctx_ref, gqkv_ref, sems, store_sems = refs[38:]
    rows, features = gac_ref.shape
    heads = probs_ref.shape[0]
    loads = Stream(list(zip(inputs, places)), sems, len(inputs))
    half = own_ref.shape[0]
    core, index = core_ref[0], index_ref[0]
    gq_ref[pl.ds(pl.multiple_of(core * half, half), half), :] = own_ref[...]
    gq_ref[pl.ds(pl.multiple_of((1 - core) * half, half), half), :] = other_ref[...]
    high, low = split(gq_ref[...])
    loads.take()
    upstream = nt(high, cq_ref[...]) + nt(low, cq_ref[...])
    loads.take(6)
    grad, gain_cross_grad = norm_back(after_ref[...], gain_cross_ref[...], upstream)
    gas = gac_ref[...] + grad
    gself = gas.astype(LOW)
    gctx_ref[...] = nt(gself, wo_ref[...]).astype(LOW)
    normed = window(norm_two_ref, index, share).astype(LOW)
    packed_ref[0] = tn(normed, high) + tn(normed, low)
    packed_ref[1] = tn(window(ctx_ref, index, share).astype(LOW), gself)
    loads.take(5)
    first = lax.broadcasted_iota(jnp.int32, (rows, LANES), 1) < HEAD
    for pair in range(heads // 2):
        at = slice(pair * LANES, (pair + 1) * LANES)
        query, key, value, grad_ctx = q_ref[:, at], k_ref[:, at], v_ref[:, at], gctx_ref[:, at]
        gqs, gks, gvs = [], [], []
        for part in range(2):
            head = 2 * pair + part
            own = jnp.where(first if part == 0 else ~first, grad_ctx.astype(F32), 0.0).astype(LOW)
            grad_probs = nt(own, value)
            probs = probs_ref[head]
            grad_scores = probs * (grad_probs - jnp.sum(probs * grad_probs, axis=1, keepdims=True))
            blocks = [grad_scores[k * 2 * ans : (k + 1) * 2 * ans] for k in range(rows // (2 * ans))]
            both = functools.reduce(lambda a, b: a + b, blocks)
            table_ref[head] = both[:ans] + both[ans:]
            low_scores = grad_scores.astype(LOW)
            gqs.append(nn(low_scores, key))
            gks.append(tn(low_scores, query))
            gvs.append(tn(probs.astype(LOW), grad_ctx))
        for k, parts in enumerate((gqs, gks, gvs)):
            place = slice(k * features + pair * LANES, k * features + (pair + 1) * LANES)
            gqkv_ref[:, place] = jnp.where(first, parts[0], parts[1]).astype(LOW)
    normed = window(norm_one_ref, index, share).astype(LOW)
    for k in range(3):
        packed_ref[2 + k] = tn(normed, gqkv_ref[:, k * features : (k + 1) * features])
    stores = copies([(packed_ref, packed_hbm), (table_ref, table_hbm)], store_sems)
    loads.take(5)
    upstream = jnp.zeros((rows, features), F32)
    for k, weight in enumerate((wq_ref, wk_ref, wv_ref)):
        upstream = upstream + nt(gqkv_ref[:, k * features : (k + 1) * features], weight[...])
    grad, gain_self_grad = norm_back(flat(x_ref), gain_self_ref[...], upstream)
    gains_ref[...] = jnp.zeros(gains_ref.shape, F32)
    for k, row in enumerate((gain_self_grad, gain_cross_grad)):
        gains_ref[k : k + 1, :] = row
    unflat(grad_in_ref, gas + grad)
    for each in stores + copies([(gains_ref, gains_hbm), (grad_in_ref, grad_in_hbm)], store_sems, 2):
        each.wait()


def self_backward(core, index, own, other, inputs, ans, share):
    gac, probs, x = inputs[3], inputs[10], inputs[15]
    rows, features = gac.shape
    heads = probs.shape[0]
    outs = [((5, share, features), F32), ((heads, ans, rows), F32), ((8, features), F32), (x.shape, F32)]
    return call(
        functools.partial(self_backward_kernel, ans, share),
        outs,
        "self_backward",
        [core, index, own, other] + inputs,
        scratch=[pltpu.VMEM(each.shape, each.dtype) for each in inputs]
        + [pltpu.VMEM(shape, dtype) for shape, dtype in outs]
        + [
            pltpu.VMEM((rows, features), F32),
            pltpu.VMEM((rows, features), LOW),
            pltpu.VMEM((rows, 3 * features), LOW),
            pltpu.SemaphoreType.DMA((len(inputs),)),
            pltpu.SemaphoreType.DMA((4,)),
        ],
        smem=(0, 1),
        hbm=tuple(range(4, 4 + len(inputs))),
        hbm_out=(0, 1, 2, 3),
        us=SELF_US, limit=24,
    )


def partner(value, axis, bit):
    count = lax.axis_size(axis)
    return lax.ppermute(value, axis, [(k, k ^ bit) for k in range(count)])


def axis_bits(axis):
    bits, bit = [], 1
    while bit < lax.axis_size(axis):
        bits.append(bit)
        bit *= 2
    return bits


def add_kernel(side_ref, a_ref, b_ref, *refs):
    outs, out_ref = refs[:-1], refs[-1]
    out_ref[...] = a_ref[...] + b_ref[...]
    if outs:
        by_side(out_ref, outs, side_ref)


def add(side, a, b, halved=False):
    rows, width = a.shape
    return call(
        add_kernel,
        [((rows // 2, width), F32)] * 2 if halved else [(a.shape, F32)],
        "add_partials",
        (side, a, b),
        scratch=[pltpu.VMEM(a.shape, F32)] if halved else [],
        smem=(0,),
        us=0.05, limit=4,
    )


def exchange(keep, give, combine, sides):
    bits = axis_bits("blk")
    keep, give = combine(sides[1], keep, partner(give, "blk", bits[0]), True)
    (keep,) = combine(sides[1], keep, partner(give, "blk", bits[1]), False)
    for bit in bits[2:]:
        (keep,) = combine(sides[1], keep, partner(keep, "blk", bit), False)
    keep = join(sides[1], keep, partner(keep, "blk", bits[1]))
    return keep, partner(keep, "blk", bits[0])


def after(value, *others):
    return lax.optimization_barrier((value,) + others)[0]


def body(
    decoder_in, encoded, key_ids, buckets, gain_self, gain_cross, gain_ffn, rel_bias, self_q, self_k, self_v, self_o,
    cross_q, cross_k, cross_v, cross_o, ffn_in, ffn_out, cotangent,
):
    questions, ans, features = decoder_in.shape
    heads = rel_bias.shape[1]
    hidden = ffn_in.shape[1]
    blk_count = lax.axis_size("blk")
    blk_index = lax.axis_index("blk")
    index, core = blk_index.reshape(1), (blk_index % 2).reshape(1)
    share, hidden_share = features // blk_count, hidden // blk_count
    bits = axis_bits("blk")
    sides = [((blk_index // bit) % 2).reshape(1) for bit in bits[:2]]
    turned_in, turned_cot = jnp.transpose(decoder_in, (1, 0, 2)), jnp.transpose(cotangent, (1, 0, 2))
    (
        keep, give, stat, query, after_self, norm_one, norm_two, ctx_self, qs, ks, vs, probs_self, q_wide, ctx_wide,
        probs,
    ) = decoder_forward(
        core, turned_in, encoded, key_ids, buckets, rel_bias.T, gain_self, gain_cross, self_q, self_k, self_v, self_o,
        cross_q, cross_k, cross_v,
    )
    keep, other = exchange(keep, give, lambda s, a, b, halved: merge(s, a, b, heads, halved), sides)
    (
        keep, give, gctx, weight, query_wide, output, grad_gain_ffn, gac, context, norm_three, active, grad_inner,
        gcross, gout, grad_scores, g_wide,
    ) = decoder_backward(
        core, keep, other, stat, after_self, turned_cot, gain_ffn, cross_o, ffn_in, ffn_out, cross_v, cross_k, encoded,
        probs, heads,
    )

    def scatter_step(state, bit, *others, later=None):
        held, got, left = state
        place = sum(1 for b in left if b < bit)
        side = ((blk_index // bit) % 2).reshape(1)
        held, give = halve(side, held, after(got, *others), place)
        left = [b for b in left if b != bit]
        if later:
            return held, lambda value: partner(after(give, value), "blk", bit), left
        return held, partner(give, "blk", bit), left

    middle, end = questions // 4, questions - questions // 4
    inner = ((blk_index // bits[2]) % 2).reshape(1)
    keep, give = add(inner, keep, partner(give, "blk", bits[0]), True)
    got = partner(give, "blk", bits[2])
    key_keep, key_give, value_keep, value_give = key_value_gradients(
        core, query_wide, gctx, after(weight, keep), ctx_wide, query, blk_count, ans
    )
    (keep,) = add(inner, keep, after(got, value_give))
    key_state = (key_keep, partner(after(key_give, keep), "blk", bits[0]), list(bits[1:]))
    value_state = (value_keep, partner(after(value_give, keep), "blk", bits[0]), list(bits[1:]))
    got = partner(keep, "blk", bits[1])
    packed = weight_gradients(
        index, after(active, keep), grad_inner, norm_three, gout, gcross, context, share, hidden_share
    )
    packed_got = partner(packed, "pb", 1)
    key_state = scatter_step(key_state, bits[1], packed)
    held = key_state[0]
    for bit in bits[3:]:
        (keep,) = add(inner, keep, after(got, held))
        got = partner(keep, "blk", bit)
        held = keep
    grad_encoded = encoded_gradient(after(grad_scores, keep), probs, q_wide, g_wide, 0, middle)
    value_state = scatter_step(value_state, bits[1], grad_encoded, later=True)
    (keep,) = add(inner, keep, after(got, value_state[0]))
    value_state = (value_state[0], value_state[1](keep), value_state[2])
    got = partner(keep, "blk", bits[2])
    keep = join(inner, keep, got)
    other = partner(keep, "blk", bits[0])
    key_state = scatter_step(key_state, bits[2], keep)
    stack, table, gains, grad_in = self_backward(
        core, index, keep, after(other, key_state[0]),
        [
            cross_q, after_self, gain_cross, gac, self_o, norm_two, ctx_self, vs, ks, qs, probs_self, norm_one, self_q,
            self_k, self_v, turned_in, gain_self,
        ],
        ans, share,
    )
    stack_got = partner(stack, "pb", 1)
    value_state = scatter_step(value_state, bits[2], stack)
    last = value_state[0]
    for bit in bits[3:]:
        key_state = scatter_step(key_state, bit, last)
        last = key_state[0]
    grad_encoded = encoded_gradient(
        after(grad_scores, last), probs, q_wide, g_wide, middle, end, grad_encoded, us=LAST_US
    )
    last = grad_encoded
    for bit in bits[3:]:
        value_state = scatter_step(value_state, bit, last)
        last = value_state[0]
    small, grad_ffn_in, grad_ffn_out, grad_cross_o = weight_sum(
        after(table, last), buckets, gains, grad_gain_ffn, packed, packed_got, share, hidden_share, hidden
    )
    small_got = partner(small, "pb", 1)
    grad_encoded = encoded_gradient(
        after(grad_scores, small), probs, q_wide, g_wide, end, questions, grad_encoded, us=LAST_US
    )
    key_value = final_blocks(key_state[0], after(key_state[1], grad_encoded), value_state[0], value_state[1])
    key_value_got = partner(key_value, "pb", 1)
    (
        grad_cross_q, grad_self_o, grad_self_q, grad_self_k, grad_self_v, grad_cross_k, grad_cross_v, gain_self_sum,
        gain_cross_sum, gain_ffn_sum, bias_sum,
    ) = last_sum([(stack, stack_got), (key_value, key_value_got), (small, small_got)], rel_bias.shape[::-1])
    return (
        jnp.transpose(output, (1, 0, 2)),
        jnp.transpose(grad_in, (1, 0, 2)),
        grad_encoded,
        gain_self_sum,
        gain_cross_sum,
        gain_ffn_sum,
        bias_sum.T,
        grad_self_q,
        grad_self_k,
        grad_self_v,
        grad_self_o,
        grad_cross_q,
        grad_cross_k,
        grad_cross_v,
        grad_cross_o,
        grad_ffn_in,
        grad_ffn_out,
    )


def solution(mesh):
    rows, tokens, share = P("pb", None, None), P("pb", "blk", None), P("blk", None)
    return jax.shard_map(
        body,
        mesh=mesh,
        in_specs=(rows, tokens, P("pb", "blk")) + (P(),) * 15 + (rows,),
        out_specs=(rows, rows, tokens) + (P(),) * 4 + (share,) * 10,
        check_vma=False,
    )
```

```python
import functools

import jax
import jax.numpy as jnp
from jax import lax
from jax.experimental import pallas as pl
from jax.experimental.pallas import tpu as pltpu
from jax.sharding import PartitionSpec as P

EPSILON = 1e-06
MASKED = -1000000000.0
HIGHEST = lax.Precision.HIGHEST
HEAD = 64
GROUP = 4
WIDE = GROUP * HEAD
LANES = 128
LOW = jnp.bfloat16
F32 = jnp.float32
GELU_A = 0.7978845608028654
GELU_B = 0.044715
FORWARD_DEPTH = 8
BACKWARD_DEPTH = 16
FORWARD_BATCH = 4
BACKWARD_BATCH = 8
WIDE_BATCH = 4
SELF_US = 0.1
LAST_US = 0.1


def nn(a, b):
    return jnp.dot(a, b, preferred_element_type=F32)


def nt(a, b):
    return lax.dot_general(a, b, (((1,), (1,)), ((), ())), preferred_element_type=F32)


def tn(a, b):
    return lax.dot_general(a, b, (((0,), (0,)), ((), ())), preferred_element_type=F32)


def split(values):
    high = values.astype(LOW)
    return high, (values - high.astype(F32)).astype(LOW)


def call(kernel, outs, name, args, scratch=(), smem=(), hbm=(), hbm_out=(), limit=24, aliases=None, us=1.0):
    spaces = [pltpu.SMEM if k in smem else pltpu.HBM if k in hbm else pltpu.VMEM for k in range(len(args))]
    out_spaces = [pltpu.HBM if k in hbm_out else pltpu.VMEM for k in range(len(outs))]
    args = [
        each if space == pltpu.SMEM else pltpu.with_memory_space_constraint(each, space)
        for each, space in zip(args, spaces)
    ]
    return pl.pallas_call(
        kernel,
        in_specs=[pl.BlockSpec(memory_space=space) for space in spaces],
        out_specs=[pl.BlockSpec(memory_space=space) for space in out_spaces],
        out_shape=[space(shape, dtype) for space, (shape, dtype) in zip(out_spaces, outs)],
        scratch_shapes=list(scratch),
        input_output_aliases=aliases or {},
        compiler_params=pltpu.CompilerParams(vmem_limit_bytes=int(limit * 2**20)),
        cost_estimate=pl.CostEstimate(flops=int(us * 1.15e9), bytes_accessed=int(us * 3.6e6), transcendentals=0),
        name=name,
    )(*args)


def copies(pairs, sems, first=0):
    started = planned(pairs, sems, first)
    for each in started:
        each.start()
    return started


def planned(pairs, sems, first=0):
    return [pltpu.make_async_copy(src, dst, sems.at[first + k]) for k, (src, dst) in enumerate(pairs)]


class Stream:
    def __init__(self, pairs, sems, depth, first=0):
        self.copies = planned(pairs, sems, first)
        self.depth, self.done = depth, 0
        for each in self.copies[:depth]:
            each.start()

    def take(self, count=1):
        for _ in range(count):
            self.copies[self.done].wait()
            if self.done + self.depth < len(self.copies):
                self.copies[self.done + self.depth].start()
            self.done += 1


def flat(ref3):
    return jnp.concatenate([ref3[:, q, :] for q in range(ref3.shape[1])], axis=0)


def unflat(dest_ref, values):
    ans, questions, _ = dest_ref.shape
    for q in range(questions):
        dest_ref[:, q, :] = values[q * ans : (q + 1) * ans]


def row_head(ans, width):
    row = lax.broadcasted_iota(jnp.int32, (GROUP * ans, width), 0)
    head = jnp.zeros_like(row)
    for k in range(1, GROUP):
        head = head + (row >= k * ans).astype(jnp.int32)
    return head


def own_columns(ans):
    col = lax.broadcasted_iota(jnp.int32, (GROUP * ans, WIDE), 1)
    return (col // HEAD) == row_head(ans, WIDE)


def own_lane(ans, group, first=0):
    col = lax.broadcasted_iota(jnp.int32, (GROUP * ans, LANES), 1)
    return col == row_head(ans, LANES) + (group * GROUP + first)


def fold(block, ans):
    half = block[: 2 * ans] + block[2 * ans :]
    return half[:ans] + half[ans:]


def spread(rows):
    twice = jnp.concatenate([rows, rows], axis=0)
    return jnp.concatenate([twice, twice], axis=0)


def block_diagonal(values_ref, dest_ref, questions, ans, groups):
    own = own_columns(ans)
    per = GROUP * ans
    for q in range(questions):
        rows = spread(values_ref[q * ans : (q + 1) * ans, :])
        for g in range(groups):
            part = jnp.where(own, rows[:, g * WIDE : (g + 1) * WIDE], 0.0)
            dest_ref[g, q * per : (q + 1) * per, :] = part.astype(LOW)


def group_rows(wide_ref, group, per):
    return jnp.concatenate([wide_ref[q, group * per : (group + 1) * per, :] for q in range(wide_ref.shape[0])], axis=0)


def project_heads(wide_ref, weight_ref, dest_ref, questions, ans, groups):
    own = own_columns(ans)
    per = GROUP * ans
    for g in range(groups):
        got = nn(group_rows(wide_ref, g, per), weight_ref[:, g * WIDE : (g + 1) * WIDE])
        for q in range(questions):
            part = jnp.where(own, got[q * per : (q + 1) * per], 0.0)
            dest_ref[q * ans : (q + 1) * ans, g * WIDE : (g + 1) * WIDE] = fold(part, ans)


def head_lanes(values, pair, rows):
    lane = lax.broadcasted_iota(jnp.int32, (rows, LANES), 1)
    return jnp.where(lane < HEAD, values[:, 2 * pair : 2 * pair + 1], values[:, 2 * pair + 1 : 2 * pair + 2])


def norm_of(values, gain):
    inv = lax.rsqrt(jnp.mean(values * values, axis=1, keepdims=True) + EPSILON)
    return inv, values * inv * gain


def norm_back(values, gain, upstream):
    inv = lax.rsqrt(jnp.mean(values * values, axis=1, keepdims=True) + EPSILON)
    unit = values * inv
    scaled = upstream * gain
    grad = inv * (scaled - unit * jnp.mean(scaled * unit, axis=1, keepdims=True))
    return grad, jnp.sum(upstream * unit, axis=0, keepdims=True)


def decoder_forward_kernel(
    ans, heads, core_ref, rel_hbm, x_hbm, bucket_hbm, gain_self_hbm, gain_cross_hbm, wq_hbm, wk_hbm, wv_hbm, wo_hbm,
    cq_hbm, ck_hbm, cv_hbm, ids_hbm, enc_hbm,
    keep_ref, give_ref, stat_ref,
    query_hbm, after_hbm, norm_one_hbm, norm_two_hbm, ctx_hbm, q_hbm, k_hbm, v_hbm, probs_hbm, a_hbm, c_hbm, p_hbm,
    rel_ref, x_ref, bucket_ref, gain_self_ref, gain_cross_ref, wq_ref, wk_ref, wv_ref, wo_ref, cq_ref, ck_ref, cv_ref,
    ids_ref, enc_ref,
    query_ref, after_ref, norm_one_ref, norm_two_ref, ctx_ref, q_ref, k_ref, v_ref, probs_ref, a_ref, c_ref, p_ref,
    bd_ref, full_scr, m_scr, l_scr, load_sems, store_sems,
):
    questions, _, features = enc_ref.shape
    rows = questions * ans
    groups = features // WIDE
    per = GROUP * ans
    first_loads = [
        (x_hbm, x_ref), (gain_self_hbm, gain_self_ref), (wq_hbm, wq_ref), (wk_hbm, wk_ref), (wv_hbm, wv_ref),
        (rel_hbm, rel_ref), (bucket_hbm, bucket_ref), (wo_hbm, wo_ref), (gain_cross_hbm, gain_cross_ref),
        (cq_hbm, cq_ref), (ck_hbm, ck_ref), (ids_hbm, ids_ref),
    ]
    enc_loads = [(enc_hbm.at[q], enc_ref.at[q]) for q in range(questions)]
    loads = Stream(first_loads + enc_loads + [(cv_hbm, cv_ref)], load_sems, FORWARD_DEPTH)
    stores = []

    def store(*pairs):
        stores.extend(copies(pairs, store_sems, len(stores)))

    loads.take(2)
    x = flat(x_ref)
    normed = norm_of(x, gain_self_ref[...])[1].astype(LOW)
    row = lax.broadcasted_iota(jnp.int32, (rows, rows), 0)
    col = lax.broadcasted_iota(jnp.int32, (rows, rows), 1)
    mask = jnp.where((col <= row) & (col >= (row // ans) * ans), 0.0, MASKED)
    first = lax.broadcasted_iota(jnp.int32, (rows, LANES), 1) < HEAD
    for weight, dest in zip((wq_ref, wk_ref, wv_ref), (q_ref, k_ref, v_ref)):
        loads.take()
        dest[...] = nn(normed, weight[...]).astype(LOW)
    store((q_ref, q_hbm), (k_ref, k_hbm), (v_ref, v_hbm))
    norm_one_ref[...] = normed
    store((norm_one_ref, norm_one_hbm))
    loads.take(2)
    bucket = jnp.concatenate([bucket_ref[...]] * questions, axis=1)
    for pair in range(heads // 2):
        at = slice(pair * LANES, (pair + 1) * LANES)
        query, key, value = q_ref[:, at], k_ref[:, at], v_ref[:, at]
        parts = []
        for half in range(2):
            head = 2 * pair + half
            bias = jnp.zeros(bucket.shape, F32)
            for b in range(rel_ref.shape[1]):
                bias = jnp.where(bucket == b, rel_ref[head, b], bias)
            twice = jnp.concatenate([bias, bias], axis=0)
            bias = jnp.concatenate([twice] * (questions // 2), axis=0)
            own = jnp.where(first if half == 0 else ~first, query.astype(F32), 0.0).astype(LOW)
            scores = nt(own, key) + bias + mask
            top = jnp.max(scores, axis=1, keepdims=True)
            probs = jnp.exp(scores - top)
            probs = probs / jnp.sum(probs, axis=1, keepdims=True)
            probs_ref[head] = probs
            parts.append(nn(probs.astype(LOW), value))
        ctx_ref[:, at] = jnp.where(first, parts[0], parts[1]).astype(LOW)
    store((probs_ref, probs_hbm))
    loads.take()
    after = x + nn(ctx_ref[...], wo_ref[...])
    after_ref[...] = after
    store((ctx_ref, ctx_hbm), (after_ref, after_hbm))
    loads.take()
    normed = norm_of(after, gain_cross_ref[...])[1].astype(LOW)
    loads.take()
    query_ref[...] = nn(normed, cq_ref[...]).astype(LOW).astype(F32)
    norm_two_ref[...] = normed
    store((norm_two_ref, norm_two_hbm), (query_ref, query_hbm))

    block_diagonal(query_ref, bd_ref, questions, ans, groups)
    loads.take()
    for g in range(groups):
        got = nt(bd_ref[g], ck_ref[:, g * WIDE : (g + 1) * WIDE]).astype(LOW)
        for q in range(questions):
            a_ref[q, g * per : (g + 1) * per, :] = got[q * per : (q + 1) * per]
    store((a_ref, a_hbm))
    loads.take()
    for q in range(questions):
        if q % FORWARD_BATCH == 0:
            loads.take(FORWARD_BATCH)
        tokens = enc_ref[q]
        scores = nt(a_ref[q], tokens) + jnp.where(ids_ref[q : q + 1, :] != 0, 0.0, MASKED)
        top = jnp.max(scores, axis=1, keepdims=True)
        probs = jnp.exp(scores - top)
        total = jnp.sum(probs, axis=1, keepdims=True)
        low = probs.astype(LOW)
        p_ref[q] = low
        c_ref[q] = nn(low, tokens).astype(LOW)
        if q % FORWARD_BATCH == FORWARD_BATCH - 1:
            span = pl.ds(q + 1 - FORWARD_BATCH, FORWARD_BATCH)
            store((p_ref.at[span], p_hbm.at[span]), (c_ref.at[span], c_hbm.at[span]))
        m_scr[q] = jnp.broadcast_to(top, m_scr.shape[1:])
        l_scr[q] = jnp.broadcast_to(total, l_scr.shape[1:])
    loads.take()
    project_heads(c_ref, cv_ref, full_scr, questions, ans, groups)
    for q in range(questions):
        stats = jnp.zeros((ans, LANES), F32)
        for src, lane in ((m_scr, 0), (l_scr, HEAD)):
            for g in range(groups):
                part = jnp.where(own_lane(ans, g, lane), src[q, g * per : (g + 1) * per, :], 0.0)
                stats = stats + fold(part, ans)
        stat_ref[q * ans : (q + 1) * ans, :] = stats
    full_scr[:, features:] = stat_ref[...]
    by_side(full_scr, (keep_ref, give_ref), core_ref)
    for each in stores:
        each.wait()


def decoder_forward(core, x, encoded, ids, buckets, rel_turned, gain_self, gain_cross, wq, wk, wv, wo, cq, ck, cv):
    ans, questions, features = x.shape
    tokens = encoded.shape[1]
    heads = rel_turned.shape[0]
    groups = features // WIDE
    rows, per = questions * ans, GROUP * ans
    low, full = ((rows, features), LOW), ((rows, features), F32)
    by_token = ((questions, groups * per, tokens), LOW)
    by_feature = ((questions, groups * per, features), LOW)
    hbm_outs = [full, full, low, low, low, low, low, low, ((heads, rows, rows), F32), by_feature, by_feature, by_token]
    packed = ((rows // 2, features + LANES), F32)
    outs = [packed, packed, ((rows, LANES), F32)]
    weights = [wq, wk, wv, wo, cq, ck, cv]
    inputs = [rel_turned, x, buckets, gain_self, gain_cross] + weights + [ids, encoded]
    return call(
        functools.partial(decoder_forward_kernel, ans, heads),
        outs + hbm_outs,
        "decoder_forward",
        [core] + inputs,
        scratch=[pltpu.SMEM(rel_turned.shape, F32)]
        + [pltpu.VMEM(each.shape, each.dtype) for each in inputs[1:]]
        + [pltpu.VMEM(shape, dtype) for shape, dtype in hbm_outs]
        + [
            pltpu.VMEM((groups, questions * per, WIDE), LOW),
            pltpu.VMEM((rows, features + LANES), F32),
            pltpu.VMEM((questions, groups * per, LANES), F32),
            pltpu.VMEM((questions, groups * per, LANES), F32),
            pltpu.SemaphoreType.DMA((13 + questions,)),
            pltpu.SemaphoreType.DMA((10 + 2 * questions,)),
        ],
        smem=(0,),
        hbm=tuple(range(1, 1 + len(inputs))),
        hbm_out=tuple(range(len(outs), len(outs) + len(hbm_outs))),
        us=19, limit=44,
    )


def by_side(dest, outs, side_ref):
    rows = outs[0].shape[0]
    side = side_ref[0]
    outs[0][...] = dest[pl.ds(pl.multiple_of(side * rows, rows), rows), :]
    outs[1][...] = dest[pl.ds(pl.multiple_of((1 - side) * rows, rows), rows), :]


def merge_kernel(heads, side_ref, mine_ref, other_ref, *refs):
    outs, out_ref = refs[:-1], refs[-1]
    rows = mine_ref.shape[0]
    features = heads * HEAD
    mine, other = mine_ref[:, features:], other_ref[:, features:]
    stat = lax.broadcasted_iota(jnp.int32, mine.shape, 1) < HEAD
    top_mine = jnp.where(stat, mine, pltpu.roll(mine, HEAD, 1))
    top_other = jnp.where(stat, other, pltpu.roll(other, HEAD, 1))
    top = jnp.maximum(top_mine, top_other)
    by_mine, by_other = jnp.exp(top_mine - top), jnp.exp(top_other - top)
    out_ref[:, features:] = jnp.where(stat, top, mine * by_mine + other * by_other)
    for pair in range(heads // 2):
        at = slice(pair * LANES, (pair + 1) * LANES)
        out_ref[:, at] = mine_ref[:, at] * head_lanes(by_mine, pair, rows) + other_ref[:, at] * head_lanes(
            by_other, pair, rows
        )
    if outs:
        by_side(out_ref, outs, side_ref)


def merge(side, mine, other, heads, halved=False):
    rows, width = mine.shape
    return call(
        functools.partial(merge_kernel, heads),
        [((rows // 2, width), F32)] * 2 if halved else [(mine.shape, F32)],
        "merge_partials",
        (side, mine, other),
        scratch=[pltpu.VMEM(mine.shape, F32)] if halved else [],
        smem=(0,),
        us=0.5, limit=4,
    )


def join_kernel(side_ref, mine_ref, other_ref, out_ref):
    rows = mine_ref.shape[0]
    side = side_ref[0]
    out_ref[pl.ds(pl.multiple_of(side * rows, rows), rows), :] = mine_ref[...]
    out_ref[pl.ds(pl.multiple_of((1 - side) * rows, rows), rows), :] = other_ref[...]


def join(side, mine, other):
    rows, width = mine.shape
    return call(join_kernel, [((2 * rows, width), F32)], "join_halves", (side, mine, other), smem=(0,), us=0.05, limit=4)[0]


def decoder_backward_kernel(
    ans, heads, blocks, core_ref, own_ref, other_ref, stat_ref, after_hbm, cot_hbm, gain_hbm, co_hbm,
    fin_hbm, fout_hbm, cv_hbm, ck_hbm, enc_hbm, p_hbm,
    keep_ref, give_ref, gctx_ref, w_ref,
    out_hbm, gain_grad_hbm, gac_hbm, ctx_hbm, norm_hbm, active_hbm, inner_hbm, gcross_hbm, gout_hbm, s_hbm, b_hbm, wide_hbm,
    after_ref, cot_ref, gain_ref, co_ref, fin_ref, fout_ref, cv_ref, ck_ref, enc_ref, p_ref,
    out_ref, gain_grad_ref, gac_ref, ctx_ref, norm_ref, active_ref, inner_ref, gcross_ref, gout_ref, s_ref, b_ref, wide_ref,
    full_scr, delta_ref, bd_ref, back_scr, raw_scr, w_scr, d_scr, load_sems, store_sems,
):
    questions, _, features = enc_ref.shape
    rows, per = questions * ans, GROUP * ans
    groups = features // WIDE
    hidden = fin_ref.shape[1]
    width = hidden // blocks
    spans = [slice(c * width, (c + 1) * width) for c in range(blocks)]
    pairs = [(co_hbm, co_ref), (after_hbm, after_ref), (gain_hbm, gain_ref), (cot_hbm, cot_ref)]
    for at in spans:
        pairs += [(fin_hbm.at[:, at], fin_ref.at[:, at]), (fout_hbm.at[at, :], fout_ref.at[at, :])]
    pairs += [(cv_hbm, cv_ref)]
    for q in range(questions):
        pairs += [(enc_hbm.at[q], enc_ref.at[q]), (p_hbm.at[q], p_ref.at[q])]
    loads = Stream(pairs + [(ck_hbm, ck_ref)], load_sems, BACKWARD_DEPTH)
    stores = []

    def store(*pairs):
        stores.extend(copies(pairs, store_sems, len(stores)))

    core = core_ref[0]
    half = own_ref.shape[0]
    full_scr[pl.ds(pl.multiple_of(core * half, half), half), :] = own_ref[...]
    full_scr[pl.ds(pl.multiple_of((1 - core) * half, half), half), :] = other_ref[...]
    stats = full_scr[:, features:]
    lane = lax.broadcasted_iota(jnp.int32, stats.shape, 1)
    used = lane < heads
    inverse = jnp.where(used, 1.0 / jnp.where(used, pltpu.roll(stats, HEAD, 1), 1.0), 0.0)
    w_ref[...] = jnp.where(used, jnp.exp(jnp.where(used, stat_ref[...] - stats, 0.0)) * inverse, 0.0)
    for pair in range(heads // 2):
        at = slice(pair * LANES, (pair + 1) * LANES)
        ctx_ref[:, at] = full_scr[:, at] * head_lanes(inverse, pair, rows)
    store((ctx_ref, ctx_hbm))
    high, low = split(ctx_ref[...])
    loads.take(2)
    after = after_ref[...] + (nn(high, co_ref[...]) + nn(low, co_ref[...]))
    loads.take(2)
    gain = gain_ref[...]
    normed = norm_of(after, gain)[1].astype(LOW)
    norm_ref[...] = normed
    cot = flat(cot_ref)
    gout = cot.astype(LOW)
    gout_ref[...] = gout
    store((norm_ref, norm_hbm), (gout_ref, gout_hbm))
    total = jnp.zeros((rows, features), F32)
    back = jnp.zeros((rows, features), F32)
    for at in spans:
        loads.take()
        inner = nn(normed, fin_ref[:, at])
        square = inner * inner
        wave = jnp.tanh(GELU_A * inner * (1.0 + GELU_B * square))
        active = (0.5 * inner * (1.0 + wave)).astype(LOW)
        slope = 0.5 * (1.0 + wave) + 0.5 * inner * (1.0 - wave * wave) * (GELU_A * (1.0 + 3.0 * GELU_B * square))
        active_ref[:, at] = active
        loads.take()
        total = total + nn(active, fout_ref[at, :])
        grad_active = nt(gout, fout_ref[at, :]).astype(LOW).astype(F32)
        grad_inner = (grad_active * slope).astype(LOW)
        inner_ref[:, at] = grad_inner
        back = back + nt(grad_inner, fin_ref[:, at])
    unflat(out_ref, after + total)
    store((active_ref, active_hbm), (inner_ref, inner_hbm), (out_ref, out_hbm))
    grad, gain_grad = norm_back(after, gain, back)
    gain_grad_ref[...] = gain_grad
    gac = cot + grad
    gac_ref[...] = gac
    gcross = gac.astype(LOW)
    gcross_ref[...] = gcross
    gctx = nt(gcross, co_ref[...]).astype(LOW).astype(F32)
    gctx_ref[...] = gctx
    store((gac_ref, gac_hbm), (gcross_ref, gcross_hbm), (gain_grad_ref, gain_grad_hbm))
    select_row = lax.broadcasted_iota(jnp.int32, (features, LANES), 0) // HEAD
    select = jnp.where(select_row == lax.broadcasted_iota(jnp.int32, (features, LANES), 1), 1.0, 0.0).astype(LOW)
    high, low = split(gctx * ctx_ref[...])
    delta_ref[...] = nn(high, select) + nn(low, select)

    block_diagonal(gctx_ref, bd_ref, questions, ans, groups)
    for q in range(questions):
        for src, dst in ((w_ref, w_scr), (delta_ref, d_scr)):
            wide_rows = spread(src[q * ans : (q + 1) * ans, :])
            for g in range(groups):
                part = jnp.sum(jnp.where(own_lane(ans, g), wide_rows, 0.0), axis=1, keepdims=True)
                dst[q, g * per : (g + 1) * per, :] = jnp.broadcast_to(part, (per, LANES))
    loads.take()
    for g in range(groups):
        got = nt(bd_ref[g], cv_ref[:, g * WIDE : (g + 1) * WIDE])
        for q in range(questions):
            part = got[q * per : (q + 1) * per]
            raw_scr[q, g * per : (g + 1) * per, :] = part.astype(LOW)
            b_ref[q, g * per : (g + 1) * per, :] = (part * w_scr[q, g * per : (g + 1) * per, :1]).astype(LOW)
    store((b_ref, b_hbm))
    for q in range(questions):
        if q % BACKWARD_BATCH == 0:
            loads.take(2 * BACKWARD_BATCH)
        tokens = enc_ref[q]
        grad_probs = nt(raw_scr[q], tokens)
        probs = p_ref[q].astype(F32) * w_scr[q][:, :1]
        grad_scores = (probs * (grad_probs - d_scr[q][:, :1])).astype(LOW)
        s_ref[q] = grad_scores
        wide_ref[q] = nn(grad_scores, tokens).astype(LOW)
        if q % BACKWARD_BATCH == BACKWARD_BATCH - 1:
            span = pl.ds(q + 1 - BACKWARD_BATCH, BACKWARD_BATCH)
            store((s_ref.at[span], s_hbm.at[span]))
        if q % WIDE_BATCH == WIDE_BATCH - 1:
            span = pl.ds(q + 1 - WIDE_BATCH, WIDE_BATCH)
            store((wide_ref.at[span], wide_hbm.at[span]))
    loads.take()
    project_heads(wide_ref, ck_ref, back_scr, questions, ans, groups)
    by_side(back_scr, (keep_ref, give_ref), core_ref)
    for each in stores:
        each.wait()


def decoder_backward(core, own, other, stat, after, cot, gain, co, fin, fout, cv, ck, encoded, probs, heads):
    rows, features = after.shape
    ans, questions, _ = cot.shape
    tokens = encoded.shape[1]
    groups, per = features // WIDE, GROUP * ans
    hidden = fin.shape[1]
    blocks = 6
    low, full = ((rows, features), LOW), ((rows, features), F32)
    thin = ((rows, LANES), F32)
    wide = ((rows, hidden), LOW)
    half = ((rows // 2, features), F32)
    by_token = ((questions, groups * per, tokens), LOW)
    by_feature = ((questions, groups * per, features), LOW)
    outs = [half, half, full, thin]
    hbm_outs = [(cot.shape, F32), ((1, features), F32), full, full, low, wide, wide, low, low, by_token, by_feature, by_feature]
    inputs = [after, cot, gain, co, fin, fout, cv, ck, encoded, probs]
    return call(
        functools.partial(decoder_backward_kernel, ans, heads, blocks),
        outs + hbm_outs,
        "decoder_backward",
        [core, own, other, stat] + inputs,
        scratch=[pltpu.VMEM(each.shape, each.dtype) for each in inputs]
        + [pltpu.VMEM(shape, dtype) for shape, dtype in hbm_outs]
        + [
            pltpu.VMEM((rows, features + LANES), F32),
            pltpu.VMEM((rows, LANES), F32),
            pltpu.VMEM((groups, questions * per, WIDE), LOW),
            pltpu.VMEM((rows, features), F32),
            pltpu.VMEM(by_feature[0], LOW),
            pltpu.VMEM((questions, groups * per, LANES), F32),
            pltpu.VMEM((questions, groups * per, LANES), F32),
            pltpu.SemaphoreType.DMA((6 + 2 * blocks + 2 * questions,)),
            pltpu.SemaphoreType.DMA((10 + 2 * questions,)),
        ],
        smem=(0,),
        hbm=tuple(range(4, 4 + len(inputs))),
        hbm_out=tuple(range(len(outs), len(outs) + len(hbm_outs))),
        us=22.5, limit=54,
    )


def window(ref, index, share):
    start = index * share
    base = jnp.minimum((start // LANES) * LANES, ref.shape[1] - 2 * LANES)
    block = ref[:, pl.ds(pl.multiple_of(base, LANES), 2 * LANES)].astype(F32)
    return pltpu.roll(block, lax.rem(2 * LANES - (start - base), 2 * LANES), 1)[:, :share]


def weight_kernel(
    share, hidden_share, index_ref, active_hbm, inner_hbm, norm_hbm, gout_hbm, gcross_hbm, ctx_hbm, out_ref,
    active_ref, inner_ref, norm_ref, gout_ref, gcross_ref, ctx_ref, sems,
):
    loads = Stream(
        [(norm_hbm, norm_ref), (inner_hbm, inner_ref), (active_hbm, active_ref), (gout_hbm, gout_ref),
         (ctx_hbm, ctx_ref), (gcross_hbm, gcross_ref)],
        sems,
        3,
    )
    index = index_ref[0]
    features = gout_ref.shape[1]
    loads.take(2)
    normed = window(norm_ref, index, share).astype(LOW)
    at = 0
    for c in range(inner_ref.shape[1] // features):
        out_ref[at : at + share, :] = tn(normed, inner_ref[:, c * features : (c + 1) * features])
        at += share
    loads.take(2)
    out_ref[at : at + hidden_share, :] = tn(window(active_ref, index, hidden_share).astype(LOW), gout_ref[...])
    at += hidden_share
    loads.take(2)
    high, low = split(window(ctx_ref, index, share))
    out_ref[at : at + share, :] = tn(high, gcross_ref[...]) + tn(low, gcross_ref[...])


def weight_gradients(index, active, inner, norm, gout, gcross, ctx, share, hidden_share):
    features, hidden = gout.shape[1], inner.shape[1]
    inputs = [active, inner, norm, gout, gcross, ctx]
    rows = share * (hidden // features) + hidden_share + share
    return call(
        functools.partial(weight_kernel, share, hidden_share),
        [((rows, features), F32)],
        "weight_gradients",
        [index] + inputs,
        scratch=[pltpu.VMEM(each.shape, each.dtype) for each in inputs] + [pltpu.SemaphoreType.DMA((6,))],
        smem=(0,),
        hbm=tuple(range(1, 7)),
        us=3.3, limit=16,
    )[0]


def weight_sum_kernel(
    share, hidden_share, table_hbm, bucket_hbm, self_hbm, cross_hbm, ffn_hbm, mine_hbm, other_hbm,
    small_hbm, fin_hbm, fout_hbm, co_hbm,
    table_ref, bucket_ref, self_ref, cross_ref, ffn_ref, mine_ref, other_ref, small_ref, fin_ref, fout_ref, co_ref, sems,
):
    loads = copies(
        [(table_hbm, table_ref), (bucket_hbm, bucket_ref), (self_hbm, self_ref), (cross_hbm, cross_ref),
         (ffn_hbm, ffn_ref), (mine_hbm, mine_ref), (other_hbm, other_ref)],
        sems,
    )
    for load in loads[:5]:
        load.wait()
    heads, ans, rows = table_ref.shape
    total = jnp.zeros((heads, LANES), F32)
    which = lax.broadcasted_iota(jnp.int32, (LANES, rows), 0)
    wide_bucket = jnp.concatenate([bucket_ref[...]] * (rows // ans), axis=1)
    for i in range(ans):
        hot = jnp.where(which == wide_bucket[i : i + 1, :], 1.0, 0.0).astype(LOW)
        high, low = split(table_ref[:, i, :])
        total = total + (nt(high, hot) + nt(low, hot))
    small_ref[...] = jnp.zeros(small_ref.shape, F32)
    for k, row in enumerate((self_ref, cross_ref, ffn_ref)):
        small_ref[k : k + 1, :] = row[...]
    small_ref[8 : 8 + heads, :LANES] = total
    for load in loads[5:]:
        load.wait()
    features = mine_ref.shape[1]
    at = 0
    for c in range(fin_ref.shape[1] // features):
        fin_ref[:, c * features : (c + 1) * features] = mine_ref[at : at + share, :] + other_ref[at : at + share, :]
        at += share
    fout_ref[...] = mine_ref[at : at + hidden_share, :] + other_ref[at : at + hidden_share, :]
    at += hidden_share
    co_ref[...] = mine_ref[at : at + share, :] + other_ref[at : at + share, :]
    pairs = [(small_ref, small_hbm), (fin_ref, fin_hbm), (fout_ref, fout_hbm), (co_ref, co_hbm)]
    for each in copies(pairs, sems, 7):
        each.wait()


def weight_sum(table, buckets, gain_grads, mine, other, share, hidden_share, hidden):
    features = mine.shape[1]
    inputs = [table, buckets] + gain_grads + [mine, other]
    outs = [
        ((8 + table.shape[0], features), F32), ((share, hidden), F32), ((hidden_share, features), F32),
        ((share, features), F32),
    ]
    return call(
        functools.partial(weight_sum_kernel, share, hidden_share),
        outs,
        "weight_sum",
        inputs,
        scratch=[pltpu.VMEM(each.shape, each.dtype) for each in inputs]
        + [pltpu.VMEM(shape, dtype) for shape, dtype in outs]
        + [pltpu.SemaphoreType.DMA((11,))],
        hbm=tuple(range(7)),
        hbm_out=(0, 1, 2, 3),
        us=0.1, limit=10,
    )


def last_sum_kernel(mine_ref, other_ref, *refs):
    inputs, refs = refs[:4], refs[4:]
    sems, places = refs[-1], refs[-5:-1]
    refs = refs[:-5]
    outs, held = refs[: len(refs) // 2], refs[len(refs) // 2 :]
    loads = copies(list(zip(inputs, places)), sems)
    stores = []
    at = 0
    for k in range(mine_ref.shape[0]):
        held[at][...] = mine_ref[k] + other_ref[k]
        stores += copies([(held[at], outs[at])], sems, 4 + at)
        at += 1
    for load in loads:
        load.wait()
    for k in range(places[0].shape[0]):
        held[at][...] = places[0][k] + places[1][k]
        at += 1
    total = places[2][...] + places[3][...]
    for k in range(3):
        held[at + k][...] = total[k]
    heads, buckets = held[at + 3].shape
    held[at + 3][...] = total[8 : 8 + heads, :buckets]
    first = len(stores)
    for each in stores + copies(list(zip(held[first:], outs[first:])), sems, 4 + first):
        each.wait()


def last_sum(fresh, stack, small, bias_shape):
    row = ((small[0].shape[1],), F32)
    outs = [(mine.shape[1:], F32) for mine, _ in (fresh, stack) for _ in range(mine.shape[0])]
    outs += [row, row, row, (bias_shape, F32)]
    inputs = list(stack) + list(small)
    return call(
        last_sum_kernel,
        outs,
        "last_sum",
        list(fresh) + inputs,
        scratch=[pltpu.VMEM(shape, dtype) for shape, dtype in outs]
        + [pltpu.VMEM(each.shape, each.dtype) for each in inputs]
        + [pltpu.SemaphoreType.DMA((4 + len(outs),))],
        hbm=(2, 3, 4, 5),
        hbm_out=tuple(range(len(outs))),
        us=0.1, limit=16,
    )


def encoded_kernel(start, stop, has_base, s_hbm, p_hbm, a_hbm, b_hbm, *refs):
    out_ref, s_ref, p_ref, a_ref, b_ref, slots, in_sems, sems = refs[1:] if has_base else refs
    count = stop - start
    pairs = ((p_hbm, p_ref), (b_hbm, b_ref), (s_hbm, s_ref), (a_hbm, a_ref))
    loads = Stream([(src.at[start + k], dst.at[k]) for k in range(count) for src, dst in pairs], in_sems, 8)

    def copy(k, slot):
        return pltpu.make_async_copy(slots.at[slot], out_ref.at[start + k], sems.at[slot])

    for k in range(count):
        if k % 2 == 0:
            loads.take(8)
            if k >= 4:
                copy(k - 4, k % 4).wait()
                copy(k - 3, (k + 1) % 4).wait()
        slots[k % 4] = (tn(p_ref[k], b_ref[k]) + tn(s_ref[k], a_ref[k])).astype(LOW)
        if k % 2 == 1:
            copy(k - 1, (k - 1) % 4).start()
            copy(k, k % 4).start()
    for k in range(max(count - 4, 0), count):
        copy(k, k % 4).wait()


def encoded_gradient(grad_scores, probs, a, b, start, stop, base=None, us=5):
    questions, _, tokens = probs.shape
    features = a.shape[2]
    args = [grad_scores, probs, a, b] + ([] if base is None else [base])
    return call(
        functools.partial(encoded_kernel, start, stop, base is not None),
        [((questions, tokens, features), LOW)],
        "encoded_gradient",
        args,
        scratch=[pltpu.VMEM((stop - start,) + x.shape[1:], LOW) for x in (grad_scores, probs, a, b)]
        + [
            pltpu.VMEM((4, tokens, features), LOW),
            pltpu.SemaphoreType.DMA((4 * (stop - start),)),
            pltpu.SemaphoreType.DMA((4,)),
        ],
        hbm=tuple(range(len(args))),
        hbm_out=(0,),
        us=us, limit=26,
        aliases={} if base is None else {4: 0},
    )[0]


def split_owner(full_ref, outs, core_ref):
    count, share, _ = outs[0].shape
    core = core_ref[0]
    for k in range(count):
        for out, side in zip(outs, (core, 1 - core)):
            out[k] = full_ref[pl.ds(pl.multiple_of((2 * k + side) * share, share), share), :]


def key_value_kernel(ans, core_ref, gctx_ref, w_ref, wide_hbm, c_hbm, query_hbm, *refs):
    outs, (wide_ref, c_ref, query_ref, blocks_ref, scaled_ref, full_ref, sems) = refs[:-9], refs[-9:-2]
    held, store_sems = refs[-2:]
    stores = []
    questions, per = wide_ref.shape[0], GROUP * ans
    groups = wide_ref.shape[2] // WIDE
    loads = Stream([(query_hbm, query_ref), (wide_hbm, wide_ref), (c_hbm, c_ref)], sems, 3)
    for pair in range(groups * GROUP // 2):
        at = slice(pair * LANES, (pair + 1) * LANES)
        scaled_ref[:, at] = gctx_ref[:, at] * head_lanes(w_ref[...], pair, gctx_ref.shape[0])
    loads.take()
    count = len(outs) // 2
    for turn, (left, values, dests) in enumerate(
        ((wide_ref, query_ref, outs[:count]), (c_ref, scaled_ref, outs[count:]))
    ):
        block_diagonal(values, blocks_ref, questions, ans, groups)
        loads.take()
        dest = full_ref if count == 2 else dests[0]
        for g in range(groups):
            dest[:, g * WIDE : (g + 1) * WIDE] = tn(group_rows(left, g, per), blocks_ref[g])
        if count == 2:
            split_owner(full_ref, (held.at[turn], dests[1]), core_ref)
            stores += copies([(held.at[turn], dests[0])], store_sems, turn)
    for each in stores:
        each.wait()


def key_value_gradients(core, wide, gctx, weight, ctx_wide, query, count, ans):
    questions, _, features = wide.shape
    groups, per = features // WIDE, GROUP * ans
    share = features // count
    split_rows = share % 8 == 0
    half = ((count // 2, share, features), F32)
    outs = call(
        functools.partial(key_value_kernel, ans),
        [half] * 4 if split_rows else [((features, features), F32)] * 2,
        "key_value_gradients",
        (core, gctx, weight, wide, ctx_wide, query),
        scratch=[
            pltpu.VMEM(wide.shape, LOW),
            pltpu.VMEM(ctx_wide.shape, LOW),
            pltpu.VMEM(query.shape, F32),
            pltpu.VMEM((groups, questions * per, WIDE), LOW),
            pltpu.VMEM(gctx.shape, F32),
            pltpu.VMEM((features, features), F32),
            pltpu.SemaphoreType.DMA((3,)),
            pltpu.VMEM((2,) + half[0], F32),
            pltpu.SemaphoreType.DMA((2,)),
        ],
        smem=(0,),
        hbm=(3, 4, 5),
        hbm_out=(0, 2) if split_rows else (),
        us=4.3, limit=22,
    )
    if split_rows:
        return outs
    pairs = [each.reshape(count // 2, 2, share, features) for each in outs]
    return [
        lax.dynamic_index_in_dim(each, side, 1, keepdims=False) for each in pairs for side in (core[0], 1 - core[0])
    ]


def halve_kernel(place, side_ref, keep_ref, got_ref, *outs):
    count = keep_ref.shape[0]
    if count == 1:
        outs[0][...] = keep_ref[...] + got_ref[...]
        return
    side = side_ref[0]
    low = 1 << place
    for k in range(count // 2):
        base = (k // low) * 2 * low + k % low
        for out, bit in zip(outs, (side, 1 - side)):
            at = base + bit * low
            out[k] = keep_ref[at] + got_ref[at]


def halve(side, keep, got, place):
    count = keep.shape[0]
    half = ((max(count // 2, 1),) + keep.shape[1:], F32)
    return call(
        functools.partial(halve_kernel, place),
        [half] if count == 1 else [half, half],
        "halve_blocks",
        (side, keep, got),
        smem=(0,),
        us=0.05, limit=8,
    )


def final_kernel(key_keep_ref, key_got_ref, value_keep_ref, value_got_ref, out_ref):
    out_ref[0] = key_keep_ref[0] + key_got_ref[0]
    out_ref[1] = value_keep_ref[0] + value_got_ref[0]


def final_blocks(key_keep, key_got, value_keep, value_got):
    shape = ((2,) + key_keep.shape[1:], F32)
    return call(final_kernel, [shape], "final_blocks", (key_keep, key_got, value_keep, value_got), us=0.3, limit=4)[0]


def self_backward_kernel(
    ans, share, core_ref, index_ref, own_ref, other_ref, *refs,
):
    inputs = refs[:12]
    packed_hbm, table_hbm, gain_hbm, gas_hbm, gqkv_hbm = refs[12:17]
    (
        cq_ref, after_ref, gain_cross_ref, gac_ref, wo_ref, norm_two_ref, ctx_ref, v_ref, k_ref, q_ref, probs_ref,
        norm_one_ref,
    ) = places = refs[17:29]
    packed_ref, table_ref, gain_grad_ref, gas_ref, gqkv_ref, gq_ref, gctx_ref, sems, store_sems = refs[29:]
    rows, features = gac_ref.shape
    heads = probs_ref.shape[0]
    loads = Stream(list(zip(inputs, places)), sems, len(inputs))
    half = own_ref.shape[0]
    core, index = core_ref[0], index_ref[0]
    gq_ref[pl.ds(pl.multiple_of(core * half, half), half), :] = own_ref[...]
    gq_ref[pl.ds(pl.multiple_of((1 - core) * half, half), half), :] = other_ref[...]
    high, low = split(gq_ref[...])
    loads.take()
    upstream = nt(high, cq_ref[...]) + nt(low, cq_ref[...])
    loads.take(6)
    grad, gain_cross_grad = norm_back(after_ref[...], gain_cross_ref[...], upstream)
    gas = gac_ref[...] + grad
    gas_ref[...] = gas
    gain_grad_ref[...] = gain_cross_grad
    gself = gas.astype(LOW)
    gctx_ref[...] = nt(gself, wo_ref[...]).astype(LOW)
    normed = window(norm_two_ref, index, share).astype(LOW)
    packed_ref[0] = tn(normed, high) + tn(normed, low)
    packed_ref[1] = tn(window(ctx_ref, index, share).astype(LOW), gself)
    loads.take(5)
    first = lax.broadcasted_iota(jnp.int32, (rows, LANES), 1) < HEAD
    for pair in range(heads // 2):
        at = slice(pair * LANES, (pair + 1) * LANES)
        query, key, value, grad_ctx = q_ref[:, at], k_ref[:, at], v_ref[:, at], gctx_ref[:, at]
        gqs, gks, gvs = [], [], []
        for part in range(2):
            head = 2 * pair + part
            own = jnp.where(first if part == 0 else ~first, grad_ctx.astype(F32), 0.0).astype(LOW)
            grad_probs = nt(own, value)
            probs = probs_ref[head]
            grad_scores = probs * (grad_probs - jnp.sum(probs * grad_probs, axis=1, keepdims=True))
            blocks = [grad_scores[k * 2 * ans : (k + 1) * 2 * ans] for k in range(rows // (2 * ans))]
            both = functools.reduce(lambda a, b: a + b, blocks)
            table_ref[head] = both[:ans] + both[ans:]
            low_scores = grad_scores.astype(LOW)
            gqs.append(nn(low_scores, key))
            gks.append(tn(low_scores, query))
            gvs.append(tn(probs.astype(LOW), grad_ctx))
        for k, parts in enumerate((gqs, gks, gvs)):
            place = slice(k * features + pair * LANES, k * features + (pair + 1) * LANES)
            gqkv_ref[:, place] = jnp.where(first, parts[0], parts[1]).astype(LOW)
    normed = window(norm_one_ref, index, share).astype(LOW)
    for k in range(3):
        packed_ref[2 + k] = tn(normed, gqkv_ref[:, k * features : (k + 1) * features])
    pairs = [
        (packed_ref, packed_hbm), (table_ref, table_hbm), (gain_grad_ref, gain_hbm), (gas_ref, gas_hbm),
        (gqkv_ref, gqkv_hbm),
    ]
    for each in copies(pairs, store_sems):
        each.wait()

def input_back_kernel(
    gqkv_hbm, wq_hbm, wk_hbm, wv_hbm, x_hbm, gain_hbm, gas_hbm, grad_in_hbm, gain_grad_hbm,
    gqkv_ref, wq_ref, wk_ref, wv_ref, x_ref, gain_ref, gas_ref, grad_in_ref, gain_grad_ref, sems, store_sems,
):
    loads = Stream(
        [(gqkv_hbm, gqkv_ref), (wq_hbm, wq_ref), (wk_hbm, wk_ref), (wv_hbm, wv_ref), (x_hbm, x_ref),
         (gain_hbm, gain_ref), (gas_hbm, gas_ref)],
        sems,
        7,
    )
    rows, features = gas_ref.shape
    loads.take(4)
    upstream = jnp.zeros((rows, features), F32)
    for k, weight in enumerate((wq_ref, wk_ref, wv_ref)):
        upstream = upstream + nt(gqkv_ref[:, k * features : (k + 1) * features], weight[...])
    loads.take(3)
    grad, gain_grad = norm_back(flat(x_ref), gain_ref[...], upstream)
    gain_grad_ref[...] = gain_grad
    unflat(grad_in_ref, gas_ref[...] + grad)
    for each in copies([(grad_in_ref, grad_in_hbm), (gain_grad_ref, gain_grad_hbm)], store_sems):
        each.wait()


def input_back(gqkv, wq, wk, wv, x, gain, gas):
    inputs = [gqkv, wq, wk, wv, x, gain, gas]
    outs = [(x.shape, F32), ((1, x.shape[2]), F32)]
    return call(
        input_back_kernel,
        outs,
        "input_back",
        inputs,
        scratch=[pltpu.VMEM(each.shape, each.dtype) for each in inputs]
        + [pltpu.VMEM(shape, dtype) for shape, dtype in outs]
        + [pltpu.SemaphoreType.DMA((7,)), pltpu.SemaphoreType.DMA((2,))],
        hbm=tuple(range(7)),
        hbm_out=(0, 1),
        us=0.1, limit=16,
    )


def self_backward(core, index, own, other, inputs, ans, share):
    gac, probs = inputs[3], inputs[10]
    rows, features = gac.shape
    heads = probs.shape[0]
    outs = [
        ((5, share, features), F32), ((heads, ans, rows), F32), ((1, features), F32), ((rows, features), F32),
        ((rows, 3 * features), LOW),
    ]
    return call(
        functools.partial(self_backward_kernel, ans, share),
        outs,
        "self_backward",
        [core, index, own, other] + inputs,
        scratch=[pltpu.VMEM(each.shape, each.dtype) for each in inputs]
        + [pltpu.VMEM(shape, dtype) for shape, dtype in outs]
        + [
            pltpu.VMEM((rows, features), F32),
            pltpu.VMEM((rows, features), LOW),
            pltpu.SemaphoreType.DMA((len(inputs),)),
            pltpu.SemaphoreType.DMA((5,)),
        ],
        smem=(0, 1),
        hbm=tuple(range(4, 4 + len(inputs))),
        hbm_out=(0, 1, 2, 3, 4),
        us=SELF_US, limit=24,
    )


def partner(value, axis, bit):
    count = lax.axis_size(axis)
    return lax.ppermute(value, axis, [(k, k ^ bit) for k in range(count)])


def axis_bits(axis):
    bits, bit = [], 1
    while bit < lax.axis_size(axis):
        bits.append(bit)
        bit *= 2
    return bits


def add_kernel(side_ref, a_ref, b_ref, *refs):
    outs, out_ref = refs[:-1], refs[-1]
    out_ref[...] = a_ref[...] + b_ref[...]
    if outs:
        by_side(out_ref, outs, side_ref)


def add(side, a, b, halved=False):
    rows, width = a.shape
    return call(
        add_kernel,
        [((rows // 2, width), F32)] * 2 if halved else [(a.shape, F32)],
        "add_partials",
        (side, a, b),
        scratch=[pltpu.VMEM(a.shape, F32)] if halved else [],
        smem=(0,),
        us=0.05, limit=4,
    )


def exchange(keep, give, combine, sides):
    bits = axis_bits("blk")
    keep, give = combine(sides[1], keep, partner(give, "blk", bits[0]), True)
    (keep,) = combine(sides[1], keep, partner(give, "blk", bits[1]), False)
    for bit in bits[2:]:
        (keep,) = combine(sides[1], keep, partner(keep, "blk", bit), False)
    keep = join(sides[1], keep, partner(keep, "blk", bits[1]))
    return keep, partner(keep, "blk", bits[0])


def after(value, *others):
    return lax.optimization_barrier((value,) + others)[0]


def body(
    decoder_in, encoded, key_ids, buckets, gain_self, gain_cross, gain_ffn, rel_bias, self_q, self_k, self_v, self_o,
    cross_q, cross_k, cross_v, cross_o, ffn_in, ffn_out, cotangent,
):
    questions, ans, features = decoder_in.shape
    heads = rel_bias.shape[1]
    hidden = ffn_in.shape[1]
    blk_count = lax.axis_size("blk")
    blk_index = lax.axis_index("blk")
    index, core = blk_index.reshape(1), (blk_index % 2).reshape(1)
    share, hidden_share = features // blk_count, hidden // blk_count
    bits = axis_bits("blk")
    sides = [((blk_index // bit) % 2).reshape(1) for bit in bits[:2]]
    turned_in, turned_cot = jnp.transpose(decoder_in, (1, 0, 2)), jnp.transpose(cotangent, (1, 0, 2))
    (
        keep, give, stat, query, after_self, norm_one, norm_two, ctx_self, qs, ks, vs, probs_self, q_wide, ctx_wide,
        probs,
    ) = decoder_forward(
        core, turned_in, encoded, key_ids, buckets, rel_bias.T, gain_self, gain_cross, self_q, self_k, self_v, self_o,
        cross_q, cross_k, cross_v,
    )
    keep, other = exchange(keep, give, lambda s, a, b, halved: merge(s, a, b, heads, halved), sides)
    (
        keep, give, gctx, weight, output, grad_gain_ffn, gac, context, norm_three, active, grad_inner, gcross, gout,
        grad_scores, g_wide, query_wide,
    ) = decoder_backward(
        core, keep, other, stat, after_self, turned_cot, gain_ffn, cross_o, ffn_in, ffn_out, cross_v, cross_k, encoded,
        probs, heads,
    )

    def scatter_step(state, bit, *others, later=None):
        held, got, left = state
        place = sum(1 for b in left if b < bit)
        side = ((blk_index // bit) % 2).reshape(1)
        held, give = halve(side, held, after(got, *others), place)
        left = [b for b in left if b != bit]
        if later:
            return held, lambda value: partner(after(give, value), "blk", bit), left
        return held, partner(give, "blk", bit), left

    middle, end = questions // 2, questions - questions // 4
    inner = ((blk_index // bits[2]) % 2).reshape(1)
    keep, give = add(inner, keep, partner(give, "blk", bits[0]), True)
    got = partner(give, "blk", bits[2])
    key_keep, key_give, value_keep, value_give = key_value_gradients(
        core, query_wide, gctx, after(weight, keep), ctx_wide, query, blk_count, ans
    )
    (keep,) = add(inner, keep, after(got, value_give))
    key_state = (key_keep, partner(after(key_give, keep), "blk", bits[0]), list(bits[1:]))
    value_state = (value_keep, partner(after(value_give, keep), "blk", bits[0]), list(bits[1:]))
    got = partner(keep, "blk", bits[1])
    packed = weight_gradients(
        index, after(active, keep), grad_inner, norm_three, gout, gcross, context, share, hidden_share
    )
    packed_got = partner(packed, "pb", 1)
    key_state = scatter_step(key_state, bits[1], packed)
    held = key_state[0]
    for bit in bits[3:]:
        (keep,) = add(inner, keep, after(got, held))
        got = partner(keep, "blk", bit)
        held = keep
    grad_encoded = encoded_gradient(after(grad_scores, keep), probs, q_wide, g_wide, 0, middle)
    value_state = scatter_step(value_state, bits[1], grad_encoded, later=True)
    (keep,) = add(inner, keep, after(got, value_state[0]))
    value_state = (value_state[0], value_state[1](keep), value_state[2])
    got = partner(keep, "blk", bits[2])
    keep = join(inner, keep, got)
    other = partner(keep, "blk", bits[0])
    key_state = scatter_step(key_state, bits[2], keep)
    stack, table, grad_gain_cross, gas, grad_qkv = self_backward(
        core, index, keep, after(other, key_state[0]),
        [
            cross_q, after_self, gain_cross, gac, self_o, norm_two, ctx_self, vs, ks, qs, probs_self, norm_one,
        ],
        ans, share,
    )
    stack_got = partner(stack, "pb", 1)
    value_state = scatter_step(value_state, bits[2], stack)
    last = value_state[0]
    for bit in bits[3:]:
        key_state = scatter_step(key_state, bit, last)
        last = key_state[0]
    grad_in, grad_gain_self = input_back(
        after(grad_qkv, last), self_q, self_k, self_v, turned_in, gain_self, gas
    )
    last = grad_gain_self
    for bit in bits[3:]:
        value_state = scatter_step(value_state, bit, last)
        last = value_state[0]
    grad_encoded = encoded_gradient(
        after(grad_scores, last), probs, q_wide, g_wide, middle, end, grad_encoded, us=LAST_US
    )
    small, grad_ffn_in, grad_ffn_out, grad_cross_o = weight_sum(
        after(table, grad_encoded), buckets, [grad_gain_self, grad_gain_cross, grad_gain_ffn], packed, packed_got, share,
        hidden_share, hidden,
    )
    small_got = partner(small, "pb", 1)
    key_value = final_blocks(key_state[0], after(key_state[1], small), value_state[0], value_state[1])
    key_value_got = partner(key_value, "pb", 1)
    grad_encoded = encoded_gradient(
        after(grad_scores, key_value), probs, q_wide, g_wide, end, questions, grad_encoded, us=5.0
    )
    (
        grad_cross_k, grad_cross_v, grad_cross_q, grad_self_o, grad_self_q, grad_self_k, grad_self_v, gain_self_sum,
        gain_cross_sum, gain_ffn_sum, bias_sum,
    ) = last_sum((after(key_value, grad_encoded), key_value_got), (stack, stack_got), (small, small_got), rel_bias.shape[::-1])
    return (
        jnp.transpose(output, (1, 0, 2)),
        jnp.transpose(grad_in, (1, 0, 2)),
        grad_encoded,
        gain_self_sum,
        gain_cross_sum,
        gain_ffn_sum,
        bias_sum.T,
        grad_self_q,
        grad_self_k,
        grad_self_v,
        grad_self_o,
        grad_cross_q,
        grad_cross_k,
        grad_cross_v,
        grad_cross_o,
        grad_ffn_in,
        grad_ffn_out,
    )


def solution(mesh):
    rows, tokens, share = P("pb", None, None), P("pb", "blk", None), P("blk", None)
    return jax.shard_map(
        body,
        mesh=mesh,
        in_specs=(rows, tokens, P("pb", "blk")) + (P(),) * 15 + (rows,),
        out_specs=(rows, rows, tokens) + (P(),) * 4 + (share,) * 10,
        check_vma=False,
    )
```

```python
import functools

import jax
import jax.numpy as jnp
from jax import lax
from jax.experimental import pallas as pl
from jax.experimental.pallas import tpu as pltpu
from jax.sharding import PartitionSpec as P

EPSILON = 1e-06
MASKED = -1000000000.0
HIGHEST = lax.Precision.HIGHEST
HEAD = 64
GROUP = 4
WIDE = GROUP * HEAD
LANES = 128
LOW = jnp.bfloat16
F32 = jnp.float32
GELU_A = 0.7978845608028654
GELU_B = 0.044715
FORWARD_DEPTH = 8
BACKWARD_DEPTH = 16
FORWARD_BATCH = 4
BACKWARD_BATCH = 8
WIDE_BATCH = 4
SELF_US = 0.1
LAST_US = 0.1


def nn(a, b):
    return jnp.dot(a, b, preferred_element_type=F32)


def nt(a, b):
    return lax.dot_general(a, b, (((1,), (1,)), ((), ())), preferred_element_type=F32)


def tn(a, b):
    return lax.dot_general(a, b, (((0,), (0,)), ((), ())), preferred_element_type=F32)


def split(values):
    high = values.astype(LOW)
    return high, (values - high.astype(F32)).astype(LOW)


def call(kernel, outs, name, args, scratch=(), smem=(), hbm=(), hbm_out=(), limit=24, aliases=None, us=1.0):
    spaces = [pltpu.SMEM if k in smem else pltpu.HBM if k in hbm else pltpu.VMEM for k in range(len(args))]
    out_spaces = [pltpu.HBM if k in hbm_out else pltpu.VMEM for k in range(len(outs))]
    args = [
        each if space == pltpu.SMEM else pltpu.with_memory_space_constraint(each, space)
        for each, space in zip(args, spaces)
    ]
    return pl.pallas_call(
        kernel,
        in_specs=[pl.BlockSpec(memory_space=space) for space in spaces],
        out_specs=[pl.BlockSpec(memory_space=space) for space in out_spaces],
        out_shape=[space(shape, dtype) for space, (shape, dtype) in zip(out_spaces, outs)],
        scratch_shapes=list(scratch),
        input_output_aliases=aliases or {},
        compiler_params=pltpu.CompilerParams(vmem_limit_bytes=int(limit * 2**20)),
        cost_estimate=pl.CostEstimate(flops=int(us * 1.15e9), bytes_accessed=int(us * 3.6e6), transcendentals=0),
        name=name,
    )(*args)


def copies(pairs, sems, first=0):
    started = planned(pairs, sems, first)
    for each in started:
        each.start()
    return started


def planned(pairs, sems, first=0):
    return [pltpu.make_async_copy(src, dst, sems.at[first + k]) for k, (src, dst) in enumerate(pairs)]


class Stream:
    def __init__(self, pairs, sems, depth, first=0):
        self.copies = planned(pairs, sems, first)
        self.depth, self.done = depth, 0
        for each in self.copies[:depth]:
            each.start()

    def take(self, count=1):
        for _ in range(count):
            self.copies[self.done].wait()
            if self.done + self.depth < len(self.copies):
                self.copies[self.done + self.depth].start()
            self.done += 1


def flat(ref3):
    return jnp.concatenate([ref3[:, q, :] for q in range(ref3.shape[1])], axis=0)


def unflat(dest_ref, values):
    ans, questions, _ = dest_ref.shape
    for q in range(questions):
        dest_ref[:, q, :] = values[q * ans : (q + 1) * ans]


def row_head(ans, width):
    row = lax.broadcasted_iota(jnp.int32, (GROUP * ans, width), 0)
    head = jnp.zeros_like(row)
    for k in range(1, GROUP):
        head = head + (row >= k * ans).astype(jnp.int32)
    return head


def own_columns(ans):
    col = lax.broadcasted_iota(jnp.int32, (GROUP * ans, WIDE), 1)
    return (col // HEAD) == row_head(ans, WIDE)


def own_lane(ans, group, first=0):
    col = lax.broadcasted_iota(jnp.int32, (GROUP * ans, LANES), 1)
    return col == row_head(ans, LANES) + (group * GROUP + first)


def fold(block, ans):
    half = block[: 2 * ans] + block[2 * ans :]
    return half[:ans] + half[ans:]


def spread(rows):
    twice = jnp.concatenate([rows, rows], axis=0)
    return jnp.concatenate([twice, twice], axis=0)


def block_diagonal(values_ref, dest_ref, questions, ans, groups):
    own = own_columns(ans)
    per = GROUP * ans
    for q in range(questions):
        rows = spread(values_ref[q * ans : (q + 1) * ans, :])
        for g in range(groups):
            part = jnp.where(own, rows[:, g * WIDE : (g + 1) * WIDE], 0.0)
            dest_ref[g, q * per : (q + 1) * per, :] = part.astype(LOW)


def group_rows(wide_ref, group, per):
    return jnp.concatenate([wide_ref[q, group * per : (group + 1) * per, :] for q in range(wide_ref.shape[0])], axis=0)


def project_heads(wide_ref, weight_ref, dest_ref, questions, ans, groups):
    own = own_columns(ans)
    per = GROUP * ans
    for g in range(groups):
        got = nn(group_rows(wide_ref, g, per), weight_ref[:, g * WIDE : (g + 1) * WIDE])
        for q in range(questions):
            part = jnp.where(own, got[q * per : (q + 1) * per], 0.0)
            dest_ref[q * ans : (q + 1) * ans, g * WIDE : (g + 1) * WIDE] = fold(part, ans)


def head_lanes(values, pair, rows):
    lane = lax.broadcasted_iota(jnp.int32, (rows, LANES), 1)
    return jnp.where(lane < HEAD, values[:, 2 * pair : 2 * pair + 1], values[:, 2 * pair + 1 : 2 * pair + 2])


def norm_of(values, gain):
    inv = lax.rsqrt(jnp.mean(values * values, axis=1, keepdims=True) + EPSILON)
    return inv, values * inv * gain


def norm_back(values, gain, upstream):
    inv = lax.rsqrt(jnp.mean(values * values, axis=1, keepdims=True) + EPSILON)
    unit = values * inv
    scaled = upstream * gain
    grad = inv * (scaled - unit * jnp.mean(scaled * unit, axis=1, keepdims=True))
    return grad, jnp.sum(upstream * unit, axis=0, keepdims=True)


def decoder_forward_kernel(
    ans, heads, core_ref, rel_hbm, x_hbm, bucket_hbm, gain_self_hbm, gain_cross_hbm, wq_hbm, wk_hbm, wv_hbm, wo_hbm,
    cq_hbm, ck_hbm, cv_hbm, ids_hbm, enc_hbm,
    keep_ref, give_ref, stat_ref,
    query_hbm, after_hbm, norm_one_hbm, norm_two_hbm, ctx_hbm, q_hbm, k_hbm, v_hbm, probs_hbm, a_hbm, c_hbm, p_hbm,
    rel_ref, x_ref, bucket_ref, gain_self_ref, gain_cross_ref, wq_ref, wk_ref, wv_ref, wo_ref, cq_ref, ck_ref, cv_ref,
    ids_ref, enc_ref,
    query_ref, after_ref, norm_one_ref, norm_two_ref, ctx_ref, q_ref, k_ref, v_ref, probs_ref, a_ref, c_ref, p_ref,
    bd_ref, full_scr, m_scr, l_scr, load_sems, store_sems,
):
    questions, _, features = enc_ref.shape
    rows = questions * ans
    groups = features // WIDE
    per = GROUP * ans
    first_loads = [
        (x_hbm, x_ref), (gain_self_hbm, gain_self_ref), (wq_hbm, wq_ref), (wk_hbm, wk_ref), (wv_hbm, wv_ref),
        (rel_hbm, rel_ref), (bucket_hbm, bucket_ref), (wo_hbm, wo_ref), (gain_cross_hbm, gain_cross_ref),
        (cq_hbm, cq_ref), (ck_hbm, ck_ref), (ids_hbm, ids_ref),
    ]
    enc_loads = [(enc_hbm.at[q], enc_ref.at[q]) for q in range(questions)]
    loads = Stream(first_loads + enc_loads + [(cv_hbm, cv_ref)], load_sems, FORWARD_DEPTH)
    stores = []

    def store(*pairs):
        stores.extend(copies(pairs, store_sems, len(stores)))

    loads.take(2)
    x = flat(x_ref)
    normed = norm_of(x, gain_self_ref[...])[1].astype(LOW)
    row = lax.broadcasted_iota(jnp.int32, (rows, rows), 0)
    col = lax.broadcasted_iota(jnp.int32, (rows, rows), 1)
    mask = jnp.where((col <= row) & (col >= (row // ans) * ans), 0.0, MASKED)
    first = lax.broadcasted_iota(jnp.int32, (rows, LANES), 1) < HEAD
    for weight, dest in zip((wq_ref, wk_ref, wv_ref), (q_ref, k_ref, v_ref)):
        loads.take()
        dest[...] = nn(normed, weight[...]).astype(LOW)
    store((q_ref, q_hbm), (k_ref, k_hbm), (v_ref, v_hbm))
    norm_one_ref[...] = normed
    store((norm_one_ref, norm_one_hbm))
    loads.take(2)
    bucket = jnp.concatenate([bucket_ref[...]] * questions, axis=1)
    for pair in range(heads // 2):
        at = slice(pair * LANES, (pair + 1) * LANES)
        query, key, value = q_ref[:, at], k_ref[:, at], v_ref[:, at]
        parts = []
        for half in range(2):
            head = 2 * pair + half
            bias = jnp.zeros(bucket.shape, F32)
            for b in range(rel_ref.shape[1]):
                bias = jnp.where(bucket == b, rel_ref[head, b], bias)
            twice = jnp.concatenate([bias, bias], axis=0)
            bias = jnp.concatenate([twice] * (questions // 2), axis=0)
            own = jnp.where(first if half == 0 else ~first, query.astype(F32), 0.0).astype(LOW)
            scores = nt(own, key) + bias + mask
            top = jnp.max(scores, axis=1, keepdims=True)
            probs = jnp.exp(scores - top)
            probs = probs / jnp.sum(probs, axis=1, keepdims=True)
            probs_ref[head] = probs
            parts.append(nn(probs.astype(LOW), value))
        ctx_ref[:, at] = jnp.where(first, parts[0], parts[1]).astype(LOW)
    store((probs_ref, probs_hbm))
    loads.take()
    after = x + nn(ctx_ref[...], wo_ref[...])
    after_ref[...] = after
    store((ctx_ref, ctx_hbm), (after_ref, after_hbm))
    loads.take()
    normed = norm_of(after, gain_cross_ref[...])[1].astype(LOW)
    loads.take()
    query_ref[...] = nn(normed, cq_ref[...]).astype(LOW).astype(F32)
    norm_two_ref[...] = normed
    store((norm_two_ref, norm_two_hbm), (query_ref, query_hbm))

    block_diagonal(query_ref, bd_ref, questions, ans, groups)
    loads.take()
    for g in range(groups):
        got = nt(bd_ref[g], ck_ref[:, g * WIDE : (g + 1) * WIDE]).astype(LOW)
        for q in range(questions):
            a_ref[q, g * per : (g + 1) * per, :] = got[q * per : (q + 1) * per]
    store((a_ref, a_hbm))
    loads.take()
    for q in range(questions):
        if q % FORWARD_BATCH == 0:
            loads.take(FORWARD_BATCH)
        tokens = enc_ref[q]
        scores = nt(a_ref[q], tokens) + jnp.where(ids_ref[q : q + 1, :] != 0, 0.0, MASKED)
        top = jnp.max(scores, axis=1, keepdims=True)
        probs = jnp.exp(scores - top)
        total = jnp.sum(probs, axis=1, keepdims=True)
        low = probs.astype(LOW)
        p_ref[q] = low
        c_ref[q] = nn(low, tokens).astype(LOW)
        if q % FORWARD_BATCH == FORWARD_BATCH - 1:
            span = pl.ds(q + 1 - FORWARD_BATCH, FORWARD_BATCH)
            store((p_ref.at[span], p_hbm.at[span]), (c_ref.at[span], c_hbm.at[span]))
        m_scr[q] = jnp.broadcast_to(top, m_scr.shape[1:])
        l_scr[q] = jnp.broadcast_to(total, l_scr.shape[1:])
    loads.take()
    project_heads(c_ref, cv_ref, full_scr, questions, ans, groups)
    for q in range(questions):
        stats = jnp.zeros((ans, LANES), F32)
        for src, lane in ((m_scr, 0), (l_scr, HEAD)):
            for g in range(groups):
                part = jnp.where(own_lane(ans, g, lane), src[q, g * per : (g + 1) * per, :], 0.0)
                stats = stats + fold(part, ans)
        stat_ref[q * ans : (q + 1) * ans, :] = stats
    full_scr[:, features:] = stat_ref[...]
    by_side(full_scr, (keep_ref, give_ref), core_ref)
    for each in stores:
        each.wait()


def decoder_forward(core, x, encoded, ids, buckets, rel_turned, gain_self, gain_cross, wq, wk, wv, wo, cq, ck, cv):
    ans, questions, features = x.shape
    tokens = encoded.shape[1]
    heads = rel_turned.shape[0]
    groups = features // WIDE
    rows, per = questions * ans, GROUP * ans
    low, full = ((rows, features), LOW), ((rows, features), F32)
    by_token = ((questions, groups * per, tokens), LOW)
    by_feature = ((questions, groups * per, features), LOW)
    hbm_outs = [full, full, low, low, low, low, low, low, ((heads, rows, rows), F32), by_feature, by_feature, by_token]
    packed = ((rows // 2, features + LANES), F32)
    outs = [packed, packed, ((rows, LANES), F32)]
    weights = [wq, wk, wv, wo, cq, ck, cv]
    inputs = [rel_turned, x, buckets, gain_self, gain_cross] + weights + [ids, encoded]
    return call(
        functools.partial(decoder_forward_kernel, ans, heads),
        outs + hbm_outs,
        "decoder_forward",
        [core] + inputs,
        scratch=[pltpu.SMEM(rel_turned.shape, F32)]
        + [pltpu.VMEM(each.shape, each.dtype) for each in inputs[1:]]
        + [pltpu.VMEM(shape, dtype) for shape, dtype in hbm_outs]
        + [
            pltpu.VMEM((groups, questions * per, WIDE), LOW),
            pltpu.VMEM((rows, features + LANES), F32),
            pltpu.VMEM((questions, groups * per, LANES), F32),
            pltpu.VMEM((questions, groups * per, LANES), F32),
            pltpu.SemaphoreType.DMA((13 + questions,)),
            pltpu.SemaphoreType.DMA((10 + 2 * questions,)),
        ],
        smem=(0,),
        hbm=tuple(range(1, 1 + len(inputs))),
        hbm_out=tuple(range(len(outs), len(outs) + len(hbm_outs))),
        us=19, limit=44,
    )


def by_side(dest, outs, side_ref):
    rows = outs[0].shape[0]
    side = side_ref[0]
    outs[0][...] = dest[pl.ds(pl.multiple_of(side * rows, rows), rows), :]
    outs[1][...] = dest[pl.ds(pl.multiple_of((1 - side) * rows, rows), rows), :]


def merge_kernel(heads, side_ref, mine_ref, other_ref, *refs):
    outs, out_ref = refs[:-1], refs[-1]
    rows = mine_ref.shape[0]
    features = heads * HEAD
    mine, other = mine_ref[:, features:], other_ref[:, features:]
    stat = lax.broadcasted_iota(jnp.int32, mine.shape, 1) < HEAD
    top_mine = jnp.where(stat, mine, pltpu.roll(mine, HEAD, 1))
    top_other = jnp.where(stat, other, pltpu.roll(other, HEAD, 1))
    top = jnp.maximum(top_mine, top_other)
    by_mine, by_other = jnp.exp(top_mine - top), jnp.exp(top_other - top)
    out_ref[:, features:] = jnp.where(stat, top, mine * by_mine + other * by_other)
    for pair in range(heads // 2):
        at = slice(pair * LANES, (pair + 1) * LANES)
        out_ref[:, at] = mine_ref[:, at] * head_lanes(by_mine, pair, rows) + other_ref[:, at] * head_lanes(
            by_other, pair, rows
        )
    if outs:
        by_side(out_ref, outs, side_ref)


def merge(side, mine, other, heads, halved=False):
    rows, width = mine.shape
    return call(
        functools.partial(merge_kernel, heads),
        [((rows // 2, width), F32)] * 2 if halved else [(mine.shape, F32)],
        "merge_partials",
        (side, mine, other),
        scratch=[pltpu.VMEM(mine.shape, F32)] if halved else [],
        smem=(0,),
        us=0.5, limit=4,
    )


def join_kernel(side_ref, mine_ref, other_ref, out_ref):
    rows = mine_ref.shape[0]
    side = side_ref[0]
    out_ref[pl.ds(pl.multiple_of(side * rows, rows), rows), :] = mine_ref[...]
    out_ref[pl.ds(pl.multiple_of((1 - side) * rows, rows), rows), :] = other_ref[...]


def join(side, mine, other):
    rows, width = mine.shape
    return call(join_kernel, [((2 * rows, width), F32)], "join_halves", (side, mine, other), smem=(0,), us=0.05, limit=4)[0]


def decoder_backward_kernel(
    ans, heads, blocks, core_ref, own_ref, other_ref, stat_ref, after_hbm, cot_hbm, gain_hbm, co_hbm,
    fin_hbm, fout_hbm, cv_hbm, ck_hbm, enc_hbm, p_hbm,
    keep_ref, give_ref, gctx_ref, w_ref,
    out_hbm, gain_grad_hbm, gac_hbm, ctx_hbm, norm_hbm, active_hbm, inner_hbm, gcross_hbm, gout_hbm, s_hbm, b_hbm, wide_hbm,
    after_ref, cot_ref, gain_ref, co_ref, fin_ref, fout_ref, cv_ref, ck_ref, enc_ref, p_ref,
    out_ref, gain_grad_ref, gac_ref, ctx_ref, norm_ref, active_ref, inner_ref, gcross_ref, gout_ref, s_ref, b_ref, wide_ref,
    full_scr, delta_ref, bd_ref, back_scr, raw_scr, w_scr, d_scr, load_sems, store_sems,
):
    questions, _, features = enc_ref.shape
    rows, per = questions * ans, GROUP * ans
    groups = features // WIDE
    hidden = fin_ref.shape[1]
    width = hidden // blocks
    spans = [slice(c * width, (c + 1) * width) for c in range(blocks)]
    pairs = [(co_hbm, co_ref), (after_hbm, after_ref), (gain_hbm, gain_ref), (cot_hbm, cot_ref)]
    for at in spans:
        pairs += [(fin_hbm.at[:, at], fin_ref.at[:, at]), (fout_hbm.at[at, :], fout_ref.at[at, :])]
    pairs += [(cv_hbm, cv_ref)]
    for q in range(questions):
        pairs += [(enc_hbm.at[q], enc_ref.at[q]), (p_hbm.at[q], p_ref.at[q])]
    loads = Stream(pairs + [(ck_hbm, ck_ref)], load_sems, BACKWARD_DEPTH)
    stores = []

    def store(*pairs):
        stores.extend(copies(pairs, store_sems, len(stores)))

    core = core_ref[0]
    half = own_ref.shape[0]
    full_scr[pl.ds(pl.multiple_of(core * half, half), half), :] = own_ref[...]
    full_scr[pl.ds(pl.multiple_of((1 - core) * half, half), half), :] = other_ref[...]
    stats = full_scr[:, features:]
    lane = lax.broadcasted_iota(jnp.int32, stats.shape, 1)
    used = lane < heads
    inverse = jnp.where(used, 1.0 / jnp.where(used, pltpu.roll(stats, HEAD, 1), 1.0), 0.0)
    w_ref[...] = jnp.where(used, jnp.exp(jnp.where(used, stat_ref[...] - stats, 0.0)) * inverse, 0.0)
    for pair in range(heads // 2):
        at = slice(pair * LANES, (pair + 1) * LANES)
        ctx_ref[:, at] = full_scr[:, at] * head_lanes(inverse, pair, rows)
    store((ctx_ref, ctx_hbm))
    high, low = split(ctx_ref[...])
    loads.take(2)
    after = after_ref[...] + (nn(high, co_ref[...]) + nn(low, co_ref[...]))
    loads.take(2)
    gain = gain_ref[...]
    normed = norm_of(after, gain)[1].astype(LOW)
    norm_ref[...] = normed
    cot = flat(cot_ref)
    gout = cot.astype(LOW)
    gout_ref[...] = gout
    store((norm_ref, norm_hbm), (gout_ref, gout_hbm))
    total = jnp.zeros((rows, features), F32)
    back = jnp.zeros((rows, features), F32)
    for c, at in enumerate(spans):
        if c % 2 == 0:
            loads.take(4)
        inner = nn(normed, fin_ref[:, at])
        square = inner * inner
        wave = jnp.tanh(GELU_A * inner * (1.0 + GELU_B * square))
        active = (0.5 * inner * (1.0 + wave)).astype(LOW)
        slope = 0.5 * (1.0 + wave) + 0.5 * inner * (1.0 - wave * wave) * (GELU_A * (1.0 + 3.0 * GELU_B * square))
        active_ref[:, at] = active
        total = total + nn(active, fout_ref[at, :])
        grad_active = nt(gout, fout_ref[at, :]).astype(LOW).astype(F32)
        grad_inner = (grad_active * slope).astype(LOW)
        inner_ref[:, at] = grad_inner
        back = back + nt(grad_inner, fin_ref[:, at])
    unflat(out_ref, after + total)
    store((active_ref, active_hbm), (inner_ref, inner_hbm), (out_ref, out_hbm))
    grad, gain_grad = norm_back(after, gain, back)
    gain_grad_ref[...] = gain_grad
    gac = cot + grad
    gac_ref[...] = gac
    gcross = gac.astype(LOW)
    gcross_ref[...] = gcross
    gctx = nt(gcross, co_ref[...]).astype(LOW).astype(F32)
    gctx_ref[...] = gctx
    store((gac_ref, gac_hbm), (gcross_ref, gcross_hbm), (gain_grad_ref, gain_grad_hbm))
    select_row = lax.broadcasted_iota(jnp.int32, (features, LANES), 0) // HEAD
    select = jnp.where(select_row == lax.broadcasted_iota(jnp.int32, (features, LANES), 1), 1.0, 0.0).astype(LOW)
    high, low = split(gctx * ctx_ref[...])
    delta_ref[...] = nn(high, select) + nn(low, select)

    block_diagonal(gctx_ref, bd_ref, questions, ans, groups)
    for q in range(questions):
        for src, dst in ((w_ref, w_scr), (delta_ref, d_scr)):
            wide_rows = spread(src[q * ans : (q + 1) * ans, :])
            for g in range(groups):
                part = jnp.sum(jnp.where(own_lane(ans, g), wide_rows, 0.0), axis=1, keepdims=True)
                dst[q, g * per : (g + 1) * per, :] = jnp.broadcast_to(part, (per, LANES))
    loads.take()
    for g in range(groups):
        got = nt(bd_ref[g], cv_ref[:, g * WIDE : (g + 1) * WIDE])
        for q in range(questions):
            part = got[q * per : (q + 1) * per]
            raw_scr[q, g * per : (g + 1) * per, :] = part.astype(LOW)
            b_ref[q, g * per : (g + 1) * per, :] = (part * w_scr[q, g * per : (g + 1) * per, :1]).astype(LOW)
    store((b_ref, b_hbm))
    for q in range(questions):
        if q % BACKWARD_BATCH == 0:
            loads.take(2 * BACKWARD_BATCH)
        tokens = enc_ref[q]
        grad_probs = nt(raw_scr[q], tokens)
        probs = p_ref[q].astype(F32) * w_scr[q][:, :1]
        grad_scores = (probs * (grad_probs - d_scr[q][:, :1])).astype(LOW)
        s_ref[q] = grad_scores
        wide_ref[q] = nn(grad_scores, tokens).astype(LOW)
        if q % BACKWARD_BATCH == BACKWARD_BATCH - 1:
            span = pl.ds(q + 1 - BACKWARD_BATCH, BACKWARD_BATCH)
            store((s_ref.at[span], s_hbm.at[span]))
        if q % WIDE_BATCH == WIDE_BATCH - 1:
            span = pl.ds(q + 1 - WIDE_BATCH, WIDE_BATCH)
            store((wide_ref.at[span], wide_hbm.at[span]))
    loads.take()
    project_heads(wide_ref, ck_ref, back_scr, questions, ans, groups)
    by_side(back_scr, (keep_ref, give_ref), core_ref)
    for each in stores:
        each.wait()


def decoder_backward(core, own, other, stat, after, cot, gain, co, fin, fout, cv, ck, encoded, probs, heads):
    rows, features = after.shape
    ans, questions, _ = cot.shape
    tokens = encoded.shape[1]
    groups, per = features // WIDE, GROUP * ans
    hidden = fin.shape[1]
    blocks = 6
    low, full = ((rows, features), LOW), ((rows, features), F32)
    thin = ((rows, LANES), F32)
    wide = ((rows, hidden), LOW)
    half = ((rows // 2, features), F32)
    by_token = ((questions, groups * per, tokens), LOW)
    by_feature = ((questions, groups * per, features), LOW)
    outs = [half, half, full, thin]
    hbm_outs = [(cot.shape, F32), ((1, features), F32), full, full, low, wide, wide, low, low, by_token, by_feature, by_feature]
    inputs = [after, cot, gain, co, fin, fout, cv, ck, encoded, probs]
    return call(
        functools.partial(decoder_backward_kernel, ans, heads, blocks),
        outs + hbm_outs,
        "decoder_backward",
        [core, own, other, stat] + inputs,
        scratch=[pltpu.VMEM(each.shape, each.dtype) for each in inputs]
        + [pltpu.VMEM(shape, dtype) for shape, dtype in hbm_outs]
        + [
            pltpu.VMEM((rows, features + LANES), F32),
            pltpu.VMEM((rows, LANES), F32),
            pltpu.VMEM((groups, questions * per, WIDE), LOW),
            pltpu.VMEM((rows, features), F32),
            pltpu.VMEM(by_feature[0], LOW),
            pltpu.VMEM((questions, groups * per, LANES), F32),
            pltpu.VMEM((questions, groups * per, LANES), F32),
            pltpu.SemaphoreType.DMA((6 + 2 * blocks + 2 * questions,)),
            pltpu.SemaphoreType.DMA((10 + 2 * questions,)),
        ],
        smem=(0,),
        hbm=tuple(range(4, 4 + len(inputs))),
        hbm_out=tuple(range(len(outs), len(outs) + len(hbm_outs))),
        us=22.5, limit=54,
    )


def window(ref, index, share):
    start = index * share
    base = jnp.minimum((start // LANES) * LANES, ref.shape[1] - 2 * LANES)
    block = ref[:, pl.ds(pl.multiple_of(base, LANES), 2 * LANES)].astype(F32)
    return pltpu.roll(block, lax.rem(2 * LANES - (start - base), 2 * LANES), 1)[:, :share]


def weight_kernel(
    share, hidden_share, index_ref, active_hbm, inner_hbm, norm_hbm, gout_hbm, gcross_hbm, ctx_hbm, out_ref,
    active_ref, inner_ref, norm_ref, gout_ref, gcross_ref, ctx_ref, sems,
):
    loads = Stream(
        [(norm_hbm, norm_ref), (inner_hbm, inner_ref), (active_hbm, active_ref), (gout_hbm, gout_ref),
         (ctx_hbm, ctx_ref), (gcross_hbm, gcross_ref)],
        sems,
        3,
    )
    index = index_ref[0]
    features = gout_ref.shape[1]
    loads.take(2)
    normed = window(norm_ref, index, share).astype(LOW)
    at = 0
    for c in range(inner_ref.shape[1] // features):
        out_ref[at : at + share, :] = tn(normed, inner_ref[:, c * features : (c + 1) * features])
        at += share
    loads.take(2)
    out_ref[at : at + hidden_share, :] = tn(window(active_ref, index, hidden_share).astype(LOW), gout_ref[...])
    at += hidden_share
    loads.take(2)
    high, low = split(window(ctx_ref, index, share))
    out_ref[at : at + share, :] = tn(high, gcross_ref[...]) + tn(low, gcross_ref[...])


def weight_gradients(index, active, inner, norm, gout, gcross, ctx, share, hidden_share):
    features, hidden = gout.shape[1], inner.shape[1]
    inputs = [active, inner, norm, gout, gcross, ctx]
    rows = share * (hidden // features) + hidden_share + share
    return call(
        functools.partial(weight_kernel, share, hidden_share),
        [((rows, features), F32)],
        "weight_gradients",
        [index] + inputs,
        scratch=[pltpu.VMEM(each.shape, each.dtype) for each in inputs] + [pltpu.SemaphoreType.DMA((6,))],
        smem=(0,),
        hbm=tuple(range(1, 7)),
        us=3.3, limit=16,
    )[0]


def weight_sum_kernel(
    share, hidden_share, table_hbm, bucket_hbm, self_hbm, cross_hbm, ffn_hbm, mine_hbm, other_hbm,
    small_hbm, fin_hbm, fout_hbm, co_hbm,
    table_ref, bucket_ref, self_ref, cross_ref, ffn_ref, mine_ref, other_ref, small_ref, fin_ref, fout_ref, co_ref, sems,
):
    loads = copies(
        [(table_hbm, table_ref), (bucket_hbm, bucket_ref), (self_hbm, self_ref), (cross_hbm, cross_ref),
         (ffn_hbm, ffn_ref), (mine_hbm, mine_ref), (other_hbm, other_ref)],
        sems,
    )
    for load in loads[:5]:
        load.wait()
    heads, ans, rows = table_ref.shape
    total = jnp.zeros((heads, LANES), F32)
    which = lax.broadcasted_iota(jnp.int32, (LANES, rows), 0)
    wide_bucket = jnp.concatenate([bucket_ref[...]] * (rows // ans), axis=1)
    for i in range(ans):
        hot = jnp.where(which == wide_bucket[i : i + 1, :], 1.0, 0.0).astype(LOW)
        high, low = split(table_ref[:, i, :])
        total = total + (nt(high, hot) + nt(low, hot))
    small_ref[...] = jnp.zeros(small_ref.shape, F32)
    for k, row in enumerate((self_ref, cross_ref, ffn_ref)):
        small_ref[k : k + 1, :] = row[...]
    small_ref[8 : 8 + heads, :LANES] = total
    for load in loads[5:]:
        load.wait()
    features = mine_ref.shape[1]
    at = 0
    for c in range(fin_ref.shape[1] // features):
        fin_ref[:, c * features : (c + 1) * features] = mine_ref[at : at + share, :] + other_ref[at : at + share, :]
        at += share
    fout_ref[...] = mine_ref[at : at + hidden_share, :] + other_ref[at : at + hidden_share, :]
    at += hidden_share
    co_ref[...] = mine_ref[at : at + share, :] + other_ref[at : at + share, :]
    pairs = [(small_ref, small_hbm), (fin_ref, fin_hbm), (fout_ref, fout_hbm), (co_ref, co_hbm)]
    for each in copies(pairs, sems, 7):
        each.wait()


def weight_sum(table, buckets, gain_grads, mine, other, share, hidden_share, hidden):
    features = mine.shape[1]
    inputs = [table, buckets] + gain_grads + [mine, other]
    outs = [
        ((8 + table.shape[0], features), F32), ((share, hidden), F32), ((hidden_share, features), F32),
        ((share, features), F32),
    ]
    return call(
        functools.partial(weight_sum_kernel, share, hidden_share),
        outs,
        "weight_sum",
        inputs,
        scratch=[pltpu.VMEM(each.shape, each.dtype) for each in inputs]
        + [pltpu.VMEM(shape, dtype) for shape, dtype in outs]
        + [pltpu.SemaphoreType.DMA((11,))],
        hbm=tuple(range(7)),
        hbm_out=(0, 1, 2, 3),
        us=0.1, limit=10,
    )


def last_sum_kernel(mine_ref, other_ref, *refs):
    inputs, refs = refs[:4], refs[4:]
    sems, places = refs[-1], refs[-5:-1]
    refs = refs[:-5]
    outs, held = refs[: len(refs) // 2], refs[len(refs) // 2 :]
    loads = copies(list(zip(inputs, places)), sems)
    stores = []
    at = 0
    for k in range(mine_ref.shape[0]):
        held[at][...] = mine_ref[k] + other_ref[k]
        stores += copies([(held[at], outs[at])], sems, 4 + at)
        at += 1
    for load in loads:
        load.wait()
    for k in range(places[0].shape[0]):
        held[at][...] = places[0][k] + places[1][k]
        at += 1
    total = places[2][...] + places[3][...]
    for k in range(3):
        held[at + k][...] = total[k]
    heads, buckets = held[at + 3].shape
    held[at + 3][...] = total[8 : 8 + heads, :buckets]
    first = len(stores)
    for each in stores + copies(list(zip(held[first:], outs[first:])), sems, 4 + first):
        each.wait()


def last_sum(fresh, stack, small, bias_shape):
    row = ((small[0].shape[1],), F32)
    outs = [(mine.shape[1:], F32) for mine, _ in (fresh, stack) for _ in range(mine.shape[0])]
    outs += [row, row, row, (bias_shape, F32)]
    inputs = list(stack) + list(small)
    return call(
        last_sum_kernel,
        outs,
        "last_sum",
        list(fresh) + inputs,
        scratch=[pltpu.VMEM(shape, dtype) for shape, dtype in outs]
        + [pltpu.VMEM(each.shape, each.dtype) for each in inputs]
        + [pltpu.SemaphoreType.DMA((4 + len(outs),))],
        hbm=(2, 3, 4, 5),
        hbm_out=tuple(range(len(outs))),
        us=0.1, limit=16,
    )


def encoded_kernel(start, stop, has_base, s_hbm, p_hbm, a_hbm, b_hbm, *refs):
    out_ref, s_ref, p_ref, a_ref, b_ref, slots, in_sems, sems = refs[1:] if has_base else refs
    count = stop - start
    pairs = ((p_hbm, p_ref), (b_hbm, b_ref), (s_hbm, s_ref), (a_hbm, a_ref))
    loads = Stream([(src.at[start + k], dst.at[k]) for k in range(count) for src, dst in pairs], in_sems, 8)

    def copy(k, slot):
        return pltpu.make_async_copy(slots.at[slot], out_ref.at[start + k], sems.at[slot])

    for k in range(count):
        if k % 2 == 0:
            loads.take(8)
            if k >= 4:
                copy(k - 4, k % 4).wait()
                copy(k - 3, (k + 1) % 4).wait()
        slots[k % 4] = (tn(p_ref[k], b_ref[k]) + tn(s_ref[k], a_ref[k])).astype(LOW)
        if k % 2 == 1:
            copy(k - 1, (k - 1) % 4).start()
            copy(k, k % 4).start()
    for k in range(max(count - 4, 0), count):
        copy(k, k % 4).wait()


def encoded_gradient(grad_scores, probs, a, b, start, stop, base=None, us=5):
    questions, _, tokens = probs.shape
    features = a.shape[2]
    args = [grad_scores, probs, a, b] + ([] if base is None else [base])
    return call(
        functools.partial(encoded_kernel, start, stop, base is not None),
        [((questions, tokens, features), LOW)],
        "encoded_gradient",
        args,
        scratch=[pltpu.VMEM((stop - start,) + x.shape[1:], LOW) for x in (grad_scores, probs, a, b)]
        + [
            pltpu.VMEM((4, tokens, features), LOW),
            pltpu.SemaphoreType.DMA((4 * (stop - start),)),
            pltpu.SemaphoreType.DMA((4,)),
        ],
        hbm=tuple(range(len(args))),
        hbm_out=(0,),
        us=us, limit=26,
        aliases={} if base is None else {4: 0},
    )[0]


def split_owner(full_ref, outs, core_ref):
    count, share, _ = outs[0].shape
    core = core_ref[0]
    for k in range(count):
        for out, side in zip(outs, (core, 1 - core)):
            out[k] = full_ref[pl.ds(pl.multiple_of((2 * k + side) * share, share), share), :]


def key_value_kernel(ans, core_ref, gctx_ref, w_ref, wide_hbm, c_hbm, query_hbm, *refs):
    outs, (wide_ref, c_ref, query_ref, blocks_ref, scaled_ref, full_ref, sems) = refs[:-9], refs[-9:-2]
    held, store_sems = refs[-2:]
    stores = []
    questions, per = wide_ref.shape[0], GROUP * ans
    groups = wide_ref.shape[2] // WIDE
    loads = Stream([(query_hbm, query_ref), (wide_hbm, wide_ref), (c_hbm, c_ref)], sems, 3)
    for pair in range(groups * GROUP // 2):
        at = slice(pair * LANES, (pair + 1) * LANES)
        scaled_ref[:, at] = gctx_ref[:, at] * head_lanes(w_ref[...], pair, gctx_ref.shape[0])
    loads.take()
    count = len(outs) // 2
    for turn, (left, values, dests) in enumerate(
        ((wide_ref, query_ref, outs[:count]), (c_ref, scaled_ref, outs[count:]))
    ):
        block_diagonal(values, blocks_ref, questions, ans, groups)
        loads.take()
        dest = full_ref if count == 2 else dests[0]
        for g in range(groups):
            dest[:, g * WIDE : (g + 1) * WIDE] = tn(group_rows(left, g, per), blocks_ref[g])
        if count == 2:
            split_owner(full_ref, (held.at[turn], dests[1]), core_ref)
            stores += copies([(held.at[turn], dests[0])], store_sems, turn)
    for each in stores:
        each.wait()


def key_value_gradients(core, wide, gctx, weight, ctx_wide, query, count, ans):
    questions, _, features = wide.shape
    groups, per = features // WIDE, GROUP * ans
    share = features // count
    split_rows = share % 8 == 0
    half = ((count // 2, share, features), F32)
    outs = call(
        functools.partial(key_value_kernel, ans),
        [half] * 4 if split_rows else [((features, features), F32)] * 2,
        "key_value_gradients",
        (core, gctx, weight, wide, ctx_wide, query),
        scratch=[
            pltpu.VMEM(wide.shape, LOW),
            pltpu.VMEM(ctx_wide.shape, LOW),
            pltpu.VMEM(query.shape, F32),
            pltpu.VMEM((groups, questions * per, WIDE), LOW),
            pltpu.VMEM(gctx.shape, F32),
            pltpu.VMEM((features, features), F32),
            pltpu.SemaphoreType.DMA((3,)),
            pltpu.VMEM((2,) + half[0], F32),
            pltpu.SemaphoreType.DMA((2,)),
        ],
        smem=(0,),
        hbm=(3, 4, 5),
        hbm_out=(0, 2) if split_rows else (),
        us=4.3, limit=22,
    )
    if split_rows:
        return outs
    pairs = [each.reshape(count // 2, 2, share, features) for each in outs]
    return [
        lax.dynamic_index_in_dim(each, side, 1, keepdims=False) for each in pairs for side in (core[0], 1 - core[0])
    ]


def halve_kernel(place, side_ref, keep_ref, got_ref, *outs):
    count = keep_ref.shape[0]
    if count == 1:
        outs[0][...] = keep_ref[...] + got_ref[...]
        return
    side = side_ref[0]
    low = 1 << place
    for k in range(count // 2):
        base = (k // low) * 2 * low + k % low
        for out, bit in zip(outs, (side, 1 - side)):
            at = base + bit * low
            out[k] = keep_ref[at] + got_ref[at]


def halve(side, keep, got, place):
    count = keep.shape[0]
    half = ((max(count // 2, 1),) + keep.shape[1:], F32)
    return call(
        functools.partial(halve_kernel, place),
        [half] if count == 1 else [half, half],
        "halve_blocks",
        (side, keep, got),
        smem=(0,),
        us=0.05, limit=8,
    )


def final_kernel(key_keep_ref, key_got_ref, value_keep_ref, value_got_ref, out_ref):
    out_ref[0] = key_keep_ref[0] + key_got_ref[0]
    out_ref[1] = value_keep_ref[0] + value_got_ref[0]


def final_blocks(key_keep, key_got, value_keep, value_got):
    shape = ((2,) + key_keep.shape[1:], F32)
    return call(final_kernel, [shape], "final_blocks", (key_keep, key_got, value_keep, value_got), us=0.3, limit=4)[0]


def self_backward_kernel(
    ans, share, core_ref, index_ref, own_ref, other_ref, *refs,
):
    inputs = refs[:12]
    packed_hbm, table_hbm, gain_hbm, gas_hbm, gqkv_hbm = refs[12:17]
    (
        cq_ref, after_ref, gain_cross_ref, gac_ref, wo_ref, norm_two_ref, ctx_ref, v_ref, k_ref, q_ref, probs_ref,
        norm_one_ref,
    ) = places = refs[17:29]
    packed_ref, table_ref, gain_grad_ref, gas_ref, gqkv_ref, gq_ref, gctx_ref, sems, store_sems = refs[29:]
    rows, features = gac_ref.shape
    heads = probs_ref.shape[0]
    loads = Stream(list(zip(inputs, places)), sems, len(inputs))
    half = own_ref.shape[0]
    core, index = core_ref[0], index_ref[0]
    gq_ref[pl.ds(pl.multiple_of(core * half, half), half), :] = own_ref[...]
    gq_ref[pl.ds(pl.multiple_of((1 - core) * half, half), half), :] = other_ref[...]
    high, low = split(gq_ref[...])
    loads.take()
    upstream = nt(high, cq_ref[...]) + nt(low, cq_ref[...])
    loads.take(6)
    grad, gain_cross_grad = norm_back(after_ref[...], gain_cross_ref[...], upstream)
    gas = gac_ref[...] + grad
    gas_ref[...] = gas
    gain_grad_ref[...] = gain_cross_grad
    gself = gas.astype(LOW)
    gctx_ref[...] = nt(gself, wo_ref[...]).astype(LOW)
    normed = window(norm_two_ref, index, share).astype(LOW)
    packed_ref[0] = tn(normed, high) + tn(normed, low)
    packed_ref[1] = tn(window(ctx_ref, index, share).astype(LOW), gself)
    loads.take(5)
    first = lax.broadcasted_iota(jnp.int32, (rows, LANES), 1) < HEAD
    for pair in range(heads // 2):
        at = slice(pair * LANES, (pair + 1) * LANES)
        query, key, value, grad_ctx = q_ref[:, at], k_ref[:, at], v_ref[:, at], gctx_ref[:, at]
        gqs, gks, gvs = [], [], []
        for part in range(2):
            head = 2 * pair + part
            own = jnp.where(first if part == 0 else ~first, grad_ctx.astype(F32), 0.0).astype(LOW)
            grad_probs = nt(own, value)
            probs = probs_ref[head]
            grad_scores = probs * (grad_probs - jnp.sum(probs * grad_probs, axis=1, keepdims=True))
            blocks = [grad_scores[k * 2 * ans : (k + 1) * 2 * ans] for k in range(rows // (2 * ans))]
            both = functools.reduce(lambda a, b: a + b, blocks)
            table_ref[head] = both[:ans] + both[ans:]
            low_scores = grad_scores.astype(LOW)
            gqs.append(nn(low_scores, key))
            gks.append(tn(low_scores, query))
            gvs.append(tn(probs.astype(LOW), grad_ctx))
        for k, parts in enumerate((gqs, gks, gvs)):
            place = slice(k * features + pair * LANES, k * features + (pair + 1) * LANES)
            gqkv_ref[:, place] = jnp.where(first, parts[0], parts[1]).astype(LOW)
    normed = window(norm_one_ref, index, share).astype(LOW)
    for k in range(3):
        packed_ref[2 + k] = tn(normed, gqkv_ref[:, k * features : (k + 1) * features])
    pairs = [
        (packed_ref, packed_hbm), (table_ref, table_hbm), (gain_grad_ref, gain_hbm), (gas_ref, gas_hbm),
        (gqkv_ref, gqkv_hbm),
    ]
    for each in copies(pairs, store_sems):
        each.wait()

def input_back_kernel(
    gqkv_hbm, wq_hbm, wk_hbm, wv_hbm, x_hbm, gain_hbm, gas_hbm, grad_in_hbm, gain_grad_hbm,
    gqkv_ref, wq_ref, wk_ref, wv_ref, x_ref, gain_ref, gas_ref, grad_in_ref, gain_grad_ref, sems, store_sems,
):
    loads = Stream(
        [(gqkv_hbm, gqkv_ref), (wq_hbm, wq_ref), (wk_hbm, wk_ref), (wv_hbm, wv_ref), (x_hbm, x_ref),
         (gain_hbm, gain_ref), (gas_hbm, gas_ref)],
        sems,
        7,
    )
    rows, features = gas_ref.shape
    loads.take(4)
    upstream = jnp.zeros((rows, features), F32)
    for k, weight in enumerate((wq_ref, wk_ref, wv_ref)):
        upstream = upstream + nt(gqkv_ref[:, k * features : (k + 1) * features], weight[...])
    loads.take(3)
    grad, gain_grad = norm_back(flat(x_ref), gain_ref[...], upstream)
    gain_grad_ref[...] = gain_grad
    unflat(grad_in_ref, gas_ref[...] + grad)
    for each in copies([(grad_in_ref, grad_in_hbm), (gain_grad_ref, gain_grad_hbm)], store_sems):
        each.wait()


def input_back(gqkv, wq, wk, wv, x, gain, gas):
    inputs = [gqkv, wq, wk, wv, x, gain, gas]
    outs = [(x.shape, F32), ((1, x.shape[2]), F32)]
    return call(
        input_back_kernel,
        outs,
        "input_back",
        inputs,
        scratch=[pltpu.VMEM(each.shape, each.dtype) for each in inputs]
        + [pltpu.VMEM(shape, dtype) for shape, dtype in outs]
        + [pltpu.SemaphoreType.DMA((7,)), pltpu.SemaphoreType.DMA((2,))],
        hbm=tuple(range(7)),
        hbm_out=(0, 1),
        us=0.1, limit=16,
    )


def self_backward(core, index, own, other, inputs, ans, share):
    gac, probs = inputs[3], inputs[10]
    rows, features = gac.shape
    heads = probs.shape[0]
    outs = [
        ((5, share, features), F32), ((heads, ans, rows), F32), ((1, features), F32), ((rows, features), F32),
        ((rows, 3 * features), LOW),
    ]
    return call(
        functools.partial(self_backward_kernel, ans, share),
        outs,
        "self_backward",
        [core, index, own, other] + inputs,
        scratch=[pltpu.VMEM(each.shape, each.dtype) for each in inputs]
        + [pltpu.VMEM(shape, dtype) for shape, dtype in outs]
        + [
            pltpu.VMEM((rows, features), F32),
            pltpu.VMEM((rows, features), LOW),
            pltpu.SemaphoreType.DMA((len(inputs),)),
            pltpu.SemaphoreType.DMA((5,)),
        ],
        smem=(0, 1),
        hbm=tuple(range(4, 4 + len(inputs))),
        hbm_out=(0, 1, 2, 3, 4),
        us=SELF_US, limit=24,
    )


def partner(value, axis, bit):
    count = lax.axis_size(axis)
    return lax.ppermute(value, axis, [(k, k ^ bit) for k in range(count)])


def axis_bits(axis):
    bits, bit = [], 1
    while bit < lax.axis_size(axis):
        bits.append(bit)
        bit *= 2
    return bits


def add_kernel(side_ref, a_ref, b_ref, *refs):
    outs, out_ref = refs[:-1], refs[-1]
    out_ref[...] = a_ref[...] + b_ref[...]
    if outs:
        by_side(out_ref, outs, side_ref)


def add(side, a, b, halved=False):
    rows, width = a.shape
    return call(
        add_kernel,
        [((rows // 2, width), F32)] * 2 if halved else [(a.shape, F32)],
        "add_partials",
        (side, a, b),
        scratch=[pltpu.VMEM(a.shape, F32)] if halved else [],
        smem=(0,),
        us=0.05, limit=4,
    )


def exchange(keep, give, combine, sides):
    bits = axis_bits("blk")
    keep, give = combine(sides[1], keep, partner(give, "blk", bits[0]), True)
    (keep,) = combine(sides[1], keep, partner(give, "blk", bits[1]), False)
    for bit in bits[2:]:
        (keep,) = combine(sides[1], keep, partner(keep, "blk", bit), False)
    keep = join(sides[1], keep, partner(keep, "blk", bits[1]))
    return keep, partner(keep, "blk", bits[0])


def after(value, *others):
    return lax.optimization_barrier((value,) + others)[0]


def body(
    decoder_in, encoded, key_ids, buckets, gain_self, gain_cross, gain_ffn, rel_bias, self_q, self_k, self_v, self_o,
    cross_q, cross_k, cross_v, cross_o, ffn_in, ffn_out, cotangent,
):
    questions, ans, features = decoder_in.shape
    heads = rel_bias.shape[1]
    hidden = ffn_in.shape[1]
    blk_count = lax.axis_size("blk")
    blk_index = lax.axis_index("blk")
    index, core = blk_index.reshape(1), (blk_index % 2).reshape(1)
    share, hidden_share = features // blk_count, hidden // blk_count
    bits = axis_bits("blk")
    sides = [((blk_index // bit) % 2).reshape(1) for bit in bits[:2]]
    turned_in, turned_cot = jnp.transpose(decoder_in, (1, 0, 2)), jnp.transpose(cotangent, (1, 0, 2))
    (
        keep, give, stat, query, after_self, norm_one, norm_two, ctx_self, qs, ks, vs, probs_self, q_wide, ctx_wide,
        probs,
    ) = decoder_forward(
        core, turned_in, encoded, key_ids, buckets, rel_bias.T, gain_self, gain_cross, self_q, self_k, self_v, self_o,
        cross_q, cross_k, cross_v,
    )
    keep, other = exchange(keep, give, lambda s, a, b, halved: merge(s, a, b, heads, halved), sides)
    (
        keep, give, gctx, weight, output, grad_gain_ffn, gac, context, norm_three, active, grad_inner, gcross, gout,
        grad_scores, g_wide, query_wide,
    ) = decoder_backward(
        core, keep, other, stat, after_self, turned_cot, gain_ffn, cross_o, ffn_in, ffn_out, cross_v, cross_k, encoded,
        probs, heads,
    )

    def scatter_step(state, bit, *others, later=None):
        held, got, left = state
        place = sum(1 for b in left if b < bit)
        side = ((blk_index // bit) % 2).reshape(1)
        held, give = halve(side, held, after(got, *others), place)
        left = [b for b in left if b != bit]
        if later:
            return held, lambda value: partner(after(give, value), "blk", bit), left
        return held, partner(give, "blk", bit), left

    middle, end = questions // 2, questions - questions // 4
    inner = ((blk_index // bits[2]) % 2).reshape(1)
    keep, give = add(inner, keep, partner(give, "blk", bits[0]), True)
    got = partner(give, "blk", bits[2])
    key_keep, key_give, value_keep, value_give = key_value_gradients(
        core, query_wide, gctx, after(weight, keep), ctx_wide, query, blk_count, ans
    )
    (keep,) = add(inner, keep, after(got, value_give))
    key_state = (key_keep, partner(after(key_give, keep), "blk", bits[0]), list(bits[1:]))
    value_state = (value_keep, partner(after(value_give, keep), "blk", bits[0]), list(bits[1:]))
    got = partner(keep, "blk", bits[1])
    packed = weight_gradients(
        index, after(active, keep), grad_inner, norm_three, gout, gcross, context, share, hidden_share
    )
    packed_got = partner(packed, "pb", 1)
    key_state = scatter_step(key_state, bits[1], packed)
    held = key_state[0]
    for bit in bits[3:]:
        (keep,) = add(inner, keep, after(got, held))
        got = partner(keep, "blk", bit)
        held = keep
    grad_encoded = encoded_gradient(after(grad_scores, keep), probs, q_wide, g_wide, 0, middle)
    value_state = scatter_step(value_state, bits[1], grad_encoded, later=True)
    (keep,) = add(inner, keep, after(got, value_state[0]))
    value_state = (value_state[0], value_state[1](keep), value_state[2])
    got = partner(keep, "blk", bits[2])
    keep = join(inner, keep, got)
    other = partner(keep, "blk", bits[0])
    key_state = scatter_step(key_state, bits[2], keep)
    stack, table, grad_gain_cross, gas, grad_qkv = self_backward(
        core, index, keep, after(other, key_state[0]),
        [
            cross_q, after_self, gain_cross, gac, self_o, norm_two, ctx_self, vs, ks, qs, probs_self, norm_one,
        ],
        ans, share,
    )
    stack_got = partner(stack, "pb", 1)
    value_state = scatter_step(value_state, bits[2], stack)
    last = value_state[0]
    for bit in bits[3:]:
        key_state = scatter_step(key_state, bit, last)
        last = key_state[0]
    grad_in, grad_gain_self = input_back(
        after(grad_qkv, last), self_q, self_k, self_v, turned_in, gain_self, gas
    )
    last = grad_gain_self
    for bit in bits[3:]:
        value_state = scatter_step(value_state, bit, last)
        last = value_state[0]
    grad_encoded = encoded_gradient(
        after(grad_scores, last), probs, q_wide, g_wide, middle, end, grad_encoded, us=LAST_US
    )
    small, grad_ffn_in, grad_ffn_out, grad_cross_o = weight_sum(
        after(table, grad_encoded), buckets, [grad_gain_self, grad_gain_cross, grad_gain_ffn], packed, packed_got, share,
        hidden_share, hidden,
    )
    small_got = partner(small, "pb", 1)
    key_value = final_blocks(key_state[0], after(key_state[1], small), value_state[0], value_state[1])
    key_value_got = partner(key_value, "pb", 1)
    grad_encoded = encoded_gradient(
        after(grad_scores, key_value), probs, q_wide, g_wide, end, questions, grad_encoded, us=5.0
    )
    (
        grad_cross_k, grad_cross_v, grad_cross_q, grad_self_o, grad_self_q, grad_self_k, grad_self_v, gain_self_sum,
        gain_cross_sum, gain_ffn_sum, bias_sum,
    ) = last_sum((after(key_value, grad_encoded), key_value_got), (stack, stack_got), (small, small_got), rel_bias.shape[::-1])
    return (
        jnp.transpose(output, (1, 0, 2)),
        jnp.transpose(grad_in, (1, 0, 2)),
        grad_encoded,
        gain_self_sum,
        gain_cross_sum,
        gain_ffn_sum,
        bias_sum.T,
        grad_self_q,
        grad_self_k,
        grad_self_v,
        grad_self_o,
        grad_cross_q,
        grad_cross_k,
        grad_cross_v,
        grad_cross_o,
        grad_ffn_in,
        grad_ffn_out,
    )


def solution(mesh):
    rows, tokens, share = P("pb", None, None), P("pb", "blk", None), P("blk", None)
    return jax.shard_map(
        body,
        mesh=mesh,
        in_specs=(rows, tokens, P("pb", "blk")) + (P(),) * 15 + (rows,),
        out_specs=(rows, rows, tokens) + (P(),) * 4 + (share,) * 10,
        check_vma=False,
    )
```
